32 devices in a mesh: rep: 8 (over y, x, core), fsdp: 4 (over z).
Axes of the slice: x: 2, y: 2, z: 4, core: 2. Of those that a mesh axis runs over, the one named last changes fastest.
Arguments:
- tokens: bfloat16 [16, 1024, 2048], P('rep', 'fsdp'), may hold values from -6 to 6
- lengths: int32 [16], P('rep'), may hold values from 256 to 1024, as said below
- query_weight: bfloat16 [2048, 2048], P('fsdp'), may hold values from -0.125 to 0.125
- key_weight: bfloat16 [2048, 2048], P('fsdp'), may hold values from -0.125 to 0.125
- value_weight: bfloat16 [2048, 2048], P('fsdp'), may hold values from -0.125 to 0.125
- out_weight: bfloat16 [2048, 2048], P('fsdp'), may hold values from -3 to 3
- query_bias: bfloat16 [2048], P('fsdp'), may hold values from -3 to 3
- value_bias: bfloat16 [2048], P('fsdp'), may hold values from -3 to 3
- out_bias: bfloat16 [2048], P('fsdp'), may hold values from -3 to 3
- first_gain: bfloat16 [2048], P('fsdp'), may hold values from 0.5 to 1.5
- first_shift: bfloat16 [2048], P('fsdp'), may hold values from -3 to 3
- up_weight: bfloat16 [2048, 8192], P('fsdp'), may hold values from -0.125 to 0.125
- up_bias: bfloat16 [8192], P('fsdp'), may hold values from -3 to 3
- down_weight: bfloat16 [8192, 2048], P('fsdp'), may hold values from -0.0625 to 0.0625
- down_bias: bfloat16 [2048], P('fsdp'), may hold values from -3 to 3
- second_gain: bfloat16 [2048], P('fsdp'), may hold values from 0.5 to 1.5
- second_shift: bfloat16 [2048], P('fsdp'), may hold values from -3 to 3
- cotangent: bfloat16 [16, 1024, 2048], P('rep', 'fsdp'), may hold values from -6 to 6
Outputs:
- layer_out: bfloat16 [16, 1024, 2048], P('rep', 'fsdp')
- tokens_grad: float32 [16, 1024, 2048], P('rep', 'fsdp')
- grad_query_weight: float32 [2048, 2048], P('fsdp')
- grad_key_weight: float32 [2048, 2048], P('fsdp')
- grad_value_weight: float32 [2048, 2048], P('fsdp')
- grad_out_weight: float32 [2048, 2048], P('fsdp')
- grad_query_bias: float32 [2048], P('fsdp')
- grad_value_bias: float32 [2048], P('fsdp')
- grad_out_bias: float32 [2048], P('fsdp')
- grad_first_gain: float32 [2048], P('fsdp')
- grad_first_shift: float32 [2048], P('fsdp')
- grad_up_weight: float32 [2048, 8192], P('fsdp')
- grad_up_bias: float32 [8192], P('fsdp')
- grad_down_weight: float32 [8192, 2048], P('fsdp')
- grad_down_bias: float32 [2048], P('fsdp')
- grad_second_gain: float32 [2048], P('fsdp')
- grad_second_shift: float32 [2048], P('fsdp')
The draws below stay inside these ranges and needn't reach their ends.
Inputs may be any that keep to these rules, and one draw needn't show every extreme that they name: `lengths`: of each replica group's 2 consecutive slots, one, drawn from the seed, has length 1024; the others are at least 256.
All inputs are finite; a program needn't handle non-finite values.
Results may differ from the reference program's by a relative error of at most 0.02.
Values may be sent and summed in bfloat16 or wider, within the bound.
No kernel may reach another device: no remote copies, remote signals or barrier semaphores. Data moves between devices by JAX's collectives and lax.ppermute only.
A program may use at most 384 MiB of HBM per device.

```python
import jax
import jax.numpy as jnp
from jax import lax

D = 2048
FF = 8192
HEADS = 16
SEQ = 1024
GROUP_SLOTS = 2
SLOTS = 16


def draw_lengths(key, part):
    key = jax.random.fold_in(key, 7)
    first_key, second_key = jax.random.split(key)
    base = jax.random.randint(first_key, (SLOTS,), SEQ // 4, SEQ + 1)
    groups = SLOTS // GROUP_SLOTS
    chosen = jax.random.randint(second_key, (groups,), 0, GROUP_SLOTS)
    within = jnp.arange(SLOTS, dtype=jnp.int32) % GROUP_SLOTS
    longest = within == jnp.repeat(chosen, GROUP_SLOTS)
    return jnp.where(longest, SEQ, base).astype(jnp.int32)


def shard_levels(own_key, extent, shards, smallest, high):
    def one(axis_at, shards_of):
        steps = jax.random.uniform(jax.random.fold_in(jax.random.fold_in(own_key, 6), axis_at), (shards_of,), jnp.float32, smallest / len(shards), high / len(shards))
        return jnp.repeat(jnp.exp(steps), extent[axis_at] // shards_of).reshape((-1,) + (1,) * (len(extent) - axis_at - 1))

    factor_of = one(*shards[0])
    for cut in shards[1:]:
        factor_of = factor_of * one(*cut)
    return factor_of


def scatter_about(key, shape, width, most, shards=(), kind=jnp.bfloat16):
    drawn = jax.random.normal(key, shape, jnp.float32) * width
    if len(shards) > 0:
        drawn = shard_levels(key, shape, shards, -0.22, 0.18) * drawn
    return jnp.clip(drawn, min=-most, max=most).astype(kind)


def setup_inputs(seed: int = 0) -> dict:
    seeds = jax.random.split(jax.random.key(seed), 19)
    return {
        "tokens": scatter_about(seeds[0], (SLOTS, SEQ, D), 1.0, 6.0, ((0, 8), (1, 4))),
        "lengths": draw_lengths(jax.random.fold_in(seeds[18], 71), 0),
        "query_weight": scatter_about(seeds[2], (D, D), D ** -0.5, 0.125, ((0, 4),)),
        "key_weight": scatter_about(seeds[3], (D, D), D ** -0.5, 0.125, ((0, 4),)),
        "value_weight": scatter_about(seeds[4], (D, D), D ** -0.5, 0.125, ((0, 4),)),
        "out_weight": scatter_about(seeds[5], (D, D), (max(1, 2 * D // SEQ)) ** -0.5, 3.0, ((0, 4),)),
        "query_bias": scatter_about(seeds[6], (D,), 0.5, 3.0, ((0, 4),)),
        "value_bias": scatter_about(seeds[7], (D,), 0.5, 3.0, ((0, 4),)),
        "out_bias": scatter_about(seeds[8], (D,), 0.5, 3.0, ((0, 4),)),
        "first_gain": jnp.clip(0.5 + 1.0 * jax.random.uniform(seeds[9], (D,), jnp.float32) ** shard_levels(seeds[9], (D,), ((0, 4),), -0.2, 0.2), 0.5, 1.5).astype(jnp.bfloat16),
        "first_shift": scatter_about(seeds[10], (D,), 0.5, 3.0, ((0, 4),)),
        "up_weight": scatter_about(seeds[11], (D, FF), D ** -0.5, 0.125, ((0, 4),)),
        "up_bias": scatter_about(seeds[12], (FF,), 0.5, 3.0, ((0, 4),)),
        "down_weight": scatter_about(seeds[13], (FF, D), FF ** -0.5, 0.0625, ((0, 4),)),
        "down_bias": scatter_about(seeds[14], (D,), 0.5, 3.0, ((0, 4),)),
        "second_gain": jnp.clip(0.5 + 1.0 * jax.random.uniform(seeds[15], (D,), jnp.float32) ** shard_levels(seeds[15], (D,), ((0, 4),), -0.2, 0.2), 0.5, 1.5).astype(jnp.bfloat16),
        "second_shift": scatter_about(seeds[16], (D,), 0.5, 3.0, ((0, 4),)),
        "cotangent": scatter_about(seeds[17], (SLOTS, SEQ, D), 1.0, 6.0, ((0, 8), (1, 4))),
    }


@jax.custom_vjp
def low(v):
    return lax.optimization_barrier(v.astype(jnp.bfloat16)).astype(jnp.float32)

@jax.custom_vjp
def low_back(v):
    return v

def low_keep(v):
    return (low(v), None)

def low_pass(kept, grad):
    return (grad,)

def back_keep(v):
    return (v, None)

def back_low(kept, grad):
    return (low(grad),)
low.defvjp(low_keep, low_pass)
low_back.defvjp(back_keep, back_low)
EPSILON = 1e-06
HIGHEST = lax.Precision.HIGHEST

def matmul(left, right):
    return jnp.dot(left, right, precision=HIGHEST)

def rounded_both(value):
    return low(low_back(value))

def layer_norm(summed, gain, shift):
    center = summed - lax.optimization_barrier(jnp.mean(summed, axis=-1, keepdims=True))
    spread = lax.optimization_barrier(jnp.mean(center * center, axis=-1, keepdims=True))
    return center * lax.rsqrt(spread + EPSILON) * gain + shift

def slot_forward(params, inputs, length):
    query_weight, key_weight, value_weight, out_weight, query_bias, value_bias, out_bias, first_gain, first_shift, up_weight, up_bias, down_weight, down_bias, second_gain, second_shift = params
    positions = jnp.arange(SEQ, dtype=jnp.int32)
    valid = (positions < length).astype(jnp.float32)[:, None]
    query = rounded_both(matmul(inputs, query_weight) + query_bias)
    keys = rounded_both(matmul(inputs, key_weight))
    values = rounded_both(matmul(inputs, value_weight) + value_bias)
    head_dim = D // HEADS
    query3 = query.reshape(SEQ, HEADS, head_dim)
    keys3 = keys.reshape(SEQ, HEADS, head_dim)
    values3 = values.reshape(SEQ, HEADS, head_dim)
    scores = jnp.einsum('qhd,khd->hqk', query3, keys3, precision=HIGHEST) * head_dim ** (-0.5)
    masked = positions[None, None, :] < length
    scores = low_back(jnp.where(masked, scores, -1e+30))
    probs = low(jax.nn.softmax(scores, axis=-1))
    context = jnp.einsum('hqk,khd->qhd', probs, values3, precision=HIGHEST).reshape(SEQ, D)
    context = rounded_both(context)
    attended = low_back(matmul(context, out_weight) + out_bias)
    normed1 = layer_norm(inputs + attended, first_gain, first_shift)
    before = low_back(matmul(low(normed1), up_weight) + up_bias)
    activated = low(jax.nn.gelu(before, approximate=True))
    down_out = low_back(matmul(activated, down_weight) + down_bias)
    return valid * layer_norm(normed1 + down_out, second_gain, second_shift)

def reference(tokens, lengths, query_weight, key_weight, value_weight, out_weight, query_bias, value_bias, out_bias, first_gain, first_shift, up_weight, up_bias, down_weight, down_bias, second_gain, second_shift, cotangent):
    params = tuple((item.astype(jnp.float32) for item in (query_weight, key_weight, value_weight, out_weight, query_bias, value_bias, out_bias, first_gain, first_shift, up_weight, up_bias, down_weight, down_bias, second_gain, second_shift)))
    inputs = tokens.astype(jnp.float32)

    def whole(params_in, inputs_in):
        step = jax.checkpoint(lambda item: slot_forward(params_in, item[0], item[1]))
        return lax.map(step, (inputs_in, lengths))
    outputs, pull = jax.vjp(whole, params, inputs)
    grads, tokens_grad = pull(cotangent.astype(jnp.float32))
    return (outputs.astype(jnp.bfloat16), tokens_grad, grads[0], grads[1], grads[2], grads[3], grads[4], grads[5], grads[6], grads[7], grads[8], grads[9], grads[10], grads[11], grads[12], grads[13], grads[14])
```

```python
import jax
import jax.numpy as jnp
from jax import lax
from jax.sharding import PartitionSpec as P

HEADS = 16
TEAM = 4
EPSILON = 1e-06
BF = jnp.bfloat16
F32 = jnp.float32


def mm(left, right):
    return jnp.dot(left, right, preferred_element_type=F32)


def mm_t(left, right):
    return lax.dot_general(left, right, (((1,), (1,)), ((), ())), preferred_element_type=F32)


def t_mm(left, right):
    return lax.dot_general(left, right, (((0,), (0,)), ((), ())), preferred_element_type=F32)


def pick(array, index, axis=0):
    return lax.dynamic_index_in_dim(array, index, axis, keepdims=False)


def normalise(summed):
    center = summed - jnp.mean(summed, axis=-1, keepdims=True)
    spread = jnp.mean(center * center, axis=-1, keepdims=True)
    scale = lax.rsqrt(spread + EPSILON)
    return center * scale, scale


def norm_backward(grad, gain, normal, scale):
    dn = grad * gain
    first = jnp.mean(dn, axis=-1, keepdims=True)
    second = jnp.mean(dn * normal, axis=-1, keepdims=True)
    return scale * (dn - first - normal * second)


def gelu_parts(u):
    inner = 0.7978845608 * (u + 0.044715 * u * u * u)
    t = jnp.tanh(inner)
    value = 0.5 * u * (1.0 + t)
    slope = 0.5 * (1.0 + t) + 0.5 * u * (1.0 - t * t) * 0.7978845608 * (
        1.0 + 3.0 * 0.044715 * u * u
    )
    return value, slope


def attend(query, keys, values, mask, scaling):
    scores = jnp.einsum("qhd,khd->hqk", query, keys, preferred_element_type=F32) * scaling
    scores = jnp.where(mask[None, None, :], scores, -1e30)
    log_total = jax.nn.logsumexp(scores, axis=-1, keepdims=True)
    probs = jnp.exp(scores - log_total).astype(BF)
    context = jnp.einsum("hqk,khd->qhd", probs, values, preferred_element_type=F32)
    return context.astype(BF), log_total


def attend_backward(query, keys, values, mask, log_total, dcontext, scaling):
    scores = jnp.einsum("qhd,khd->hqk", query, keys, preferred_element_type=F32) * scaling
    scores = jnp.where(mask[None, None, :], scores, -1e30)
    probs = jnp.exp(scores - log_total)
    low = probs.astype(BF)
    dprobs = jnp.einsum("qhd,khd->hqk", dcontext, values, preferred_element_type=F32)
    delta = jnp.sum(dprobs * probs, axis=-1, keepdims=True)
    dscores = (probs * (dprobs - delta)).astype(BF)
    dvalues = jnp.einsum("hqk,qhd->khd", low, dcontext, preferred_element_type=F32)
    dkeys = jnp.einsum("hqk,qhd->khd", dscores, query, preferred_element_type=F32) * scaling
    dquery = jnp.einsum("hqk,khd->qhd", dscores, keys, preferred_element_type=F32) * scaling
    return dquery.astype(BF), dkeys.astype(BF), dvalues.astype(BF)


def local(
    tokens,
    lengths,
    query_weight,
    key_weight,
    value_weight,
    out_weight,
    query_bias,
    value_bias,
    out_bias,
    first_gain,
    first_shift,
    up_weight,
    up_bias,
    down_weight,
    down_bias,
    second_gain,
    second_shift,
    cotangent,
):
    slots_here, block, width = tokens.shape
    reps, parts = lax.axis_size("rep"), lax.axis_size("fsdp")
    copies = reps // TEAM
    hidden = up_weight.shape[1]
    shard = query_weight.shape[0]
    head_dim = width // HEADS
    scaling = head_dim ** (-0.5)
    rep, z = lax.axis_index("rep"), lax.axis_index("fsdp")
    q, d = rep % TEAM, rep // TEAM
    parity = z % 2
    team_slots = TEAM * slots_here
    held = team_slots // parts
    rows = slots_here * block
    heads_each = HEADS // reps

    def swap(x, mask):
        return lax.ppermute(x, "rep", [(i, i ^ mask) for i in range(reps)])

    def routes(turn):
        pairs = []
        for copy in range(copies):
            for member in range(TEAM):
                for place in range(parts):
                    i = (place + turn) % 2
                    slot = member * slots_here + i
                    to_place = slot % parts
                    to_member = ((slot // parts) * parts + place) // 2
                    pairs.append(
                        (
                            (copy * TEAM + member) * parts + place,
                            (copy * TEAM + to_member) * parts + to_place,
                        )
                    )
        return pairs

    even, odd = routes(0), routes(1)
    axes = ("rep", "fsdp")

    def to_team(x):
        first = lax.ppermute(pick(x, parity), axes, even)
        second = lax.ppermute(pick(x, 1 - parity), axes, odd)
        return jnp.concatenate([first, second], axis=0)

    def from_team(x):
        first = lax.ppermute(x[:block], axes, [(b, a) for a, b in even])
        second = lax.ppermute(x[block:], axes, [(b, a) for a, b in odd])
        straight = jnp.stack([first, second])
        turned = jnp.stack([second, first])
        return jnp.where(parity == 0, straight, turned)

    def team_rows(own):
        far = swap(own, 2)
        mine = jnp.concatenate([own, swap(own, 1)], axis=0)
        other = jnp.concatenate([far, swap(far, 1)], axis=0)
        return mine, other

    def team_sum(mine, other):
        far = other[:rows] + swap(other[rows:].astype(BF), 1).astype(F32)
        far = swap(far.astype(BF), 2).astype(F32)
        near = swap(mine[rows:].astype(BF), 1).astype(F32)
        return mine[:rows] + near + far

    all_lengths = lax.all_gather(lengths, "rep", axis=0, tiled=True)

    def row_places(member):
        place = []
        for o in (parity, 1 - parity):
            at = (member * 2 + o) % parts
            place.append(at * block + jnp.arange(block))
        return jnp.concatenate(place)

    def slot_length(member):
        return all_lengths[d * team_slots + ((member * 2) // parts) * parts + z]

    members = [q ^ m for m in range(TEAM)]
    masks = [row_places(m) < slot_length(m) for m in members]
    valid = masks[0].astype(F32)[:, None]

    def by_slot(mine, other):
        if held == 2:
            return [mine, other]
        return [jnp.concatenate([mine, other], axis=0)]

    def by_pair(pieces):
        if held == 2:
            return pieces
        whole = pieces[0]
        return [whole[: 2 * rows], whole[2 * rows :]]

    key_masks = by_slot(jnp.concatenate(masks[:2]), jnp.concatenate(masks[2:]))

    def head_columns(w, e):
        lead = w.shape[:-1]
        split = w.reshape(lead + (copies, heads_each, TEAM, head_dim))
        at = len(lead)
        split = pick(pick(split, e, at), q, at + 1)
        return split.reshape(lead + (heads_each * head_dim,))

    def over_z(x):
        return lax.all_gather(x, "fsdp", axis=0, tiled=True)

    def spread(x):
        return [x] + [swap(x, TEAM * m) for m in range(1, copies)]

    qkv_own = jnp.concatenate(
        [head_columns(w, d) for w in (query_weight, key_weight, value_weight)], axis=1
    )
    span = heads_each * head_dim
    qkv = spread(over_z(qkv_own))

    vectors = jnp.concatenate(
        [
            query_bias,
            value_bias,
            out_bias,
            first_gain,
            first_shift,
            down_bias,
            second_gain,
            second_shift,
            up_bias,
        ]
    )
    vectors = lax.all_gather(vectors, "fsdp", axis=0, tiled=False).astype(F32)
    names = [vectors[:, i * shard : (i + 1) * shard].reshape(width) for i in range(8)]
    bias_query, bias_value, bias_out, gain_one, shift_one, bias_down, gain_two, shift_two = names
    bias_up = vectors[:, 8 * shard :].reshape(parts, reps, hidden // parts // reps)

    per_shard = HEADS // parts
    split_out = out_weight.reshape(-1, head_dim, copies, width // copies)
    split_out = pick(split_out, d, 2)
    if per_shard >= TEAM:
        split_out = split_out.reshape(per_shard // TEAM, TEAM, head_dim, width // copies)
        out_own = pick(split_out, q, 1)
        out_all = over_z(out_own)
    else:
        out_own = pick(split_out, q % per_shard, 0)[None]
        out_all = over_z(out_own).reshape(HEADS // TEAM, TEAM // per_shard, head_dim, -1)
        out_all = pick(out_all, q // per_shard, 1)
    out_columns = jnp.stack(spread(out_all.reshape(HEADS // TEAM * head_dim, width // copies)))
    out_full = jnp.concatenate([pick(out_columns, d ^ e) for e in range(copies)], axis=1)
    out_rows = [
        lax.dynamic_slice_in_dim(out_full, (d ^ m) * span, span, 0) for m in range(copies)
    ]
    out_rel = jnp.concatenate(out_rows, axis=0)

    unit = hidden // parts // reps
    up_own = pick(up_weight.reshape(shard, parts, reps, unit), rep, 2).reshape(shard, parts * unit)
    down_own = pick(down_weight.reshape(reps, unit, width), rep, 0)
    up = spread(over_z(up_own))
    down = spread(over_z(down_own))
    up_biases = [pick(bias_up, rep ^ (TEAM * m), 1).reshape(1, -1) for m in range(copies)]

    own_tokens = to_team(tokens)
    tokens_mine, tokens_other = team_rows(own_tokens)
    slot_tokens = by_slot(tokens_mine, tokens_other)
    kept = []
    contexts = []
    for tok, mask in zip(slot_tokens, key_masks):
        per_part = []
        context = []
        for m in range(copies):
            both = mm(tok, qkv[m])
            shape = (tok.shape[0], heads_each, head_dim)
            qb = head_columns(bias_query, d ^ m)
            vb = head_columns(bias_value, d ^ m)
            query = (both[:, :span] + qb).astype(BF).reshape(shape)
            keys = both[:, span : 2 * span].astype(BF).reshape(shape)
            values = (both[:, 2 * span :] + vb).astype(BF).reshape(shape)
            ctx, log_total = attend(query, keys, values, mask, scaling)
            per_part.append((query, keys, values, log_total))
            context.append(ctx.reshape(tok.shape[0], span))
        kept.append(per_part)
        contexts.append(jnp.concatenate(context, axis=1))
    partial = by_pair([mm(ctx, out_rel) for ctx in contexts])
    attended = team_sum(*partial)
    summed1 = own_tokens.astype(F32) + attended + bias_out
    normal1, scale1 = normalise(summed1)
    normed1 = normal1 * gain_one + shift_one
    hidden_pairs = team_rows(normed1.astype(BF))

    slopes, active, partial = [], [], []
    for rows_in in hidden_pairs:
        slope_parts, active_parts = [], []
        total = 0.0
        for m in range(copies):
            before = mm(rows_in, up[m]) + up_biases[m]
            value, slope = gelu_parts(before)
            value = value.astype(BF)
            slope_parts.append(slope)
            active_parts.append(value)
            total = total + mm(value, down[m])
        slopes.append(slope_parts)
        active.append(active_parts)
        partial.append(total)
    summed2 = normed1 + team_sum(*partial) + bias_down
    normal2, scale2 = normalise(summed2)
    result = valid * (normal2 * gain_two + shift_two)
    layer_out = from_team(result.astype(BF))

    grad_out = to_team(cotangent).astype(F32) * valid
    dsum2 = norm_backward(grad_out, gain_two, normal2, scale2)
    gain_two_grad = jnp.sum(grad_out * normal2, axis=0)
    shift_two_grad = jnp.sum(grad_out, axis=0)
    ddown = dsum2.astype(BF)
    down_bias_grad = jnp.sum(ddown.astype(F32), axis=0)
    ddown_pairs = team_rows(ddown)
    partial, dbefores = [], []
    for i, rows_in in enumerate(ddown_pairs):
        total = 0.0
        dbefore_parts = []
        for m in range(copies):
            dbefore = (mm_t(rows_in, down[m]) * slopes[i][m]).astype(BF)
            dbefore_parts.append(dbefore)
            total = total + mm_t(dbefore, up[m])
        dbefores.append(dbefore_parts)
        partial.append(total)
    dnormed1 = dsum2 + team_sum(*partial)
    dsum1 = norm_backward(dnormed1, gain_one, normal1, scale1)
    gain_one_grad = jnp.sum(dnormed1 * normal1, axis=0)
    shift_one_grad = jnp.sum(dnormed1, axis=0)
    dattn = dsum1.astype(BF)
    out_bias_grad = jnp.sum(dattn.astype(F32), axis=0)

    def over_copies(shares):
        total = shares[0]
        for m in range(1, copies):
            total = total + swap(shares[m].astype(BF), TEAM * m).astype(F32)
        return total.astype(BF)

    def to_owner(x):
        return lax.psum_scatter(x, "fsdp", scatter_dimension=0, tiled=True)

    def from_all(x):
        return lax.all_gather(x, "rep", axis=0, tiled=False)

    down_share = over_copies(
        [
            t_mm(active[0][m], ddown_pairs[0]) + t_mm(active[1][m], ddown_pairs[1])
            for m in range(copies)
        ]
    )
    down_grad = from_all(to_owner(down_share)).reshape(reps * unit, width).astype(F32)
    up_share = over_copies(
        [
            t_mm(hidden_pairs[0], dbefores[0][m]) + t_mm(hidden_pairs[1], dbefores[1][m])
            for m in range(copies)
        ]
    )
    up_grad = from_all(to_owner(up_share)).reshape(reps, shard, parts, unit)
    up_grad = up_grad.transpose(1, 2, 0, 3).reshape(shard, hidden).astype(F32)

    dattn_slots = by_slot(*team_rows(dattn))
    out_share = 0.0
    partial = []
    qkv_shares = [0.0] * copies
    query_sums, value_sums = [0.0] * copies, [0.0] * copies
    for i, rows_in in enumerate(dattn_slots):
        out_share = out_share + t_mm(contexts[i], rows_in)
        dcontext = mm_t(rows_in, out_rel).astype(BF)
        total = 0.0
        for m in range(copies):
            query, keys, values, log_total = kept[i][m]
            dctx = dcontext[:, m * span : (m + 1) * span].reshape(query.shape)
            dq, dk, dv = attend_backward(
                query, keys, values, key_masks[i], log_total, dctx, scaling
            )
            both = jnp.concatenate([g.reshape(-1, span) for g in (dq, dk, dv)], axis=1)
            total = total + mm_t(both, qkv[m])
            qkv_shares[m] = qkv_shares[m] + t_mm(slot_tokens[i], both)
            sums = jnp.sum(both.astype(F32), axis=0)
            query_sums[m] = query_sums[m] + sums[:span]
            value_sums[m] = value_sums[m] + sums[2 * span :]
        partial.append(total)
    dtokens = dsum1 + team_sum(*by_pair(partial))
    tokens_grad = from_team(dtokens.astype(BF)).astype(F32)

    out_rows = [
        lax.dynamic_slice_in_dim(out_share, (d ^ e) * span, span, 0) for e in range(copies)
    ]
    out_rows = jnp.concatenate(out_rows, axis=0).reshape(-1, copies, width // copies)
    out_mine = over_copies([pick(out_rows, d ^ m, 1) for m in range(copies)])
    if per_shard >= TEAM:
        out_final = to_owner(out_mine)
        out_final = out_final.reshape(per_shard // TEAM, head_dim, -1)
        out_grad = from_all(out_final)
        out_grad = out_grad.reshape(
            copies, TEAM, per_shard // TEAM, head_dim, width // copies
        ).transpose(2, 1, 3, 0, 4)
    else:
        fill = TEAM // per_shard
        out_mine = out_mine.reshape(HEADS // TEAM, 1, head_dim, -1)
        chosen = (jnp.arange(fill) == q // per_shard)[None, :, None, None]
        out_mine = jnp.where(chosen, out_mine, jnp.zeros((), BF))
        out_final = to_owner(out_mine.reshape(parts * head_dim, -1))
        out_grad = from_all(out_final).reshape(
            copies, fill, per_shard, head_dim, width // copies
        )
        out_grad = pick(out_grad, z % fill, 1).transpose(1, 2, 0, 3)
    out_grad = out_grad.reshape(-1, width).astype(F32)

    qkv_final = from_all(to_owner(over_copies(qkv_shares)))
    qkv_final = qkv_final.reshape(copies, TEAM, shard, 3, heads_each, head_dim)
    qkv_grads = [
        qkv_final[:, :, :, i].transpose(2, 0, 3, 1, 4).reshape(shard, width).astype(F32)
        for i in range(3)
    ]

    def place_heads(shares):
        full = jnp.zeros((copies, heads_each, TEAM, head_dim), F32)
        for m in range(copies):
            share = shares[m].reshape(1, heads_each, 1, head_dim)
            full = lax.dynamic_update_slice(full, share, (d ^ m, 0, q, 0))
        return full.reshape(width)

    up_sums = jnp.zeros((parts, reps, unit), F32)
    for m in range(copies):
        share = sum(jnp.sum(pair[m].astype(F32), axis=0) for pair in dbefores)
        up_sums = lax.dynamic_update_slice(
            up_sums, share.reshape(parts, 1, unit), (0, rep ^ (TEAM * m), 0)
        )
    sums = [
        place_heads(query_sums),
        place_heads(value_sums),
        out_bias_grad,
        gain_one_grad,
        shift_one_grad,
        down_bias_grad,
        gain_two_grad,
        shift_two_grad,
    ]
    sums = jnp.concatenate([s.reshape(parts, shard) for s in sums] + [up_sums.reshape(parts, -1)], axis=1)
    sums = pick(lax.psum(sums, ("rep", "fsdp")), z)
    small = [sums[i * shard : (i + 1) * shard] for i in range(8)]
    up_bias_grad = sums[8 * shard :]
    return (
        layer_out,
        tokens_grad,
        qkv_grads[0],
        qkv_grads[1],
        qkv_grads[2],
        out_grad,
        small[0],
        small[1],
        small[2],
        small[3],
        small[4],
        up_grad,
        up_bias_grad,
        down_grad,
        small[5],
        small[6],
        small[7],
    )


def solution(mesh):
    three, two, one = P("rep", "fsdp", None), P("fsdp", None), P("fsdp")
    placed = (three, P("rep"), two, two, two, two, one, one, one, one, one)
    placed += (two, one, two, one, one, one, three)
    given = (three, three, two, two, two, two, one, one, one, one, one)
    given += (two, one, two, one, one, one)
    return jax.shard_map(local, mesh=mesh, in_specs=placed, out_specs=given, check_vma=False)
```

```python
import jax
import jax.numpy as jnp
from jax import lax
from jax.experimental import pallas as pl
from jax.experimental.pallas import tpu as pltpu
from jax.sharding import PartitionSpec as P

HEADS = 16
TEAM = 4
LANES = 128
EPSILON = 1e-06
BF = jnp.bfloat16
F32 = jnp.float32
VMEM_LIMIT = 48 * 1024 * 1024
FREE = pl.CostEstimate(flops=0, bytes_accessed=0, transcendentals=0)

(
    QKV_Z,
    OUT_Z,
    UP_Z,
    DOWN_Z,
    FAR,
    QKV,
    OTHER,
    MINE,
    BOTH,
    CONTEXT,
    KEPT,
    AWAY,
    OUT_SWAPPED,
    SEND,
    BACK,
    UP,
    THEIRS,
    ATTENDED,
    HIDDEN,
    VALUE,
    SLOPE,
    DOWN,
    PARTIAL,
    COTANGENT,
    COT,
    NORMAL2,
    DDOWN,
    RESULT,
    LAYER,
    DBEFORE,
    SHARE,
    RECEIVED,
    PART,
    DATTN,
    DATTN_NEAR,
    DATTN_FAR,
    DATTN_MINE,
    DQKV,
    OUT,
    WHOLE,
    VECTOR,
    DATTN_OTHER,
    OWN,
    GRAD,
) = range(44)


def mm(left, right):
    return jnp.dot(left, right, preferred_element_type=F32)


def mm_t(left, right):
    return lax.dot_general(left, right, (((1,), (1,)), ((), ())), preferred_element_type=F32)


def t_mm(left, right):
    return lax.dot_general(left, right, (((0,), (0,)), ((), ())), preferred_element_type=F32)


def pick(array, index, axis=0):
    return lax.dynamic_index_in_dim(array, index, axis, keepdims=False)


def tie(*arrays):
    return lax.optimization_barrier(arrays)


def normalise(summed):
    center = summed - jnp.mean(summed, axis=-1, keepdims=True)
    spread = jnp.mean(center * center, axis=-1, keepdims=True)
    scale = lax.rsqrt(spread + EPSILON)
    return center * scale, scale


def norm_backward(grad, gain, normal, scale):
    dn = grad * gain
    first = jnp.mean(dn, axis=-1, keepdims=True)
    second = jnp.mean(dn * normal, axis=-1, keepdims=True)
    return scale * (dn - first - normal * second)


def gelu_parts(u):
    inner = 0.7978845608 * (u + 0.044715 * u * u * u)
    t = jnp.tanh(inner)
    half = 0.5 * (1.0 + t)
    slope = half + 0.5 * u * (1.0 - t * t) * (0.7978845608 + 0.7978845608 * 0.134145 * u * u)
    return u * half, slope


def dot(kind, pairs, finish, outs, columns=(), tiles=(), left=(0, 1), right=(0, 1), strip=256):
    count = len(pairs)
    xs, ws = [x for x, _ in pairs], [w for _, w in pairs]
    flip = kind == "tn"
    m = xs[0].shape[1] // left[1] if flip else xs[0].shape[0]
    n = ws[0].shape[0] if kind == "nt" else ws[0].shape[1] // right[1]
    depths = [x.shape[0] if flip else x.shape[1] for x in xs]
    by_rows = flip and m > n
    size = m if by_rows else n
    step = next((s for s in (512, 384, 256) if size % s == 0), size)
    m_block, n_block = (step, n) if by_rows else (m, step)
    strip = strip if m_block % strip == 0 else m_block
    inputs = 2 * count + len(columns) + len(tiles)

    def kernel(*refs):
        x_refs, w_refs = refs[:count], refs[count : 2 * count]
        column_refs = refs[2 * count : 2 * count + len(columns)]
        tile_refs = refs[2 * count + len(columns) : inputs]
        out_refs = refs[inputs : inputs + len(outs)]
        if flip:
            flipped = refs[inputs + len(outs) :]

            def turn():
                for a, b in zip(flipped, x_refs, strict=True):
                    a[...] = b[...].T

            if by_rows:
                turn()
            else:
                pl.when(pl.program_id(0) == 0)(turn)
            x_refs = flipped
        for at in range(0, m_block, strip):
            some = slice(at, at + strip)
            total = 0.0
            for x, w in zip(x_refs, w_refs, strict=True):
                product = mm_t(x[some, :], w[...]) if kind == "nt" else mm(x[some, :], w[...])
                total = total + product
            extra = [c[...] for c in column_refs] + [t[some, :] for t in tile_refs]
            for ref, value in zip(out_refs, finish(total, *extra), strict=True):
                ref[some, :] = value.astype(ref.dtype)

    if by_rows:
        per = left[0] * (m // step)
        x_specs = [pl.BlockSpec((k, step), lambda j: (0, per + j)) for k in depths]
        w_specs = [pl.BlockSpec((k, n), lambda j: (0, right[0])) for k in depths]
        out_spec = pl.BlockSpec((step, n), lambda j: (j, 0))
    else:
        per = right[0] * (n // step)
        if flip:
            x_specs = [pl.BlockSpec((k, m), lambda j: (0, left[0])) for k in depths]
        else:
            x_specs = [pl.BlockSpec((m, k), lambda j: (0, 0)) for k in depths]
        if kind == "nt":
            w_specs = [pl.BlockSpec((step, k), lambda j: (j, 0)) for k in depths]
        else:
            w_specs = [pl.BlockSpec((k, step), lambda j: (0, per + j)) for k in depths]
        out_spec = pl.BlockSpec((m, step), lambda j: (0, j))
    results = pl.pallas_call(
        kernel,
        grid=(size // step,),
        in_specs=x_specs
        + w_specs
        + [pl.BlockSpec((1, step), lambda j: (0, j))] * len(columns)
        + [out_spec] * len(tiles),
        out_specs=[out_spec] * len(outs),
        out_shape=[jax.ShapeDtypeStruct((m, n), t) for t in outs],
        scratch_shapes=[pltpu.VMEM((m_block, k), BF) for k in depths] if flip else [],
        compiler_params=pltpu.CompilerParams(vmem_limit_bytes=VMEM_LIMIT),
        cost_estimate=FREE,
    )(*xs, *ws, *columns, *tiles)
    return results if len(outs) > 1 else results[0]


def plain(total):
    return (total,)


def attend(qkv, mask, heads):
    rows = qkv.shape[0]
    head_dim = qkv.shape[1] // (3 * heads)
    scaling = head_dim ** (-0.5)
    step = min(256, rows)

    def kernel(qkv_ref, mask_ref, context_ref, total_ref):
        keys = qkv_ref[:, head_dim : 2 * head_dim]
        values = qkv_ref[:, 2 * head_dim :]
        keep = mask_ref[...] > 0
        for at in range(0, rows, step):
            query = qkv_ref[at : at + step, :head_dim]
            scores = jnp.where(keep, mm_t(query, keys) * scaling, -1e30)
            most = jnp.max(scores, axis=1, keepdims=True)
            shares = jnp.exp(scores - most)
            total = jnp.sum(shares, axis=1, keepdims=True)
            probs = (shares * (1.0 / total)).astype(BF)
            context_ref[at : at + step, :] = mm(probs, values).astype(BF)
            log_total = jnp.broadcast_to(most + jnp.log(total), (step, 128))
            total_ref[0, :, at : at + step] = jnp.transpose(log_total)[0:1, :]

    return pl.pallas_call(
        kernel,
        grid=(heads,),
        in_specs=[
            pl.BlockSpec((rows, 3 * head_dim), lambda h: (0, h)),
            pl.BlockSpec((1, rows), lambda h: (0, 0)),
        ],
        out_specs=[
            pl.BlockSpec((rows, head_dim), lambda h: (0, h)),
            pl.BlockSpec((1, 1, rows), lambda h: (h, 0, 0)),
        ],
        out_shape=[
            jax.ShapeDtypeStruct((rows, heads * head_dim), BF),
            jax.ShapeDtypeStruct((heads, 1, rows), F32),
        ],
        compiler_params=pltpu.CompilerParams(vmem_limit_bytes=VMEM_LIMIT),
        cost_estimate=FREE,
    )(qkv, mask)


def attend_backward(qkv, dcontext, log_total, mask, heads, part):
    rows = qkv.shape[0]
    head_dim = qkv.shape[1] // (3 * heads)
    scaling = head_dim ** (-0.5)
    step = min(256, rows)

    def kernel(qkv_ref, dcontext_ref, total_ref, mask_ref, dqkv_ref, sums_ref):
        keys = qkv_ref[:, head_dim : 2 * head_dim]
        values = qkv_ref[:, 2 * head_dim :]
        keep = mask_ref[...] > 0
        dkeys, dvalues, query_sum = 0.0, 0.0, 0.0
        for at in range(0, rows, step):
            query = qkv_ref[at : at + step, :head_dim]
            dctx = dcontext_ref[at : at + step, :]
            scores = mm_t(keys, query) * scaling
            probs = jnp.exp(scores - total_ref[0, :, at : at + step])
            probs = jnp.where(keep, probs, 0.0)
            dprobs = mm_t(values, dctx)
            delta = jnp.sum(dprobs * probs, axis=0, keepdims=True)
            dscores = (probs * (dprobs - delta)).astype(BF)
            dvalues = dvalues + mm(probs.astype(BF), dctx)
            dkeys = dkeys + mm(dscores, query)
            dquery = (t_mm(dscores, keys) * scaling).astype(BF)
            dqkv_ref[at : at + step, :head_dim] = dquery
            query_sum = query_sum + jnp.sum(dquery.astype(F32), axis=0, keepdims=True)
        dvalues = dvalues.astype(BF)
        dqkv_ref[:, head_dim : 2 * head_dim] = (dkeys * scaling).astype(BF)
        dqkv_ref[:, 2 * head_dim :] = dvalues
        value_sum = jnp.sum(dvalues.astype(F32), axis=0, keepdims=True)
        sums_ref[...] = jnp.concatenate([query_sum, query_sum, value_sum], axis=1)

    return pl.pallas_call(
        kernel,
        grid=(heads,),
        in_specs=[
            pl.BlockSpec((rows, 3 * head_dim), lambda h: (0, h)),
            pl.BlockSpec((rows, head_dim), lambda h: (0, part * heads + h)),
            pl.BlockSpec((1, 1, rows), lambda h: (h, 0, 0)),
            pl.BlockSpec((rows, 1), lambda h: (0, 0)),
        ],
        out_specs=[
            pl.BlockSpec((rows, 3 * head_dim), lambda h: (0, h)),
            pl.BlockSpec((1, 3 * head_dim), lambda h: (0, h)),
        ],
        out_shape=[
            jax.ShapeDtypeStruct(qkv.shape, BF),
            jax.ShapeDtypeStruct((1, qkv.shape[1]), F32),
        ],
        compiler_params=pltpu.CompilerParams(vmem_limit_bytes=VMEM_LIMIT),
        cost_estimate=FREE,
    )(qkv, dcontext, log_total, mask)


def place_rows(pieces, places, shape):
    count, (rows, width) = len(pieces), pieces[0].shape

    def kernel(places_ref, *refs):
        for i in range(count):

            @pl.when(pl.program_id(0) == i)
            def _(i=i):
                refs[-1][...] = refs[i][...].astype(F32)

    return pl.pallas_call(
        kernel,
        grid_spec=pltpu.PrefetchScalarGridSpec(
            num_scalar_prefetch=1,
            grid=(count,),
            in_specs=[pl.BlockSpec((rows, width), lambda i, s: (0, 0))] * count,
            out_specs=pl.BlockSpec((rows, width), lambda i, s: (s[i], 0)),
        ),
        out_shape=jax.ShapeDtypeStruct(shape, F32),
        compiler_params=pltpu.CompilerParams(vmem_limit_bytes=VMEM_LIMIT),
        cost_estimate=FREE,
    )(jnp.stack(places).astype(jnp.int32), *pieces)


def place_columns(pieces, places, shape, block, column):
    count, (rows, width) = len(pieces), pieces[0].shape
    step = min(64, rows)

    def kernel(places_ref, *refs):
        for p in range(count):
            for i in range(width // block):
                at = pl.multiple_of(column(i, places_ref[p]) * block, block)
                value = refs[p][:, i * block : (i + 1) * block].astype(F32)
                refs[-1][:, pl.ds(at, block)] = value

    return pl.pallas_call(
        kernel,
        grid_spec=pltpu.PrefetchScalarGridSpec(
            num_scalar_prefetch=1,
            grid=(rows // step,),
            in_specs=[pl.BlockSpec((step, width), lambda i, s: (i, 0))] * count,
            out_specs=pl.BlockSpec((step, shape[1]), lambda i, s: (i, 0)),
        ),
        out_shape=jax.ShapeDtypeStruct(shape, F32),
        compiler_params=pltpu.CompilerParams(vmem_limit_bytes=VMEM_LIMIT),
        cost_estimate=FREE,
    )(jnp.stack(places).astype(jnp.int32), *pieces)


def take_columns(arrays, index, count, block):
    if block % LANES != 0:
        pieces = []
        for i in range(count):
            for w in arrays:
                pieces.append(lax.dynamic_slice_in_dim(w, index[i] * block, block, 1))
        return jnp.concatenate(pieces, axis=1)
    rows, n = arrays[0].shape[0], len(arrays)

    def kernel(index_ref, *refs):
        for i in range(n):
            refs[-1][:, i * block : (i + 1) * block] = refs[i][...]

    return pl.pallas_call(
        kernel,
        grid_spec=pltpu.PrefetchScalarGridSpec(
            num_scalar_prefetch=1,
            grid=(count,),
            in_specs=[pl.BlockSpec((rows, block), lambda i, s: (0, s[i]))] * n,
            out_specs=pl.BlockSpec((rows, n * block), lambda i, s: (0, i)),
        ),
        out_shape=jax.ShapeDtypeStruct((rows, count * n * block), BF),
        compiler_params=pltpu.CompilerParams(vmem_limit_bytes=VMEM_LIMIT),
        cost_estimate=FREE,
    )(jnp.stack(index).astype(jnp.int32), *arrays)


def place_heads_grad(gathered, reps, run, head_dim):
    shard = gathered.shape[1]
    step = min(64, shard)

    def kernel(in_ref, *outs):
        for r in range(reps):
            for j in range(run):
                at = (((r // TEAM) * run + j) * TEAM + r % TEAM) * head_dim
                for i in range(3):
                    start = (3 * j + i) * head_dim
                    value = in_ref[r, :, start : start + head_dim].astype(F32)
                    outs[i][:, at : at + head_dim] = value

    return pl.pallas_call(
        kernel,
        grid=(shard // step,),
        in_specs=[pl.BlockSpec((reps, step, run * 3 * head_dim), lambda i: (0, i, 0))],
        out_specs=[pl.BlockSpec((step, HEADS * head_dim), lambda i: (i, 0))] * 3,
        out_shape=[jax.ShapeDtypeStruct((shard, HEADS * head_dim), F32)] * 3,
        compiler_params=pltpu.CompilerParams(vmem_limit_bytes=VMEM_LIMIT),
        cost_estimate=FREE,
    )(gathered)


def local(
    tokens,
    lengths,
    query_weight,
    key_weight,
    value_weight,
    out_weight,
    query_bias,
    value_bias,
    out_bias,
    first_gain,
    first_shift,
    up_weight,
    up_bias,
    down_weight,
    down_bias,
    second_gain,
    second_shift,
    cotangent,
):
    slots_here, block, width = tokens.shape
    reps, parts = lax.axis_size("rep"), lax.axis_size("fsdp")
    copies = reps // TEAM
    hidden = up_weight.shape[1]
    shard = query_weight.shape[0]
    head_dim = width // HEADS
    team_heads = HEADS // TEAM
    run = team_heads // copies
    rep, z = lax.axis_index("rep"), lax.axis_index("fsdp")
    q, d = rep % TEAM, rep // TEAM
    parity = z % 2
    held = TEAM * slots_here // parts
    rows = slots_here * block
    half = rows // 2
    unit = hidden // parts // reps
    wide = width // copies
    halves = 2 if unit % (2 * LANES) == 0 else 1
    half_unit = unit // halves
    per_shard = HEADS // parts

    def swap(x, mask):
        return lax.ppermute(x, "rep", [(i, i ^ mask) for i in range(reps)])

    def shift(x, by):
        return lax.ppermute(x, "fsdp", [(i, (i - by) % parts) for i in range(parts)])

    def from_next(k):
        return (z + k) % parts

    def routes(turn):
        pairs = []
        for copy in range(copies):
            for member in range(TEAM):
                for place in range(parts):
                    slot = member * slots_here + (place + turn) % 2
                    to_member = ((slot // parts) * parts + place) // 2
                    source = (copy * TEAM + member) * parts + place
                    target = (copy * TEAM + to_member) * parts + slot % parts
                    pairs.append((source, target))
        return pairs

    even, odd = routes(0), routes(1)
    axes = ("rep", "fsdp")
    v = {}

    def order(*names):
        names = list(dict.fromkeys(names))
        v.update(zip(names, tie(*[v[n] for n in names]), strict=True))

    def to_team(x):
        first = lax.ppermute(pick(x, parity), axes, even)
        second = lax.ppermute(pick(x, 1 - parity), axes, odd)
        return first, second

    def from_team(first, second):
        return settle(*leave_team(first, second))

    def leave_team(first, second):
        first = lax.ppermute(first, axes, [(b, a) for a, b in even])
        second = lax.ppermute(second, axes, [(b, a) for a, b in odd])
        return first, second

    def settle(first, second):
        straight = jnp.stack([first, second])
        turned = jnp.stack([second, first])
        return jnp.where(parity == 0, straight, turned)

    vectors = jnp.concatenate(
        [
            query_bias,
            value_bias,
            out_bias,
            first_gain,
            first_shift,
            down_bias,
            second_gain,
            second_shift,
            up_bias,
        ]
    )[None]
    pieces = [vectors] + [shift(vectors, k) for k in range(1, parts)]
    there = [lengths] + [swap(lengths, m) for m in range(1, TEAM)]
    first, second = to_team(tokens)
    first, second, *pieces = tie(first, second, *pieces, *there)
    pieces, there = pieces[:parts], pieces[parts:]
    vectors = jnp.zeros((parts, vectors.shape[1]), BF)
    for k, piece in enumerate(pieces):
        vectors = lax.dynamic_update_slice(vectors, piece, (from_next(k), 0))
    vectors = vectors.astype(F32)
    names = [vectors[:, i * shard : (i + 1) * shard].reshape(width) for i in range(8)]
    bias_query, bias_value, bias_out, gain_one, shift_one, bias_down, gain_two, shift_two = names
    bias_up = vectors[:, 8 * shard :].reshape(parts, reps, unit)
    slot_lengths = jnp.zeros((TEAM, slots_here), jnp.int32)
    for m in range(TEAM):
        slot_lengths = lax.dynamic_update_slice(slot_lengths, there[m][None], (q ^ m, 0))
    slot_lengths = slot_lengths.reshape(-1)

    def live(member):
        place = [
            ((member * 2 + o) % parts) * block + jnp.arange(block) for o in (parity, 1 - parity)
        ]
        length = pick(slot_lengths, ((member * 2) // parts) * parts + z)
        return jnp.concatenate(place) < length

    masks = [live(q ^ m).astype(F32) for m in range(TEAM)]
    valid = masks[0][:, None]
    mask_mine, mask_other = jnp.concatenate(masks[:2]), jnp.concatenate(masks[2:])

    def head_columns(w, e):
        lead = w.shape[:-1]
        at = len(lead)
        split = w.reshape(lead + (copies, run, TEAM, head_dim))
        return pick(pick(split, e, at), q, at + 1)

    def over_z(x):
        return lax.all_gather(x, "fsdp", axis=0, tiled=True)

    def spread(x):
        return [x] + [swap(x, TEAM * m) for m in range(1, copies)]

    heads_here = [(d * run + j) * TEAM + q for j in range(run)]
    qkv_own = [
        take_columns([query_weight, key_weight, value_weight], [h], 1, head_dim)
        for h in heads_here
    ]
    split_out = out_weight.reshape(-1, head_dim, copies, wide)
    split_out = pick(split_out, d, 2)
    if per_shard >= TEAM:
        split_out = split_out.reshape(per_shard // TEAM, TEAM, head_dim, wide)
        out_own = pick(split_out, q, 1)
    else:
        out_own = pick(split_out, q % per_shard, 0)[None]
    up_own = [
        take_columns(
            [up_weight],
            [(t * reps + rep) * halves + h for t in range(parts)],
            parts,
            half_unit,
        )
        for h in range(halves)
    ]
    down_split = pick(down_weight.reshape(reps, halves, half_unit, width), rep)
    down_own = [down_split[h] for h in range(halves)]
    first, second, out_own, *own = tie(first, second, out_own, *qkv_own, *up_own, *down_own)
    qkv_own, up_own, down_own = own[:run], own[run : run + halves], own[run + halves :]
    for j in range(run):
        v[QKV_Z, j] = over_z(qkv_own[j])
    v[OUT_Z] = over_z(out_own)
    for h in range(halves):
        v[UP_Z, h] = over_z(up_own[h])
    for h in range(halves):
        v[DOWN_Z, h] = over_z(down_own[h])
    own_tokens = jnp.concatenate([first, second], axis=0)
    v[FAR, 0], v[FAR, 1] = swap(first, 2), swap(second, 2)
    near = [swap(x, 1) for x in (first, second)]
    order((FAR, 0), (FAR, 1), (QKV_Z, 0))
    for m in range(1, copies):
        v[QKV, 0, m] = swap(v[QKV_Z, 0], TEAM * m)
    far = [v[FAR, 0], v[FAR, 1]]
    far_near = [swap(x, 1) for x in far]

    def own_units(table, m):
        return pick(table, rep ^ (TEAM * m), 1).transpose(1, 0, 2).reshape(1, -1)

    bias_up = bias_up.reshape(parts, reps, halves, half_unit)
    up_biases = [own_units(bias_up, m) for m in range(copies)]
    qkv_bias = []
    for m in range(copies):
        qb, vb = head_columns(bias_query, d ^ m), head_columns(bias_value, d ^ m)
        qkv_bias.append(jnp.stack([qb, jnp.zeros_like(qb), vb], axis=1).reshape(1, -1))
    span = run * head_dim

    tokens_mine = jnp.concatenate([first, second] + near, axis=0)
    tokens_other = jnp.concatenate(far + far_near, axis=0)
    v[OTHER] = tokens_other
    order(OTHER, *[(QKV_Z, j) for j in range(run)])
    tokens_other = v[OTHER]
    for j in range(1, run):
        for m in range(1, copies):
            v[QKV, j, m] = swap(v[QKV_Z, j], TEAM * m)
    qkv_weight = {0: jnp.concatenate([v[QKV_Z, j] for j in range(run)], axis=1)}

    if held == 2:
        slots = (OTHER, MINE)
        v[MINE] = tokens_mine
        slot_masks = {OTHER: mask_other, MINE: mask_mine}
    else:
        slots = (BOTH,)
        v[BOTH] = jnp.concatenate([tokens_mine, tokens_other], axis=0)
        slot_masks = {BOTH: jnp.concatenate([mask_mine, mask_other])}
    log_totals = {}

    def project_step(name, m):
        v[QKV, name, m] = dot(
            "nn", [(v[name], qkv_weight[m])], lambda t, b: (t + b,), [BF], columns=[qkv_bias[m]]
        )

    def attend_only(name, m):
        qkv = v[QKV, name, m]
        context, log_totals[name, m] = attend(qkv, slot_masks[name][None], run)
        v[CONTEXT, name, m] = context

    def attend_step(name, m):
        project_step(name, m)
        attend_only(name, m)

    def out_step(name, kind):
        context = jnp.concatenate([v[CONTEXT, name, m] for m in range(copies)], axis=1)
        v[CONTEXT, name] = context
        return dot("nn", [(context, out_full)], plain, [kind])

    def add(x, received):
        total = x.astype(F32)
        for y in received:
            total = total + y.astype(F32)
        return total.astype(BF)

    def first_hop(partial):
        n = partial.shape[0] // 2
        v[KEPT], v[AWAY] = partial[:n], partial[n:]

    def next_hop():
        return add(v[KEPT], [v[AWAY]])

    attend_step(slots[0], 0)
    if held == 2:
        order(MINE, (CONTEXT, OTHER, 0))
        attend_step(MINE, 0)
    order(
        (CONTEXT, slots[-1], 0),
        OUT_Z,
        *[(QKV, j, m) for j in range(run) for m in range(1, copies)],
    )
    out_z = v[OUT_Z]
    if per_shard < TEAM:
        fill = TEAM // per_shard
        out_z = out_z.reshape(HEADS // TEAM, fill, head_dim, wide)
        out_z = pick(out_z, q // per_shard, 1)
    out_z = out_z.reshape(team_heads * head_dim, wide)
    out_swapped = [out_z] + [swap(out_z, TEAM * m) for m in range(1, copies)]
    for m in range(1, copies):
        qkv_weight[m] = jnp.concatenate([v[QKV, j, m] for j in range(run)], axis=1)
        attend_step(slots[0], m)
        if m == 1:
            v[OUT_SWAPPED] = jnp.stack(out_swapped)
            order(OUT_SWAPPED, (CONTEXT, slots[0], m))
    out_columns = v[OUT_SWAPPED]
    out_full = jnp.concatenate([pick(out_columns, d ^ e) for e in range(copies)], axis=1)
    out_rows = [
        lax.dynamic_slice_in_dim(out_full, (d ^ m) * span, span, 0) for m in range(copies)
    ]
    out_full = jnp.concatenate(out_rows, axis=0)
    if held == 2:
        first_hop(out_step(OTHER, BF))
        order(KEPT, AWAY, MINE)
        v[AWAY] = swap(v[AWAY], 1)
        project_step(MINE, 1)
        order(AWAY, (QKV, MINE, 1))
        v[SEND] = next_hop()
        order(SEND, (QKV, MINE, 1), (UP_Z, 0))
        v[BACK] = swap(v[SEND], 2)
        for m in range(1, copies):
            if m > 1:
                project_step(MINE, m)
            attend_only(MINE, m)
        partial = out_step(MINE, F32)
    else:
        order((CONTEXT, BOTH, 0), (UP_Z, 0))
        partial = out_step(BOTH, F32)
        first_hop(partial[2 * rows :].astype(BF))
        v[AWAY] = swap(v[AWAY], 1)
        v[BACK] = swap(next_hop(), 2)
        partial = partial[: 2 * rows]
    for m in range(1, copies):
        v[UP, 0, m] = swap(v[UP_Z, 0], TEAM * m)
    v[THEIRS] = partial[rows:].astype(BF)
    order(
        THEIRS,
        BACK,
        *[(UP_Z, h) for h in range(1, halves)],
        *[(UP, 0, m) for m in range(1, copies)],
    )
    for h in range(1, halves):
        for m in range(1, copies):
            v[UP, h, m] = swap(v[UP_Z, h], TEAM * m)
    v[ATTENDED] = partial[:rows] + swap(v[THEIRS], 1).astype(F32)
    summed1 = own_tokens.astype(F32) + v[ATTENDED] + v[BACK].astype(F32) + bias_out
    normal1, scale1 = normalise(summed1)
    normed1 = normal1 * gain_one + shift_one

    def first_swaps(own):
        return [swap(own[:half], 2), swap(own[half:], 2)], swap(own, 1)

    def chunk_of(far_rows):
        return jnp.concatenate([far_rows, swap(far_rows, 1)], axis=0)

    def chunk_sum(sums):
        mine, theirs, backs = sums
        return mine + theirs.astype(F32) + jnp.concatenate(backs, axis=0).astype(F32)

    v[HIDDEN, 0] = normed1.astype(BF)
    (v[FAR, 0], v[FAR, 1]), v[HIDDEN, 1] = first_swaps(v[HIDDEN, 0])
    up_parts = {0: jnp.concatenate([v[UP_Z, h] for h in range(halves)], axis=1)}

    def up_step(i, m):
        v[VALUE, i, m], v[SLOPE, i, m] = dot(
            "nn",
            [(v[HIDDEN, i], up_parts[m])],
            lambda t, b: gelu_parts(t + b),
            [BF, BF],
            columns=[up_biases[m]],
        )

    up_step(0, 0)
    order(
        (HIDDEN, 1),
        (VALUE, 0, 0),
        *[(UP, h, m) for h in range(1, halves) for m in range(1, copies)],
    )
    up_step(1, 0)
    order((FAR, 0), (VALUE, 1, 0), (DOWN_Z, 0))
    for m in range(1, copies):
        v[DOWN, 0, m] = swap(v[DOWN_Z, 0], TEAM * m)
    v[HIDDEN, 2] = chunk_of(v[FAR, 0])
    up_step(2, 0)
    order((FAR, 1), (VALUE, 2, 0))
    v[HIDDEN, 3] = chunk_of(v[FAR, 1])
    up_step(3, 0)
    for m in range(1, copies):
        up_parts[m] = jnp.concatenate([v[UP, h, m] for h in range(halves)], axis=1)
        for i in (2, 3, 0, 1):
            up_step(i, m)
            if m == 1 and i == 3:
                order(
                    (VALUE, 3, 1),
                    (VALUE, 2, 1),
                    (HIDDEN, 0),
                    (HIDDEN, 1),
                    *[(DOWN_Z, h) for h in range(1, halves)],
                    *[(DOWN, 0, n) for n in range(1, copies)],
                )
                for h in range(1, halves):
                    for n in range(1, copies):
                        v[DOWN, h, n] = swap(v[DOWN_Z, h], TEAM * n)
    order(
        *[(VALUE, i, m) for i in range(2) for m in range(copies)],
        *[(DOWN, h, m) for h in range(1, halves) for m in range(1, copies)],
    )
    down_parts = {0: jnp.concatenate([v[DOWN_Z, h] for h in range(halves)], axis=0)}
    for m in range(1, copies):
        down_parts[m] = jnp.concatenate([v[DOWN, h, m] for h in range(halves)], axis=0)

    def down_step(i):
        pairs = [(v[VALUE, i, m], down_parts[m]) for m in range(copies)]
        v[PARTIAL, i] = dot("nn", pairs, plain, [F32 if i == 0 else BF])

    def hop_start(i):
        first_hop(v[PARTIAL, i])
        order(KEPT, AWAY)
        v[AWAY] = swap(v[AWAY], 1)

    def hop_end(i, *beside):
        order(KEPT, AWAY, *beside)
        v[SEND, i] = next_hop()
        order((SEND, i), *beside)
        v[BACK, i] = swap(v[SEND, i], 2)

    down_step(2)
    hop_start(2)
    down_step(3)
    hop_end(2, (PARTIAL, 3))
    hop_start(3)
    down_step(1)
    hop_end(3, (PARTIAL, 1))
    order((PARTIAL, 1), (VALUE, 0, 0), (BACK, 2))
    v[THEIRS] = swap(v[PARTIAL, 1], 1)
    down_step(0)
    order((PARTIAL, 0), THEIRS, (BACK, 2), (BACK, 3))
    theirs = v[THEIRS]
    backs = [v[BACK, 2], v[BACK, 3]]
    summed2 = normed1 + chunk_sum((v[PARTIAL, 0], theirs, backs)) + bias_down
    normal2, scale2 = normalise(summed2)
    result = (valid * (normal2 * gain_two + shift_two)).astype(BF)

    v[COTANGENT] = cotangent
    order(COTANGENT, (VALUE, 3, 0))
    v[COT, 0], v[COT, 1] = to_team(v[COTANGENT])
    v[NORMAL2] = normal2
    order(NORMAL2, (COT, 0), (COT, 1))
    normal2 = v[NORMAL2]
    grad_out = jnp.concatenate([v[COT, 0], v[COT, 1]], axis=0).astype(F32) * valid
    dsum2 = norm_backward(grad_out, gain_two, normal2, scale2)
    gain_two_grad = jnp.sum(grad_out * normal2, axis=0)
    shift_two_grad = jnp.sum(grad_out, axis=0)
    v[DDOWN, 0] = dsum2.astype(BF)
    down_bias_grad = jnp.sum(v[DDOWN, 0].astype(F32), axis=0)
    v[RESULT] = result
    order(RESULT, (DDOWN, 0))
    v[LAYER, 0], v[LAYER, 1] = leave_team(v[RESULT][:block], v[RESULT][block:])

    def over_copies(shares):
        total = shares[0].astype(F32)
        for m in range(1, copies):
            total = total + swap(shares[m], TEAM * m).astype(F32)
        return total.astype(BF)

    def to_owner(x):
        return lax.psum_scatter(x, "fsdp", scatter_dimension=0, tiled=True)

    def from_all(x):
        return lax.all_gather(x, "rep", axis=0, tiled=True)

    def in_order(pieces):
        stacked = jnp.stack([pieces[m] for m in range(reps)])
        return jnp.stack([pick(stacked, rep ^ r) for r in range(reps)])

    sub = parts * half_unit

    def backward_step(i):
        for m in range(copies):
            v[DBEFORE, i, m] = dot(
                "nt",
                [(v[DDOWN, i], down_parts[m])],
                lambda t, s: (t * s.astype(F32),),
                [BF],
                tiles=[v[SLOPE, i, m]],
            )
        pairs = [(v[DBEFORE, i, m], up_parts[m]) for m in range(copies)]
        v[PARTIAL, i] = dot("nt", pairs, plain, [F32 if i == 0 else BF])

    def down_grad_step(m, h):
        pairs = [(v[VALUE, i, m], v[DDOWN, i]) for i in range(4)]
        v[DOWN, SHARE, h, m] = dot("tn", pairs, plain, [BF], left=(h, halves))

    def up_grad_step(m, h):
        pairs = [(v[HIDDEN, i], v[DBEFORE, i, m]) for i in range(4)]
        v[UP, SHARE, h, m] = dot("tn", pairs, plain, [BF], right=(h, halves))

    def swap_share(kind, h):
        for m in range(1, copies):
            v[kind, RECEIVED, h, m] = swap(v[kind, SHARE, h, m], TEAM * m)

    def shares(kind, *those):
        return [(kind, SHARE, h, m) for h in those for m in range(1, copies)]

    def received(kind, *those):
        return [(kind, RECEIVED, h, m) for h in those for m in range(1, copies)]

    def reduce_step(kind, h):
        total = add(v[kind, SHARE, h, 0], [v[n] for n in received(kind, h)])
        v[kind, PART, h] = to_owner(total)

    more = range(1, copies)
    late = range(1, halves)
    far, v[DDOWN, 1] = first_swaps(v[DDOWN, 0])
    v[FAR, 0], v[FAR, 1] = far
    backward_step(0)
    order((DDOWN, 1), (PARTIAL, 0))
    backward_step(1)
    order((PARTIAL, 1), (FAR, 0), (FAR, 1))
    v[THEIRS] = swap(v[PARTIAL, 1], 1)
    for i in (2, 3):
        v[DDOWN, i] = chunk_of(v[FAR, i - 2])
    for h in range(halves):
        for m in more:
            down_grad_step(m, h)
    order(*shares(DOWN, *range(halves)), (DDOWN, 2))
    for h in range(halves):
        swap_share(DOWN, h)
    backward_step(2)
    hop_start(2)
    order((PARTIAL, 2), (DDOWN, 3))
    backward_step(3)
    hop_end(2, (PARTIAL, 3), (DDOWN, 0))
    hop_start(3)
    order((PARTIAL, 3), (DDOWN, 0))
    down_grad_step(0, 0)
    hop_end(3, (DOWN, SHARE, 0, 0), (DDOWN, 0), (LAYER, 0), (LAYER, 1))
    for h in late:
        down_grad_step(0, h)
    order(*[(DOWN, SHARE, h, 0) for h in range(halves)], *received(DOWN, 0), (BACK, 2))
    reduce_step(DOWN, 0)
    order(
        (PARTIAL, 0),
        (BACK, 2),
        (BACK, 3),
        THEIRS,
        *[(DOWN, SHARE, h, 0) for h in late],
    )
    backs = [v[BACK, 2], v[BACK, 3]]
    dnormed1 = dsum2 + chunk_sum((v[PARTIAL, 0], v[THEIRS], backs))
    dsum1 = norm_backward(dnormed1, gain_one, normal1, scale1)
    gain_one_grad = jnp.sum(dnormed1 * normal1, axis=0)
    shift_one_grad = jnp.sum(dnormed1, axis=0)
    v[DATTN] = dsum1.astype(BF)
    out_bias_grad = jnp.sum(v[DATTN].astype(F32), axis=0)

    order((HIDDEN, 0), DATTN)
    v[DATTN_NEAR] = swap(v[DATTN], 1)
    v[DATTN_FAR] = swap(v[DATTN], 2)
    for h in range(halves):
        for m in more:
            up_grad_step(m, h)
    order(
        *shares(UP, *range(halves)),
        DATTN_NEAR,
        (HIDDEN, 0),
        *received(DOWN, *late),
        *[(DOWN, SHARE, h, 0) for h in late],
    )
    for h in range(halves):
        swap_share(UP, h)
    for h in late:
        reduce_step(DOWN, h)

    v[DATTN_MINE] = jnp.concatenate([v[DATTN], v[DATTN_NEAR]], axis=0)
    qkv_sums = {}

    def back_step(name, dcontext, m):
        v[DQKV, name, m], qkv_sums[name, m] = attend_backward(
            v[QKV, name, m], dcontext, log_totals[name, m], slot_masks[name][:, None], run, m
        )

    def context_grad(x):
        return dot("nt", [(x, out_full)], plain, [BF])

    def far_rows():
        return jnp.concatenate([v[DATTN_FAR], swap(v[DATTN_FAR], 1)], axis=0)

    def out_grad_step():
        pairs = [(v[CONTEXT, MINE], v[DATTN_MINE]), (v[CONTEXT, OTHER], dattn_other)]
        share = dot("tn", pairs, plain, [BF])
        for m in range(copies):
            rows_of = [
                lax.dynamic_slice(share, ((d ^ e) * span, (d ^ m) * wide), (span, wide))
                for e in range(copies)
            ]
            v[OUT, SHARE, 0, m] = jnp.concatenate(rows_of, axis=0)

    def out_reduce_step():
        total = add(v[OUT, SHARE, 0, 0], [v[n] for n in received(OUT, 0)])
        if per_shard < TEAM:
            fill = TEAM // per_shard
            total = total.reshape(HEADS // TEAM, 1, head_dim, -1)
            chosen = (jnp.arange(fill) == q // per_shard)[None, :, None, None]
            total = jnp.where(chosen, total, jnp.zeros((), BF))
            total = total.reshape(parts * head_dim, -1)
        v[OUT, PART, 0] = to_owner(total)

    def to_more(kind, mask):
        for m in [m for m in range(reps) if (kind, WHOLE, m) in v]:
            v[kind, WHOLE, m ^ mask] = swap(v[kind, WHOLE, m], mask)

    def all_of(kind):
        return [(kind, WHOLE, m) for m in range(reps) if (kind, WHOLE, m) in v]

    near_far = [2] + [TEAM << i for i in range(copies.bit_length() - 1)]

    def vector_table():
        def place_heads(i):
            full = jnp.zeros((copies, run, TEAM, head_dim), F32)
            for m in range(copies):
                share = sum(qkv_sums[name, m] for name in names)
                share = share.reshape(run, 3, head_dim)[:, i].reshape(1, run, 1, head_dim)
                full = lax.dynamic_update_slice(full, share, (d ^ m, 0, q, 0))
            return full.reshape(width)

        up_sums = jnp.zeros((parts, reps, halves, half_unit), F32)
        for m in range(copies):
            share = sum(jnp.sum(v[DBEFORE, i, m].astype(F32), axis=0) for i in range(4))
            share = share.reshape(halves, parts, half_unit).transpose(1, 0, 2)[:, None]
            up_sums = lax.dynamic_update_slice(up_sums, share, (0, rep ^ (TEAM * m), 0, 0))
        vector_sums = [
            place_heads(0),
            place_heads(2),
            out_bias_grad,
            gain_one_grad,
            shift_one_grad,
            down_bias_grad,
            gain_two_grad,
            shift_two_grad,
        ]
        return jnp.concatenate(
            [s.reshape(parts, shard) for s in vector_sums] + [up_sums.reshape(parts, -1)], axis=1
        )

    def vector_start():
        vector_sums = vector_table()
        v[VECTOR, 0] = pick(vector_sums, z)
        for k in range(1, parts):
            v[VECTOR, k] = shift(pick(vector_sums, (z - k) % parts), k)

    def vector_names():
        return [(VECTOR, k) for k in range(parts)]

    def vector_step(mask):
        if mask == 1:
            v[VECTOR, 0] = sum(v[n] for n in vector_names())
        v[VECTOR, 0] = v[VECTOR, 0] + swap(v[VECTOR, 0], mask)

    backwards = list(reversed(range(copies)))
    if held == 2:
        names = (MINE, OTHER)
        dcontext = context_grad(v[DATTN_MINE])
        for m in backwards:
            back_step(MINE, dcontext, m)
        order(
            DATTN_FAR,
            *[(DQKV, MINE, m) for m in range(copies)],
        )
        v[DATTN_OTHER] = far_rows()
        dattn_other = v[DATTN_OTHER]
        out_grad_step()
        order(*[(OUT, SHARE, 0, m) for m in range(copies)], DATTN_OTHER, (HIDDEN, 0))
        swap_share(OUT, 0)
        up_grad_step(0, 0)
        order(DATTN_OTHER, *received(UP, 0), (UP, SHARE, 0, 0))
        reduce_step(UP, 0)
        dattn_other = v[DATTN_OTHER]
        dcontext = context_grad(dattn_other)
        for m in backwards:
            back_step(OTHER, dcontext, m)
    else:
        names = (BOTH,)
        dattn_other = far_rows()
        dattn_both = jnp.concatenate([v[DATTN_MINE], dattn_other], axis=0)
        dcontext = context_grad(dattn_both)
        for m in backwards:
            back_step(BOTH, dcontext, m)
        up_grad_step(0, 0)
        reduce_step(UP, 0)
        v[CONTEXT, MINE] = v[CONTEXT, BOTH][: 2 * rows]
        v[CONTEXT, OTHER] = v[CONTEXT, BOTH][2 * rows :]
        out_grad_step()
        swap_share(OUT, 0)
        for m in range(copies):
            v[DQKV, MINE, m] = v[DQKV, BOTH, m][: 2 * rows]
            v[DQKV, OTHER, m] = v[DQKV, BOTH, m][2 * rows :]
    order(
        *[(DQKV, OTHER, m) for m in range(copies)],
        *[(DOWN, PART, h) for h in range(halves)],
    )
    vector_start()
    v[DOWN, WHOLE, 0] = jnp.concatenate([v[DOWN, PART, h] for h in range(halves)], axis=0)
    to_more(DOWN, near_far[0])

    def qkv_grad_step(m):
        pairs = [(tokens_mine, v[DQKV, MINE, m]), (tokens_other, v[DQKV, OTHER, m])]
        v[QKV, SHARE, 0, m] = dot("tn", pairs, plain, [BF])

    def dtokens_partial(name, kind):
        pairs = [(v[DQKV, name, m], qkv_weight[m]) for m in range(copies)]
        return dot("nt", pairs, plain, [kind])

    for m in more:
        qkv_grad_step(m)
    first_hop(dtokens_partial(OTHER, BF))
    order(
        KEPT,
        AWAY,
        *[(DQKV, MINE, m) for m in range(copies)],
        *vector_names(),
        (HIDDEN, 0),
    )
    v[AWAY] = swap(v[AWAY], 1)
    vector_step(1)
    qkv_grad_step(0)
    for h in late:
        up_grad_step(0, h)
    order(
        *shares(QKV, 0),
        (QKV, SHARE, 0, 0),
        KEPT,
        AWAY,
        *received(OUT, 0),
        (OUT, SHARE, 0, 0),
        *received(UP, *late),
        *[(UP, SHARE, h, 0) for h in late],
        *[(DQKV, MINE, m) for m in range(copies)],
    )
    swap_share(QKV, 0)
    v[SEND] = next_hop()
    v[BACK] = swap(v[SEND], 2)
    out_reduce_step()
    for h in late:
        reduce_step(UP, h)
    partial = dtokens_partial(MINE, F32)
    v[THEIRS] = partial[rows:].astype(BF)
    order(
        THEIRS,
        BACK,
        (QKV, SHARE, 0, 0),
        *received(QKV, 0),
        *all_of(DOWN),
        (OUT, PART, 0),
        *[(UP, PART, h) for h in range(halves)],
        (VECTOR, 0),
    )
    reduce_step(QKV, 0)
    v[THEIRS] = swap(v[THEIRS], 1)
    v[OUT, WHOLE, 0] = v[OUT, PART, 0]
    v[UP, WHOLE, 0] = jnp.concatenate([v[UP, PART, h] for h in range(halves)], axis=1)
    far_near = near_far[1:] + near_far[:1]
    to_more(UP, far_near[0])
    to_more(OUT, far_near[0])
    order(THEIRS, BACK, *all_of(UP), *all_of(OUT), *all_of(DOWN))
    for i, mask in enumerate(far_near[1:]):
        to_more(UP, mask)
        to_more(OUT, mask)
        to_more(DOWN, near_far[1 + i])
    vector_step(2)
    dtokens = dsum1 + partial[:rows] + v[THEIRS].astype(F32) + v[BACK].astype(F32)
    v[OWN] = dtokens.astype(BF)
    order(
        (QKV, PART, 0),
        OWN,
        (VECTOR, 0),
        *all_of(UP),
        *all_of(OUT),
        *all_of(DOWN),
    )
    qkv_part = lax.all_gather(v[QKV, PART, 0], "rep", axis=0, tiled=False)
    v[GRAD, 0], v[GRAD, 1] = leave_team(v[OWN][:block], v[OWN][block:])
    to_more(UP, 1)
    to_more(DOWN, 1)
    to_more(OUT, 1)
    for mask in near_far[1:]:
        vector_step(mask)
    order(*all_of(UP), *all_of(OUT), *all_of(DOWN), (VECTOR, 0))
    layer_out = settle(v[LAYER, 0], v[LAYER, 1])
    tokens_grad = settle(v[GRAD, 0], v[GRAD, 1]).astype(F32)
    out_grad = in_order({m: v[OUT, WHOLE, m] for m in range(reps)})

    if per_shard >= TEAM:
        out_grad = out_grad.reshape(copies, TEAM, per_shard // TEAM, head_dim, wide)
        out_grad = out_grad.transpose(2, 1, 3, 0, 4)
    else:
        fill = TEAM // per_shard
        out_grad = out_grad.reshape(copies, fill, per_shard, head_dim, wide)
        out_grad = pick(out_grad, z % fill, 1).transpose(1, 2, 0, 3)
    out_grad = out_grad.reshape(-1, width).astype(F32)

    aligned = half_unit % LANES == 0 and head_dim % LANES == 0
    if aligned:
        places = [rep ^ m for m in range(reps)]
        down_grad = place_rows(
            [v[DOWN, WHOLE, m] for m in range(reps)], places, (hidden // parts, width)
        )
        up_grad = place_columns(
            [v[UP, WHOLE, m] for m in range(reps)],
            places,
            (shard, hidden),
            half_unit,
            lambda i, r: ((i % parts) * reps + r) * halves + i // parts,
        )
        qkv_grads = place_heads_grad(qkv_part, reps, run, head_dim)
    else:
        def in_order_of(kind):
            return in_order({m: v[kind, WHOLE, m] for m in range(reps)})

        down_grad = in_order_of(DOWN).reshape(-1, width).astype(F32)
        up_grad = in_order_of(UP).reshape(reps, shard, halves, parts, half_unit)
        up_grad = up_grad.transpose(1, 3, 0, 2, 4).reshape(shard, hidden).astype(F32)
        qkv_final = qkv_part.reshape(copies, TEAM, shard, run, 3, head_dim)
        qkv_grads = [
            qkv_final[:, :, :, :, i].transpose(2, 0, 3, 1, 4).reshape(shard, width).astype(F32)
            for i in range(3)
        ]

    total = v[VECTOR, 0]
    small = [total[i * shard : (i + 1) * shard] for i in range(8)]
    up_bias_grad = total[8 * shard :]
    return (
        layer_out,
        tokens_grad,
        qkv_grads[0],
        qkv_grads[1],
        qkv_grads[2],
        out_grad,
        small[0],
        small[1],
        small[2],
        small[3],
        small[4],
        up_grad,
        up_bias_grad,
        down_grad,
        small[5],
        small[6],
        small[7],
    )


def solution(mesh):
    three, two, one = P("rep", "fsdp", None), P("fsdp", None), P("fsdp")
    placed = (three, P("rep"), two, two, two, two, one, one, one, one, one)
    placed += (two, one, two, one, one, one, three)
    given = (three, three, two, two, two, two, one, one, one, one, one)
    given += (two, one, two, one, one, one)
    return jax.shard_map(local, mesh=mesh, in_specs=placed, out_specs=given, check_vma=False)
```

```python
import jax
import jax.numpy as jnp
from jax import lax
from jax.experimental import pallas as pl
from jax.experimental.pallas import tpu as pltpu
from jax.sharding import PartitionSpec as P

HEADS = 16
TEAM = 4
LANES = 128
EPSILON = 1e-06
BF = jnp.bfloat16
F32 = jnp.float32
VMEM_LIMIT = 48 * 1024 * 1024
FREE = pl.CostEstimate(flops=0, bytes_accessed=0, transcendentals=0)

(
    ROWS,
    COLUMNS,
    QKV_Z,
    OUT_Z,
    UP_Z,
    DOWN_Z,
    FAR,
    QKV,
    OTHER,
    MINE,
    BOTH,
    CONTEXT,
    KEPT,
    AWAY,
    OUT_SWAPPED,
    SEND,
    BACK,
    OWN,
    THEIRS,
    UP,
    ATTENDED,
    NEAR,
    HIDDEN,
    VALUE,
    SLOPE,
    DOWN,
    COTANGENT,
    COT,
    NORMAL2,
    RESULT,
    LAYER,
    DBEFORE,
    DDOWN,
    SHARE,
    RECEIVED,
    PART,
    DATTN,
    DATTN_NEAR,
    DATTN_FAR,
    DATTN_MINE,
    DQKV,
    OUT,
    WHOLE,
    VECTOR,
    DATTN_OTHER,
    GRAD,
    DOWN_GRAD,
    UP_GRAD,
) = range(48)


def mm(left, right):
    return jnp.dot(left, right, preferred_element_type=F32)


def mm_t(left, right):
    return lax.dot_general(left, right, (((1,), (1,)), ((), ())), preferred_element_type=F32)


def t_mm(left, right):
    return lax.dot_general(left, right, (((0,), (0,)), ((), ())), preferred_element_type=F32)


def pick(array, index, axis=0):
    return lax.dynamic_index_in_dim(array, index, axis, keepdims=False)


def tie(*arrays):
    return lax.optimization_barrier(arrays)


def normalise(summed):
    center = summed - jnp.mean(summed, axis=-1, keepdims=True)
    spread = jnp.mean(center * center, axis=-1, keepdims=True)
    scale = lax.rsqrt(spread + EPSILON)
    return center * scale, scale


def norm_backward(grad, gain, normal, scale):
    dn = grad * gain
    first = jnp.mean(dn, axis=-1, keepdims=True)
    second = jnp.mean(dn * normal, axis=-1, keepdims=True)
    return scale * (dn - first - normal * second)


def gelu_parts(u):
    inner = 0.7978845608 * (u + 0.044715 * u * u * u)
    t = jnp.tanh(inner)
    half = 0.5 * (1.0 + t)
    slope = half + 0.5 * u * (1.0 - t * t) * (0.7978845608 + 0.7978845608 * 0.134145 * u * u)
    return u * half, slope


def dot(
    kind, pairs, finish, outs, columns=(), tiles=(), left=(0, 1), right=(0, 1), rows=(0, 1), split=None
):
    count = len(pairs)
    xs, ws = [x for x, _ in pairs], [w for _, w in pairs]
    flip = kind == "tn"
    m = xs[0].shape[1] // left[1] if flip else xs[0].shape[0] // rows[1]
    n = ws[0].shape[0] if kind == "nt" else ws[0].shape[1] // right[1]
    depths = [x.shape[0] if flip else x.shape[1] for x in xs]
    by_rows = flip and m > n
    size = m if by_rows else n
    step = next((s for s in (512, 384, 256) if size % s == 0), size)
    m_block, n_block = (step, n) if by_rows else (m, step)
    strip = next((s for s in (256, 128, 64) if (m_block // 2) % s == 0), m_block // 2)
    inputs = 2 * count + len(columns) + len(tiles)

    def kernel(*refs):
        x_refs, w_refs = refs[:count], refs[count : 2 * count]
        column_refs = refs[2 * count : 2 * count + len(columns)]
        tile_refs = refs[2 * count + len(columns) : inputs]
        out_refs = refs[inputs : inputs + len(outs)]
        if flip:
            flipped = refs[inputs + len(outs) :]

            def turn():
                for a, b in zip(flipped, x_refs, strict=True):
                    a[...] = b[...].T

            if by_rows:
                turn()
            else:
                pl.when(pl.program_id(0) == 0)(turn)
            x_refs = flipped
        for at in range(0, m_block, strip):
            some = slice(at, at + strip)
            total = 0.0
            for x, w in zip(x_refs, w_refs, strict=True):
                product = mm_t(x[some, :], w[...]) if kind == "nt" else mm(x[some, :], w[...])
                total = total + product
            extra = [c[...] for c in column_refs] + [t[some, :] for t in tile_refs]
            values = finish(total, *extra)
            if split == ROWS:
                to = at * 2 // m_block
                at = at - to * (m_block // 2)
                out_refs[to][at : at + strip, :] = values[0].astype(out_refs[to].dtype)
                continue
            if split == COLUMNS:
                values = values[0][:, : n_block // 2], values[0][:, n_block // 2 :]
            for ref, value in zip(out_refs, values, strict=True):
                ref[some, :] = value.astype(ref.dtype)

    m_out, n_out = m // 2 if split == ROWS else m, n // 2 if split == COLUMNS else n
    if by_rows:
        per = left[0] * (m // step)
        x_specs = [pl.BlockSpec((k, step), lambda j: (0, per + j)) for k in depths]
        w_specs = [pl.BlockSpec((k, n), lambda j: (0, right[0])) for k in depths]
        out_spec = pl.BlockSpec((step, n_out), lambda j: (j, 0))
    else:
        per = right[0] * (n // step)
        if flip:
            x_specs = [pl.BlockSpec((k, m), lambda j: (0, left[0])) for k in depths]
        else:
            x_specs = [pl.BlockSpec((m, k), lambda j: (rows[0], 0)) for k in depths]
        if kind == "nt":
            w_specs = [pl.BlockSpec((step, k), lambda j: (j, 0)) for k in depths]
        else:
            w_specs = [pl.BlockSpec((k, step), lambda j: (0, per + j)) for k in depths]
        out_spec = pl.BlockSpec((m_out, step), lambda j: (0, j))
    results = pl.pallas_call(
        kernel,
        grid=(size // step,),
        in_specs=x_specs
        + w_specs
        + [pl.BlockSpec((1, step), lambda j: (0, j))] * len(columns)
        + [out_spec] * len(tiles),
        out_specs=[out_spec] * len(outs),
        out_shape=[jax.ShapeDtypeStruct((m_out, n_out), t) for t in outs],
        scratch_shapes=[pltpu.VMEM((m_block, k), BF) for k in depths] if flip else [],
        compiler_params=pltpu.CompilerParams(vmem_limit_bytes=VMEM_LIMIT),
        cost_estimate=FREE,
    )(*xs, *ws, *columns, *tiles)
    return results if len(outs) > 1 else results[0]


def plain(total):
    return (total,)


def attend(qkv, mask, heads):
    rows = qkv.shape[0]
    head_dim = qkv.shape[1] // (3 * heads)
    scaling = head_dim ** (-0.5)
    step = min(256, rows)

    def kernel(qkv_ref, mask_ref, context_ref, total_ref):
        keys = qkv_ref[:, head_dim : 2 * head_dim]
        values = qkv_ref[:, 2 * head_dim :]
        keep = mask_ref[...] > 0
        for at in range(0, rows, step):
            query = qkv_ref[at : at + step, :head_dim]
            scores = jnp.where(keep, mm_t(query, keys) * scaling, -1e30)
            most = jnp.max(scores, axis=1, keepdims=True)
            shares = jnp.exp(scores - most)
            total = jnp.sum(shares, axis=1, keepdims=True)
            probs = (shares * (1.0 / total)).astype(BF)
            context_ref[at : at + step, :] = mm(probs, values).astype(BF)
            log_total = jnp.broadcast_to(most + jnp.log(total), (step, 128))
            total_ref[0, :, at : at + step] = jnp.transpose(log_total)[0:1, :]

    return pl.pallas_call(
        kernel,
        grid=(heads,),
        in_specs=[
            pl.BlockSpec((rows, 3 * head_dim), lambda h: (0, h)),
            pl.BlockSpec((1, rows), lambda h: (0, 0)),
        ],
        out_specs=[
            pl.BlockSpec((rows, head_dim), lambda h: (0, h)),
            pl.BlockSpec((1, 1, rows), lambda h: (h, 0, 0)),
        ],
        out_shape=[
            jax.ShapeDtypeStruct((rows, heads * head_dim), BF),
            jax.ShapeDtypeStruct((heads, 1, rows), F32),
        ],
        compiler_params=pltpu.CompilerParams(vmem_limit_bytes=VMEM_LIMIT),
        cost_estimate=FREE,
    )(qkv, mask)


def attend_backward(qkv, dcontext, log_total, mask, heads, part):
    rows = qkv.shape[0]
    head_dim = qkv.shape[1] // (3 * heads)
    scaling = head_dim ** (-0.5)
    step = min(256, rows)

    def kernel(qkv_ref, dcontext_ref, total_ref, mask_ref, dqkv_ref, sums_ref):
        keys = qkv_ref[:, head_dim : 2 * head_dim]
        values = qkv_ref[:, 2 * head_dim :]
        keep = mask_ref[...] > 0
        dkeys, dvalues, query_sum = 0.0, 0.0, 0.0
        for at in range(0, rows, step):
            query = qkv_ref[at : at + step, :head_dim]
            dctx = dcontext_ref[at : at + step, :]
            scores = mm_t(keys, query) * scaling
            probs = jnp.exp(scores - total_ref[0, :, at : at + step])
            probs = jnp.where(keep, probs, 0.0)
            dprobs = mm_t(values, dctx)
            delta = jnp.sum(dprobs * probs, axis=0, keepdims=True)
            dscores = (probs * (dprobs - delta)).astype(BF)
            dvalues = dvalues + mm(probs.astype(BF), dctx)
            dkeys = dkeys + mm(dscores, query)
            dquery = (t_mm(dscores, keys) * scaling).astype(BF)
            dqkv_ref[at : at + step, :head_dim] = dquery
            query_sum = query_sum + jnp.sum(dquery.astype(F32), axis=0, keepdims=True)
        dvalues = dvalues.astype(BF)
        dqkv_ref[:, head_dim : 2 * head_dim] = (dkeys * scaling).astype(BF)
        dqkv_ref[:, 2 * head_dim :] = dvalues
        value_sum = jnp.sum(dvalues.astype(F32), axis=0, keepdims=True)
        sums_ref[...] = jnp.concatenate([query_sum, query_sum, value_sum], axis=1)

    return pl.pallas_call(
        kernel,
        grid=(heads,),
        in_specs=[
            pl.BlockSpec((rows, 3 * head_dim), lambda h: (0, h)),
            pl.BlockSpec((rows, head_dim), lambda h: (0, part * heads + h)),
            pl.BlockSpec((1, 1, rows), lambda h: (h, 0, 0)),
            pl.BlockSpec((rows, 1), lambda h: (0, 0)),
        ],
        out_specs=[
            pl.BlockSpec((rows, 3 * head_dim), lambda h: (0, h)),
            pl.BlockSpec((1, 3 * head_dim), lambda h: (0, h)),
        ],
        out_shape=[
            jax.ShapeDtypeStruct(qkv.shape, BF),
            jax.ShapeDtypeStruct((1, qkv.shape[1]), F32),
        ],
        compiler_params=pltpu.CompilerParams(vmem_limit_bytes=VMEM_LIMIT),
        cost_estimate=FREE,
    )(qkv, dcontext, log_total, mask)


def place_rows(pieces, places, shape):
    count, (rows, width) = len(pieces), pieces[0].shape

    def kernel(places_ref, *refs):
        for i in range(count):

            @pl.when(pl.program_id(0) == i)
            def _(i=i):
                refs[-1][...] = refs[i][...].astype(F32)

    return pl.pallas_call(
        kernel,
        grid_spec=pltpu.PrefetchScalarGridSpec(
            num_scalar_prefetch=1,
            grid=(count,),
            in_specs=[pl.BlockSpec((rows, width), lambda i, s: (0, 0))] * count,
            out_specs=pl.BlockSpec((rows, width), lambda i, s: (s[i], 0)),
        ),
        out_shape=jax.ShapeDtypeStruct(shape, F32),
        compiler_params=pltpu.CompilerParams(vmem_limit_bytes=VMEM_LIMIT),
        cost_estimate=FREE,
    )(jnp.stack(places).astype(jnp.int32), *pieces)


def place_columns(pieces, places, shape, block, column):
    count, (rows, width) = len(pieces), pieces[0].shape
    step = min(64, rows)

    def kernel(places_ref, *refs):
        for p in range(count):
            for i in range(width // block):
                at = pl.multiple_of(column(i, places_ref[p]) * block, block)
                value = refs[p][:, i * block : (i + 1) * block].astype(F32)
                refs[-1][:, pl.ds(at, block)] = value

    return pl.pallas_call(
        kernel,
        grid_spec=pltpu.PrefetchScalarGridSpec(
            num_scalar_prefetch=1,
            grid=(rows // step,),
            in_specs=[pl.BlockSpec((step, width), lambda i, s: (i, 0))] * count,
            out_specs=pl.BlockSpec((step, shape[1]), lambda i, s: (i, 0)),
        ),
        out_shape=jax.ShapeDtypeStruct(shape, F32),
        compiler_params=pltpu.CompilerParams(vmem_limit_bytes=VMEM_LIMIT),
        cost_estimate=FREE,
    )(jnp.stack(places).astype(jnp.int32), *pieces)


def take_columns(arrays, index, count, block):
    if block % LANES != 0:
        pieces = []
        for i in range(count):
            for w in arrays:
                pieces.append(lax.dynamic_slice_in_dim(w, index[i] * block, block, 1))
        return jnp.concatenate(pieces, axis=1)
    rows, n = arrays[0].shape[0], len(arrays)

    def kernel(index_ref, *refs):
        for i in range(n):
            refs[-1][:, i * block : (i + 1) * block] = refs[i][...]

    return pl.pallas_call(
        kernel,
        grid_spec=pltpu.PrefetchScalarGridSpec(
            num_scalar_prefetch=1,
            grid=(count,),
            in_specs=[pl.BlockSpec((rows, block), lambda i, s: (0, s[i]))] * n,
            out_specs=pl.BlockSpec((rows, n * block), lambda i, s: (0, i)),
        ),
        out_shape=jax.ShapeDtypeStruct((rows, count * n * block), BF),
        compiler_params=pltpu.CompilerParams(vmem_limit_bytes=VMEM_LIMIT),
        cost_estimate=FREE,
    )(jnp.stack(index).astype(jnp.int32), *arrays)


def place_heads_grad(gathered, reps, run, head_dim):
    shard = gathered.shape[1]
    step = min(64, shard)

    def kernel(in_ref, *outs):
        for r in range(reps):
            for j in range(run):
                at = (((r // TEAM) * run + j) * TEAM + r % TEAM) * head_dim
                for i in range(3):
                    start = (3 * j + i) * head_dim
                    value = in_ref[r, :, start : start + head_dim].astype(F32)
                    outs[i][:, at : at + head_dim] = value

    return pl.pallas_call(
        kernel,
        grid=(shard // step,),
        in_specs=[pl.BlockSpec((reps, step, run * 3 * head_dim), lambda i: (0, i, 0))],
        out_specs=[pl.BlockSpec((step, HEADS * head_dim), lambda i: (i, 0))] * 3,
        out_shape=[jax.ShapeDtypeStruct((shard, HEADS * head_dim), F32)] * 3,
        compiler_params=pltpu.CompilerParams(vmem_limit_bytes=VMEM_LIMIT),
        cost_estimate=FREE,
    )(gathered)


def local(
    tokens,
    lengths,
    query_weight,
    key_weight,
    value_weight,
    out_weight,
    query_bias,
    value_bias,
    out_bias,
    first_gain,
    first_shift,
    up_weight,
    up_bias,
    down_weight,
    down_bias,
    second_gain,
    second_shift,
    cotangent,
):
    slots_here, block, width = tokens.shape
    reps, parts = lax.axis_size("rep"), lax.axis_size("fsdp")
    copies = reps // TEAM
    hidden = up_weight.shape[1]
    shard = query_weight.shape[0]
    head_dim = width // HEADS
    team_heads = HEADS // TEAM
    run = team_heads // copies
    rep, z = lax.axis_index("rep"), lax.axis_index("fsdp")
    q, d = rep % TEAM, rep // TEAM
    parity = z % 2
    held = TEAM * slots_here // parts
    rows = slots_here * block
    half = rows // 2
    unit = hidden // parts // reps
    wide = width // copies
    halves = 2 if unit % (2 * LANES) == 0 else 1
    half_unit = unit // halves
    per_shard = HEADS // parts

    def swap(x, mask):
        return lax.ppermute(x, "rep", [(i, i ^ mask) for i in range(reps)])

    def shift(x, by):
        return lax.ppermute(x, "fsdp", [(i, (i - by) % parts) for i in range(parts)])

    def from_next(k):
        return (z + k) % parts

    def routes(turn):
        pairs = []
        for copy in range(copies):
            for member in range(TEAM):
                for place in range(parts):
                    slot = member * slots_here + (place + turn) % 2
                    to_member = ((slot // parts) * parts + place) // 2
                    source = (copy * TEAM + member) * parts + place
                    target = (copy * TEAM + to_member) * parts + slot % parts
                    pairs.append((source, target))
        return pairs

    even, odd = routes(0), routes(1)
    axes = ("rep", "fsdp")
    v = {}

    def order(*names):
        names = list(dict.fromkeys(names))
        v.update(zip(names, tie(*[v[n] for n in names]), strict=True))

    def to_team(x):
        first = lax.ppermute(pick(x, parity), axes, even)
        second = lax.ppermute(pick(x, 1 - parity), axes, odd)
        return first, second

    def from_team(first, second):
        return settle(*leave_team(first, second))

    def leave_team(first, second):
        first = lax.ppermute(first, axes, [(b, a) for a, b in even])
        second = lax.ppermute(second, axes, [(b, a) for a, b in odd])
        return first, second

    def settle(first, second):
        straight = jnp.stack([first, second])
        turned = jnp.stack([second, first])
        return jnp.where(parity == 0, straight, turned)

    vectors = jnp.concatenate(
        [
            query_bias,
            value_bias,
            out_bias,
            first_gain,
            first_shift,
            down_bias,
            second_gain,
            second_shift,
            up_bias,
        ]
    )[None]
    pieces = [vectors] + [shift(vectors, k) for k in range(1, parts)]
    there = [lengths] + [swap(lengths, m) for m in range(1, TEAM)]
    first, second = to_team(tokens)
    first, second, *pieces = tie(first, second, *pieces, *there)
    pieces, there = pieces[:parts], pieces[parts:]
    vectors = jnp.zeros((parts, vectors.shape[1]), BF)
    for k, piece in enumerate(pieces):
        vectors = lax.dynamic_update_slice(vectors, piece, (from_next(k), 0))
    vectors = vectors.astype(F32)
    names = [vectors[:, i * shard : (i + 1) * shard].reshape(width) for i in range(8)]
    bias_query, bias_value, bias_out, gain_one, shift_one, bias_down, gain_two, shift_two = names
    bias_up = vectors[:, 8 * shard :].reshape(parts, reps, unit)
    slot_lengths = jnp.zeros((TEAM, slots_here), jnp.int32)
    for m in range(TEAM):
        slot_lengths = lax.dynamic_update_slice(slot_lengths, there[m][None], (q ^ m, 0))
    slot_lengths = slot_lengths.reshape(-1)

    def live(member):
        place = [
            ((member * 2 + o) % parts) * block + jnp.arange(block) for o in (parity, 1 - parity)
        ]
        length = pick(slot_lengths, ((member * 2) // parts) * parts + z)
        return jnp.concatenate(place) < length

    masks = [live(q ^ m).astype(F32) for m in range(TEAM)]
    valid = masks[0][:, None]
    mask_mine, mask_other = jnp.concatenate(masks[:2]), jnp.concatenate(masks[2:])

    def head_columns(w, e):
        lead = w.shape[:-1]
        at = len(lead)
        split = w.reshape(lead + (copies, run, TEAM, head_dim))
        return pick(pick(split, e, at), q, at + 1)

    def over_z(x):
        return lax.all_gather(x, "fsdp", axis=0, tiled=True)

    def spread(x):
        return [x] + [swap(x, TEAM * m) for m in range(1, copies)]

    heads_here = [(d * run + j) * TEAM + q for j in range(run)]
    qkv_own = [
        take_columns([query_weight, key_weight, value_weight], [h], 1, head_dim)
        for h in heads_here
    ]
    split_out = out_weight.reshape(-1, head_dim, copies, wide)
    split_out = pick(split_out, d, 2)
    if per_shard >= TEAM:
        split_out = split_out.reshape(per_shard // TEAM, TEAM, head_dim, wide)
        out_own = pick(split_out, q, 1)
    else:
        out_own = pick(split_out, q % per_shard, 0)[None]
    up_own = [
        take_columns(
            [up_weight],
            [(t * reps + rep) * halves + h for t in range(parts)],
            parts,
            half_unit,
        )
        for h in range(halves)
    ]
    down_split = pick(down_weight.reshape(reps, halves, half_unit, width), rep)
    down_own = [down_split[h] for h in range(halves)]
    first, second, out_own, *own = tie(first, second, out_own, *qkv_own, *up_own, *down_own)
    qkv_own, up_own, down_own = own[:run], own[run : run + halves], own[run + halves :]
    for j in range(run):
        v[QKV_Z, j] = over_z(qkv_own[j])
    v[OUT_Z] = over_z(out_own)
    for h in range(halves):
        v[UP_Z, h] = over_z(up_own[h])
    for h in range(halves):
        v[DOWN_Z, h] = over_z(down_own[h])
    own_tokens = jnp.concatenate([first, second], axis=0)
    v[FAR, 0], v[FAR, 1] = swap(first, 2), swap(second, 2)
    near = [swap(x, 1) for x in (first, second)]
    order((FAR, 0), (FAR, 1), (QKV_Z, 0))
    for m in range(1, copies):
        v[QKV, 0, m] = swap(v[QKV_Z, 0], TEAM * m)
    far = [v[FAR, 0], v[FAR, 1]]
    far_near = [swap(x, 1) for x in far]

    def own_units(table, m):
        return pick(table, rep ^ (TEAM * m), 1).transpose(1, 0, 2).reshape(1, -1)

    bias_up = bias_up.reshape(parts, reps, halves, half_unit)
    up_biases = [own_units(bias_up, m) for m in range(copies)]
    qkv_bias = []
    for m in range(copies):
        qb, vb = head_columns(bias_query, d ^ m), head_columns(bias_value, d ^ m)
        qkv_bias.append(jnp.stack([qb, jnp.zeros_like(qb), vb], axis=1).reshape(1, -1))
    span = run * head_dim

    tokens_mine = jnp.concatenate([first, second] + near, axis=0)
    tokens_other = jnp.concatenate(far + far_near, axis=0)
    v[OTHER] = tokens_other
    order(OTHER, *[(QKV_Z, j) for j in range(run)])
    tokens_other = v[OTHER]
    for j in range(1, run):
        for m in range(1, copies):
            v[QKV, j, m] = swap(v[QKV_Z, j], TEAM * m)
    qkv_weight = {0: jnp.concatenate([v[QKV_Z, j] for j in range(run)], axis=1)}

    if held == 2:
        slots = (OTHER, MINE)
        v[MINE] = tokens_mine
        slot_masks = {OTHER: mask_other, MINE: mask_mine}
    else:
        slots = (BOTH,)
        v[BOTH] = jnp.concatenate([tokens_mine, tokens_other], axis=0)
        slot_masks = {BOTH: jnp.concatenate([mask_mine, mask_other])}
    log_totals = {}

    def project_step(name, m):
        v[QKV, name, m] = dot(
            "nn", [(v[name], qkv_weight[m])], lambda t, b: (t + b,), [BF], columns=[qkv_bias[m]]
        )

    def attend_only(name, m):
        qkv = v[QKV, name, m]
        context, log_totals[name, m] = attend(qkv, slot_masks[name][None], run)
        v[CONTEXT, name, m] = context

    def attend_step(name, m):
        project_step(name, m)
        attend_only(name, m)

    def out_step(name, first):
        at = (0, 1) if held == 2 else (int(name == OTHER), 2)
        pairs = [
            (v[CONTEXT, name if held == 2 else BOTH, m], out_full[m * span : (m + 1) * span])
            for m in range(copies)
        ]
        return dot("nn", pairs, plain, [first, BF], rows=at, split=ROWS)

    def add(x, received):
        total = x.astype(F32)
        for y in received:
            total = total + y.astype(F32)
        return total.astype(BF)

    def next_hop():
        return add(v[KEPT], [v[AWAY]])

    attend_step(slots[0], 0)
    if held == 2:
        order(MINE, (CONTEXT, OTHER, 0))
        attend_step(MINE, 0)
    order(
        (CONTEXT, slots[-1], 0),
        OUT_Z,
        *[(QKV, j, m) for j in range(run) for m in range(1, copies)],
    )
    out_z = v[OUT_Z]
    if per_shard < TEAM:
        fill = TEAM // per_shard
        out_z = out_z.reshape(HEADS // TEAM, fill, head_dim, wide)
        out_z = pick(out_z, q // per_shard, 1)
    out_z = out_z.reshape(team_heads * head_dim, wide)
    out_swapped = [out_z] + [swap(out_z, TEAM * m) for m in range(1, copies)]
    for m in range(1, copies):
        qkv_weight[m] = jnp.concatenate([v[QKV, j, m] for j in range(run)], axis=1)
        attend_step(slots[0], m)
        if m == 1:
            v[OUT_SWAPPED] = jnp.stack(out_swapped)
            order(OUT_SWAPPED, (CONTEXT, slots[0], m))
    out_columns = v[OUT_SWAPPED]
    out_full = jnp.concatenate([pick(out_columns, d ^ e) for e in range(copies)], axis=1)
    out_rows = [
        lax.dynamic_slice_in_dim(out_full, (d ^ m) * span, span, 0) for m in range(copies)
    ]
    out_full = jnp.concatenate(out_rows, axis=0)
    if held == 2:
        v[KEPT], v[AWAY] = out_step(OTHER, BF)
        order(KEPT, AWAY, MINE)
        v[AWAY] = swap(v[AWAY], 1)
        project_step(MINE, 1)
        order(AWAY, (QKV, MINE, 1))
        v[SEND] = next_hop()
        order(SEND, (QKV, MINE, 1), (UP_Z, 0))
        v[BACK] = swap(v[SEND], 2)
        for m in range(1, copies):
            if m > 1:
                project_step(MINE, m)
            attend_only(MINE, m)
        v[OWN], v[THEIRS] = out_step(MINE, F32)
    else:
        order((CONTEXT, BOTH, 0), (UP_Z, 0))
        v[KEPT], v[AWAY] = out_step(OTHER, BF)
        v[AWAY] = swap(v[AWAY], 1)
        v[BACK] = swap(next_hop(), 2)
        v[OWN], v[THEIRS] = out_step(MINE, F32)
    for m in range(1, copies):
        v[UP, 0, m] = swap(v[UP_Z, 0], TEAM * m)
    order(
        OWN,
        THEIRS,
        BACK,
        *[(UP_Z, h) for h in range(1, halves)],
        *[(UP, 0, m) for m in range(1, copies)],
    )
    for h in range(1, halves):
        for m in range(1, copies):
            v[UP, h, m] = swap(v[UP_Z, h], TEAM * m)
    v[ATTENDED] = v[OWN] + swap(v[THEIRS], 1).astype(F32)
    summed1 = own_tokens.astype(F32) + v[ATTENDED] + v[BACK].astype(F32) + bias_out
    normal1, scale1 = normalise(summed1)
    normed1 = normal1 * gain_one + shift_one

    def team_chunk(name):
        return jnp.concatenate([v[name], swap(v[name], 1)], axis=0)

    v[NEAR] = normed1.astype(BF)
    v[FAR] = swap(v[NEAR], 2)
    v[HIDDEN, 0] = team_chunk(NEAR)
    up_parts = {0: jnp.concatenate([v[UP_Z, h] for h in range(halves)], axis=1)}

    def up_step(i, m):
        v[VALUE, i, m], v[SLOPE, i, m] = dot(
            "nn",
            [(v[HIDDEN, i], up_parts[m])],
            lambda t, b: gelu_parts(t + b),
            [BF, BF],
            columns=[up_biases[m]],
        )

    up_step(0, 0)
    order(
        (VALUE, 0, 0),
        FAR,
        (DOWN_Z, 0),
        *[(UP, h, m) for h in range(1, halves) for m in range(1, copies)],
    )
    for m in range(1, copies):
        v[DOWN, 0, m] = swap(v[DOWN_Z, 0], TEAM * m)
    v[HIDDEN, 1] = team_chunk(FAR)
    up_step(1, 0)
    for m in range(1, copies):
        up_parts[m] = jnp.concatenate([v[UP, h, m] for h in range(halves)], axis=1)
        for i in (1, 0):
            up_step(i, m)
    order(
        *[(VALUE, i, m) for i in range(2) for m in range(copies)],
        *[(DOWN_Z, h) for h in range(1, halves)],
        *[(DOWN, 0, n) for n in range(1, copies)],
    )
    for h in range(1, halves):
        for n in range(1, copies):
            v[DOWN, h, n] = swap(v[DOWN_Z, h], TEAM * n)
    down_parts = {0: jnp.concatenate([v[DOWN_Z, h] for h in range(halves)], axis=0)}
    for m in range(1, copies):
        down_parts[m] = jnp.concatenate([v[DOWN, h, m] for h in range(halves)], axis=0)

    def down_step(i, kinds, **which):
        pairs = [(v[VALUE, i, m], down_parts[m]) for m in range(copies)]
        return dot("nn", pairs, plain, kinds, **which)

    v[KEPT], v[AWAY] = down_step(1, [BF, BF], split=ROWS)
    order(KEPT, AWAY, (VALUE, 0, 0))
    v[AWAY] = swap(v[AWAY], 1)
    v[THEIRS] = down_step(0, [BF], rows=(1, 2))
    order(KEPT, AWAY, THEIRS, (VALUE, 0, 0))
    v[SEND] = next_hop()
    order(SEND, THEIRS, (VALUE, 0, 0))
    v[BACK] = swap(v[SEND], 2)
    v[THEIRS] = swap(v[THEIRS], 1)
    v[OWN] = down_step(0, [F32], rows=(0, 2))
    order(OWN, THEIRS, BACK)

    def team_sum():
        return v[OWN] + v[THEIRS].astype(F32) + v[BACK].astype(F32)

    summed2 = normed1 + team_sum() + bias_down
    normal2, scale2 = normalise(summed2)
    result = (valid * (normal2 * gain_two + shift_two)).astype(BF)

    v[COTANGENT] = cotangent
    order(COTANGENT, (VALUE, 0, 0))
    v[COT, 0], v[COT, 1] = to_team(v[COTANGENT])
    v[NORMAL2] = normal2
    order(NORMAL2, (COT, 0), (COT, 1))
    normal2 = v[NORMAL2]
    grad_out = jnp.concatenate([v[COT, 0], v[COT, 1]], axis=0).astype(F32) * valid
    dsum2 = norm_backward(grad_out, gain_two, normal2, scale2)
    gain_two_grad = jnp.sum(grad_out * normal2, axis=0)
    shift_two_grad = jnp.sum(grad_out, axis=0)
    v[NEAR] = dsum2.astype(BF)
    down_bias_grad = jnp.sum(v[NEAR].astype(F32), axis=0)
    v[RESULT] = result
    order(RESULT, NEAR)
    v[LAYER, 0], v[LAYER, 1] = leave_team(v[RESULT][:block], v[RESULT][block:])

    def over_copies(shares):
        total = shares[0].astype(F32)
        for m in range(1, copies):
            total = total + swap(shares[m], TEAM * m).astype(F32)
        return total.astype(BF)

    def to_owner(x):
        return lax.psum_scatter(x, "fsdp", scatter_dimension=0, tiled=True)

    def from_all(x):
        return lax.all_gather(x, "rep", axis=0, tiled=True)

    def in_order(pieces):
        stacked = jnp.stack([pieces[m] for m in range(reps)])
        return jnp.stack([pick(stacked, rep ^ r) for r in range(reps)])

    sub = parts * half_unit

    def backward_step(i, first):
        for m in range(copies):
            v[DBEFORE, i, m] = dot(
                "nt",
                [(v[DDOWN, i], down_parts[m])],
                lambda t, s: (t * s.astype(F32),),
                [BF],
                tiles=[v[SLOPE, i, m]],
            )
        pairs = [(v[DBEFORE, i, m], up_parts[m]) for m in range(copies)]
        return dot("nt", pairs, plain, [first, BF], split=ROWS)

    def down_grad_step(m, *those):
        pairs = [(v[VALUE, i, m], v[DDOWN, i]) for i in range(2)]
        if len(those) == 2:
            both = dot("tn", pairs, plain, [BF, BF], split=ROWS)
        else:
            both = [dot("tn", pairs, plain, [BF], left=(h, halves)) for h in those]
        for h, share in zip(those, both, strict=True):
            v[DOWN, SHARE, h, m] = share

    def up_grad_step(m, *those):
        pairs = [(v[HIDDEN, i], v[DBEFORE, i, m]) for i in range(2)]
        if len(those) == 2:
            both = dot("tn", pairs, plain, [BF, BF], split=COLUMNS)
        else:
            both = [dot("tn", pairs, plain, [BF], right=(h, halves)) for h in those]
        for h, share in zip(those, both, strict=True):
            v[UP, SHARE, h, m] = share

    def swap_share(kind, h):
        for m in range(1, copies):
            v[kind, RECEIVED, h, m] = swap(v[kind, SHARE, h, m], TEAM * m)

    def shares(kind, *those):
        return [(kind, SHARE, h, m) for h in those for m in range(1, copies)]

    def received(kind, *those):
        return [(kind, RECEIVED, h, m) for h in those for m in range(1, copies)]

    def reduce_step(kind, h):
        total = add(v[kind, SHARE, h, 0], [v[n] for n in received(kind, h)])
        v[kind, PART, h] = to_owner(total)

    more = range(1, copies)
    late = range(1, halves)
    v[FAR] = swap(v[NEAR], 2)
    v[DDOWN, 0] = team_chunk(NEAR)
    v[OWN], v[THEIRS] = backward_step(0, F32)
    order(THEIRS, FAR, (VALUE, 0, 0))
    v[THEIRS] = swap(v[THEIRS], 1)
    v[DDOWN, 1] = team_chunk(FAR)
    for m in more:
        down_grad_step(m, *range(halves))
    order(*shares(DOWN, *range(halves)), (DDOWN, 1))
    for h in range(halves):
        swap_share(DOWN, h)
    v[KEPT], v[AWAY] = backward_step(1, BF)
    order(KEPT, AWAY, (DDOWN, 0))
    v[AWAY] = swap(v[AWAY], 1)
    down_grad_step(0, 0)
    order(KEPT, AWAY, (DOWN, SHARE, 0, 0), (DDOWN, 0))
    v[SEND] = next_hop()
    order(SEND, (DOWN, SHARE, 0, 0), (DDOWN, 0))
    v[BACK] = swap(v[SEND], 2)
    for h in late:
        down_grad_step(0, h)
    order(*[(DOWN, SHARE, h, 0) for h in range(halves)], *received(DOWN, 0))
    reduce_step(DOWN, 0)
    order(OWN, BACK, THEIRS, *[(DOWN, SHARE, h, 0) for h in late])
    dnormed1 = dsum2 + team_sum()
    dsum1 = norm_backward(dnormed1, gain_one, normal1, scale1)
    gain_one_grad = jnp.sum(dnormed1 * normal1, axis=0)
    shift_one_grad = jnp.sum(dnormed1, axis=0)
    v[DATTN] = dsum1.astype(BF)
    out_bias_grad = jnp.sum(v[DATTN].astype(F32), axis=0)

    order((HIDDEN, 0), DATTN)
    v[DATTN_NEAR] = swap(v[DATTN], 1)
    v[DATTN_FAR] = swap(v[DATTN], 2)
    for m in more:
        up_grad_step(m, *range(halves))
    order(
        *shares(UP, *range(halves)),
        DATTN_NEAR,
        (HIDDEN, 0),
        *received(DOWN, *late),
        *[(DOWN, SHARE, h, 0) for h in late],
    )
    for h in range(halves):
        swap_share(UP, h)
    for h in late:
        reduce_step(DOWN, h)

    v[DATTN_MINE] = jnp.concatenate([v[DATTN], v[DATTN_NEAR]], axis=0)
    qkv_sums = {}

    def back_step(name, dcontext, m):
        v[DQKV, name, m], qkv_sums[name, m] = attend_backward(
            v[QKV, name, m], dcontext, log_totals[name, m], slot_masks[name][:, None], run, m
        )

    def context_grad(x):
        return dot("nt", [(x, out_full)], plain, [BF])

    def far_rows():
        return jnp.concatenate([v[DATTN_FAR], swap(v[DATTN_FAR], 1)], axis=0)

    def out_grad_step():
        if held == 2:
            share = jnp.concatenate(
                [
                    dot(
                        "tn",
                        [
                            (v[CONTEXT, MINE, m], v[DATTN_MINE]),
                            (v[CONTEXT, OTHER, m], dattn_other),
                        ],
                        plain,
                        [BF],
                    )
                    for m in range(copies)
                ],
                axis=0,
            )
        else:
            pairs = [[(v[CONTEXT, BOTH, m], dattn_both)] for m in range(copies)]
            share = jnp.concatenate([dot("tn", p, plain, [BF]) for p in pairs], axis=0)
        for m in range(copies):
            rows_of = [
                lax.dynamic_slice(share, ((d ^ e) * span, (d ^ m) * wide), (span, wide))
                for e in range(copies)
            ]
            v[OUT, SHARE, 0, m] = jnp.concatenate(rows_of, axis=0)

    def out_reduce_step():
        total = add(v[OUT, SHARE, 0, 0], [v[n] for n in received(OUT, 0)])
        if per_shard < TEAM:
            fill = TEAM // per_shard
            total = total.reshape(HEADS // TEAM, 1, head_dim, -1)
            chosen = (jnp.arange(fill) == q // per_shard)[None, :, None, None]
            total = jnp.where(chosen, total, jnp.zeros((), BF))
            total = total.reshape(parts * head_dim, -1)
        v[OUT, PART, 0] = to_owner(total)

    def to_more(kind, mask):
        for m in [m for m in range(reps) if (kind, WHOLE, m) in v]:
            v[kind, WHOLE, m ^ mask] = swap(v[kind, WHOLE, m], mask)

    def all_of(kind):
        return [(kind, WHOLE, m) for m in range(reps) if (kind, WHOLE, m) in v]

    near_far = [2] + [TEAM << i for i in range(copies.bit_length() - 1)]

    def vector_table():
        def place_heads(i):
            full = jnp.zeros((copies, run, TEAM, head_dim), F32)
            for m in range(copies):
                share = sum(qkv_sums[name, m] for name in names)
                share = share.reshape(run, 3, head_dim)[:, i].reshape(1, run, 1, head_dim)
                full = lax.dynamic_update_slice(full, share, (d ^ m, 0, q, 0))
            return full.reshape(width)

        up_sums = jnp.zeros((parts, reps, halves, half_unit), F32)
        for m in range(copies):
            share = sum(jnp.sum(v[DBEFORE, i, m].astype(F32), axis=0) for i in range(2))
            share = share.reshape(halves, parts, half_unit).transpose(1, 0, 2)[:, None]
            up_sums = lax.dynamic_update_slice(up_sums, share, (0, rep ^ (TEAM * m), 0, 0))
        vector_sums = [
            place_heads(0),
            place_heads(2),
            out_bias_grad,
            gain_one_grad,
            shift_one_grad,
            down_bias_grad,
            gain_two_grad,
            shift_two_grad,
        ]
        return jnp.concatenate(
            [s.reshape(parts, shard) for s in vector_sums] + [up_sums.reshape(parts, -1)], axis=1
        )

    def vector_start():
        vector_sums = vector_table()
        v[VECTOR, 0] = pick(vector_sums, z)
        for k in range(1, parts):
            v[VECTOR, k] = shift(pick(vector_sums, (z - k) % parts), k)

    def vector_names():
        return [(VECTOR, k) for k in range(parts)]

    def vector_step(mask):
        if mask == 1:
            v[VECTOR, 0] = sum(v[n] for n in vector_names())
        v[VECTOR, 0] = v[VECTOR, 0] + swap(v[VECTOR, 0], mask)

    backwards = list(reversed(range(copies)))
    if held == 2:
        names = (MINE, OTHER)
        dcontext = context_grad(v[DATTN_MINE])
        for m in backwards:
            back_step(MINE, dcontext, m)
        order(
            DATTN_FAR,
            *[(DQKV, MINE, m) for m in range(copies)],
            *received(UP, 0),
        )
        v[DATTN_OTHER] = far_rows()
        dattn_other = v[DATTN_OTHER]
        out_grad_step()
        order(*[(OUT, SHARE, 0, m) for m in range(copies)], DATTN_OTHER, (HIDDEN, 0))
        swap_share(OUT, 0)
        up_grad_step(0, 0)
        order(DATTN_OTHER, (UP, SHARE, 0, 0))
        reduce_step(UP, 0)
        dattn_other = v[DATTN_OTHER]
        dcontext = context_grad(dattn_other)
        for m in backwards:
            back_step(OTHER, dcontext, m)
    else:
        names = (BOTH,)
        dattn_other = far_rows()
        dattn_both = jnp.concatenate([v[DATTN_MINE], dattn_other], axis=0)
        dcontext = context_grad(dattn_both)
        for m in backwards:
            back_step(BOTH, dcontext, m)
        up_grad_step(0, 0)
        reduce_step(UP, 0)
        out_grad_step()
        swap_share(OUT, 0)
        for m in range(copies):
            v[DQKV, MINE, m] = v[DQKV, BOTH, m][: 2 * rows]
            v[DQKV, OTHER, m] = v[DQKV, BOTH, m][2 * rows :]
    order(
        *[(DQKV, OTHER, m) for m in range(copies)],
        *[(DOWN, PART, h) for h in range(halves)],
        *received(OUT, 0),
        (OUT, SHARE, 0, 0),
        *received(UP, *late),
        (LAYER, 0),
        (LAYER, 1),
    )
    out_reduce_step()
    vector_start()
    v[DOWN, WHOLE, 0] = jnp.concatenate([v[DOWN, PART, h] for h in range(halves)], axis=0)
    to_more(DOWN, near_far[0])

    def qkv_grad_step(m):
        pairs = [(tokens_mine, v[DQKV, MINE, m]), (tokens_other, v[DQKV, OTHER, m])]
        v[QKV, SHARE, 0, m] = dot("tn", pairs, plain, [BF])

    def dtokens_partial(name, first):
        pairs = [(v[DQKV, name, m], qkv_weight[m]) for m in range(copies)]
        return dot("nt", pairs, plain, [first, BF], split=ROWS)

    for m in more:
        qkv_grad_step(m)
    order(
        *shares(QKV, 0),
        *[(DQKV, name, m) for name in (MINE, OTHER) for m in range(copies)],
        (HIDDEN, 0),
        *all_of(DOWN),
    )
    swap_share(QKV, 0)
    v[KEPT], v[AWAY] = dtokens_partial(OTHER, BF)
    order(
        KEPT,
        AWAY,
        *[(DQKV, MINE, m) for m in range(copies)],
        *vector_names(),
        (HIDDEN, 0),
    )
    v[AWAY] = swap(v[AWAY], 1)
    vector_step(1)
    order(KEPT, AWAY, *[(DQKV, MINE, m) for m in range(copies)], (HIDDEN, 0))
    v[SEND] = next_hop()
    v[BACK] = swap(v[SEND], 2)
    for h in late:
        up_grad_step(0, h)
        reduce_step(UP, h)
    qkv_grad_step(0)
    v[OWN], v[THEIRS] = dtokens_partial(MINE, F32)
    order(
        THEIRS,
        BACK,
        (QKV, SHARE, 0, 0),
        *received(QKV, 0),
        *all_of(DOWN),
        *[(UP, PART, h) for h in range(halves)],
        (VECTOR, 0),
        (OUT, PART, 0),
    )
    reduce_step(QKV, 0)
    v[THEIRS] = swap(v[THEIRS], 1)
    v[UP, WHOLE, 0] = jnp.concatenate([v[UP, PART, h] for h in range(halves)], axis=1)
    far_near = near_far[1:] + near_far[:1]
    to_more(UP, far_near[0])
    v[OUT, WHOLE, 0] = v[OUT, PART, 0]
    to_more(OUT, far_near[0])
    order(OWN, THEIRS, BACK, *all_of(UP), *all_of(DOWN), *all_of(OUT))
    for i, mask in enumerate(far_near[1:]):
        to_more(UP, mask)
        to_more(DOWN, near_far[1 + i])
    v[OWN] = (dsum1 + team_sum()).astype(BF)
    order((QKV, PART, 0), OWN, (VECTOR, 0), *all_of(UP), *all_of(DOWN))
    qkv_part = lax.all_gather(v[QKV, PART, 0], "rep", axis=0, tiled=False)
    v[GRAD, 0], v[GRAD, 1] = leave_team(v[OWN][:block], v[OWN][block:])
    to_more(UP, 1)
    to_more(DOWN, 1)
    for mask in far_near[1:]:
        to_more(OUT, mask)
    vector_step(2)
    layer_out = settle(v[LAYER, 0], v[LAYER, 1])
    order(*all_of(UP), *all_of(DOWN))
    places = [rep ^ m for m in range(reps)]
    aligned = half_unit % LANES == 0 and head_dim % LANES == 0
    if aligned:
        v[DOWN_GRAD] = place_rows(
            [v[DOWN, WHOLE, m] for m in range(reps)], places, (hidden // parts, width)
        )
        v[UP_GRAD] = place_columns(
            [v[UP, WHOLE, m] for m in range(reps)],
            places,
            (shard, hidden),
            half_unit,
            lambda i, r: ((i % parts) * reps + r) * halves + i // parts,
        )
        order(DOWN_GRAD, UP_GRAD, *all_of(OUT), (VECTOR, 0))
    to_more(OUT, 1)
    for mask in near_far[1:]:
        vector_step(mask)
    tokens_grad = settle(v[GRAD, 0], v[GRAD, 1]).astype(F32)
    out_grad = in_order({m: v[OUT, WHOLE, m] for m in range(reps)})

    if per_shard >= TEAM:
        out_grad = out_grad.reshape(copies, TEAM, per_shard // TEAM, head_dim, wide)
        out_grad = out_grad.transpose(2, 1, 3, 0, 4)
    else:
        fill = TEAM // per_shard
        out_grad = out_grad.reshape(copies, fill, per_shard, head_dim, wide)
        out_grad = pick(out_grad, z % fill, 1).transpose(1, 2, 0, 3)
    out_grad = out_grad.reshape(-1, width).astype(F32)

    if aligned:
        down_grad, up_grad = v[DOWN_GRAD], v[UP_GRAD]
        qkv_grads = place_heads_grad(qkv_part, reps, run, head_dim)
    else:
        def in_order_of(kind):
            return in_order({m: v[kind, WHOLE, m] for m in range(reps)})

        down_grad = in_order_of(DOWN).reshape(-1, width).astype(F32)
        up_grad = in_order_of(UP).reshape(reps, shard, halves, parts, half_unit)
        up_grad = up_grad.transpose(1, 3, 0, 2, 4).reshape(shard, hidden).astype(F32)
        qkv_final = qkv_part.reshape(copies, TEAM, shard, run, 3, head_dim)
        qkv_grads = [
            qkv_final[:, :, :, :, i].transpose(2, 0, 3, 1, 4).reshape(shard, width).astype(F32)
            for i in range(3)
        ]

    total = v[VECTOR, 0]
    small = [total[i * shard : (i + 1) * shard] for i in range(8)]
    up_bias_grad = total[8 * shard :]
    return (
        layer_out,
        tokens_grad,
        qkv_grads[0],
        qkv_grads[1],
        qkv_grads[2],
        out_grad,
        small[0],
        small[1],
        small[2],
        small[3],
        small[4],
        up_grad,
        up_bias_grad,
        down_grad,
        small[5],
        small[6],
        small[7],
    )


def solution(mesh):
    three, two, one = P("rep", "fsdp", None), P("fsdp", None), P("fsdp")
    placed = (three, P("rep"), two, two, two, two, one, one, one, one, one)
    placed += (two, one, two, one, one, one, three)
    given = (three, three, two, two, two, two, one, one, one, one, one)
    given += (two, one, two, one, one, one)
    return jax.shard_map(local, mesh=mesh, in_specs=placed, out_specs=given, check_vma=False)
```

```python
import jax
import jax.numpy as jnp
from jax import lax
from jax.experimental import pallas as pl
from jax.experimental.pallas import tpu as pltpu
from jax.sharding import PartitionSpec as P

HEADS = 16
TEAM = 4
LANES = 128
EPSILON = 1e-06
BF = jnp.bfloat16
F32 = jnp.float32
VMEM_LIMIT = 48 * 1024 * 1024
FREE = pl.CostEstimate(flops=0, bytes_accessed=0, transcendentals=0)

(
    ROWS,
    COLUMNS,
    QKV_Z,
    OUT_Z,
    UP_Z,
    DOWN_Z,
    FAR,
    QKV,
    OTHER,
    MINE,
    BOTH,
    CONTEXT,
    KEPT,
    AWAY,
    OUT_SWAPPED,
    SEND,
    BACK,
    OWN,
    THEIRS,
    UP,
    ATTENDED,
    NEAR,
    HIDDEN,
    VALUE,
    SLOPE,
    DOWN,
    COTANGENT,
    COT,
    NORMAL2,
    RESULT,
    LAYER,
    DBEFORE,
    DDOWN,
    SHARE,
    RECEIVED,
    PART,
    DATTN,
    DATTN_NEAR,
    DATTN_FAR,
    DATTN_MINE,
    DQKV,
    OUT,
    WHOLE,
    VECTOR,
    DATTN_OTHER,
    GRAD,
    DOWN_GRAD,
    UP_GRAD,
) = range(48)


def mm(left, right):
    return jnp.dot(left, right, preferred_element_type=F32)


def mm_t(left, right):
    return lax.dot_general(left, right, (((1,), (1,)), ((), ())), preferred_element_type=F32)


def t_mm(left, right):
    return lax.dot_general(left, right, (((0,), (0,)), ((), ())), preferred_element_type=F32)


def pick(array, index, axis=0):
    return lax.dynamic_index_in_dim(array, index, axis, keepdims=False)


def tie(*arrays):
    return lax.optimization_barrier(arrays)


def normalise(summed):
    center = summed - jnp.mean(summed, axis=-1, keepdims=True)
    spread = jnp.mean(center * center, axis=-1, keepdims=True)
    scale = lax.rsqrt(spread + EPSILON)
    return center * scale, scale


def norm_backward(grad, gain, normal, scale):
    dn = grad * gain
    first = jnp.mean(dn, axis=-1, keepdims=True)
    second = jnp.mean(dn * normal, axis=-1, keepdims=True)
    return scale * (dn - first - normal * second)


def gelu_parts(u):
    inner = 0.7978845608 * (u + 0.044715 * u * u * u)
    t = jnp.tanh(inner)
    half = 0.5 * (1.0 + t)
    slope = half + 0.5 * u * (1.0 - t * t) * (0.7978845608 + 0.7978845608 * 0.134145 * u * u)
    return u * half, slope


def dot(
    kind, pairs, finish, outs, columns=(), tiles=(), left=(0, 1), right=(0, 1), rows=(0, 1), split=None
):
    count = len(pairs)
    xs, ws = [x for x, _ in pairs], [w for _, w in pairs]
    flip = kind == "tn"
    m = xs[0].shape[1] // left[1] if flip else xs[0].shape[0] // rows[1]
    n = ws[0].shape[0] if kind == "nt" else ws[0].shape[1] // right[1]
    depths = [x.shape[0] if flip else x.shape[1] for x in xs]
    by_rows = flip and m > n
    size = m if by_rows else n
    step = next((s for s in (512, 384, 256) if size % s == 0), size)
    m_block, n_block = (step, n) if by_rows else (m, step)
    strip = next((s for s in (512, 256, 128, 64) if (m_block // 2) % s == 0), m_block // 2)
    inputs = 2 * count + len(columns) + len(tiles)

    def kernel(*refs):
        x_refs, w_refs = refs[:count], refs[count : 2 * count]
        column_refs = refs[2 * count : 2 * count + len(columns)]
        tile_refs = refs[2 * count + len(columns) : inputs]
        out_refs = refs[inputs : inputs + len(outs)]
        if flip:
            flipped = refs[inputs + len(outs) :]

            def turn():
                for a, b in zip(flipped, x_refs, strict=True):
                    a[...] = b[...].T

            if by_rows:
                turn()
            else:
                pl.when(pl.program_id(0) == 0)(turn)
            x_refs = flipped
        for at in range(0, m_block, strip):
            some = slice(at, at + strip)
            total = 0.0
            for x, w in zip(x_refs, w_refs, strict=True):
                product = mm_t(x[some, :], w[...]) if kind == "nt" else mm(x[some, :], w[...])
                total = total + product
            extra = [c[...] for c in column_refs] + [t[some, :] for t in tile_refs]
            values = finish(total, *extra)
            if split == ROWS:
                to = at * 2 // m_block
                at = at - to * (m_block // 2)
                out_refs[to][at : at + strip, :] = values[0].astype(out_refs[to].dtype)
                continue
            if split == COLUMNS:
                values = values[0][:, : n_block // 2], values[0][:, n_block // 2 :]
            for ref, value in zip(out_refs, values, strict=True):
                ref[some, :] = value.astype(ref.dtype)

    m_out, n_out = m // 2 if split == ROWS else m, n // 2 if split == COLUMNS else n
    if by_rows:
        per = left[0] * (m // step)
        x_specs = [pl.BlockSpec((k, step), lambda j: (0, per + j)) for k in depths]
        w_specs = [pl.BlockSpec((k, n), lambda j: (0, right[0])) for k in depths]
        out_spec = pl.BlockSpec((step, n_out), lambda j: (j, 0))
    else:
        per = right[0] * (n // step)
        if flip:
            x_specs = [pl.BlockSpec((k, m), lambda j: (0, left[0])) for k in depths]
        else:
            x_specs = [pl.BlockSpec((m, k), lambda j: (rows[0], 0)) for k in depths]
        if kind == "nt":
            w_specs = [pl.BlockSpec((step, k), lambda j: (j, 0)) for k in depths]
        else:
            w_specs = [pl.BlockSpec((k, step), lambda j: (0, per + j)) for k in depths]
        out_spec = pl.BlockSpec((m_out, step), lambda j: (0, j))
    results = pl.pallas_call(
        kernel,
        grid=(size // step,),
        in_specs=x_specs
        + w_specs
        + [pl.BlockSpec((1, step), lambda j: (0, j))] * len(columns)
        + [out_spec] * len(tiles),
        out_specs=[out_spec] * len(outs),
        out_shape=[jax.ShapeDtypeStruct((m_out, n_out), t) for t in outs],
        scratch_shapes=[pltpu.VMEM((m_block, k), BF) for k in depths] if flip else [],
        compiler_params=pltpu.CompilerParams(vmem_limit_bytes=VMEM_LIMIT),
        cost_estimate=FREE,
    )(*xs, *ws, *columns, *tiles)
    return results if len(outs) > 1 else results[0]


def plain(total):
    return (total,)


def attend(qkv, mask, heads):
    rows = qkv.shape[0]
    head_dim = qkv.shape[1] // (3 * heads)
    scaling = head_dim ** (-0.5)
    step = min(256, rows)

    def kernel(qkv_ref, mask_ref, context_ref, total_ref):
        keys = qkv_ref[:, head_dim : 2 * head_dim]
        values = qkv_ref[:, 2 * head_dim :]
        keep = mask_ref[...] > 0
        for at in range(0, rows, step):
            query = qkv_ref[at : at + step, :head_dim]
            scores = jnp.where(keep, mm_t(query, keys) * scaling, -1e30)
            most = jnp.max(scores, axis=1, keepdims=True)
            shares = jnp.exp(scores - most)
            total = jnp.sum(shares, axis=1, keepdims=True)
            probs = (shares * (1.0 / total)).astype(BF)
            context_ref[at : at + step, :] = mm(probs, values).astype(BF)
            log_total = jnp.broadcast_to(most + jnp.log(total), (step, 128))
            total_ref[0, :, at : at + step] = jnp.transpose(log_total)[0:1, :]

    return pl.pallas_call(
        kernel,
        grid=(heads,),
        in_specs=[
            pl.BlockSpec((rows, 3 * head_dim), lambda h: (0, h)),
            pl.BlockSpec((1, rows), lambda h: (0, 0)),
        ],
        out_specs=[
            pl.BlockSpec((rows, head_dim), lambda h: (0, h)),
            pl.BlockSpec((1, 1, rows), lambda h: (h, 0, 0)),
        ],
        out_shape=[
            jax.ShapeDtypeStruct((rows, heads * head_dim), BF),
            jax.ShapeDtypeStruct((heads, 1, rows), F32),
        ],
        compiler_params=pltpu.CompilerParams(vmem_limit_bytes=VMEM_LIMIT),
        cost_estimate=FREE,
    )(qkv, mask)


def attend_backward(qkv, dcontext, log_total, mask, heads, part):
    rows = qkv.shape[0]
    head_dim = qkv.shape[1] // (3 * heads)
    scaling = head_dim ** (-0.5)
    step = min(256, rows)

    def kernel(qkv_ref, dcontext_ref, total_ref, mask_ref, dqkv_ref, sums_ref):
        keys = qkv_ref[:, head_dim : 2 * head_dim]
        values = qkv_ref[:, 2 * head_dim :]
        keep = mask_ref[...] > 0
        dkeys, dvalues, query_sum = 0.0, 0.0, 0.0
        for at in range(0, rows, step):
            query = qkv_ref[at : at + step, :head_dim]
            dctx = dcontext_ref[at : at + step, :]
            scores = mm_t(keys, query) * scaling
            probs = jnp.exp(scores - total_ref[0, :, at : at + step])
            probs = jnp.where(keep, probs, 0.0)
            dprobs = mm_t(values, dctx)
            delta = jnp.sum(dprobs * probs, axis=0, keepdims=True)
            dscores = (probs * (dprobs - delta)).astype(BF)
            dvalues = dvalues + mm(probs.astype(BF), dctx)
            dkeys = dkeys + mm(dscores, query)
            dquery = (t_mm(dscores, keys) * scaling).astype(BF)
            dqkv_ref[at : at + step, :head_dim] = dquery
            query_sum = query_sum + jnp.sum(dquery.astype(F32), axis=0, keepdims=True)
        dvalues = dvalues.astype(BF)
        dqkv_ref[:, head_dim : 2 * head_dim] = (dkeys * scaling).astype(BF)
        dqkv_ref[:, 2 * head_dim :] = dvalues
        value_sum = jnp.sum(dvalues.astype(F32), axis=0, keepdims=True)
        sums_ref[...] = jnp.concatenate([query_sum, query_sum, value_sum], axis=1)

    return pl.pallas_call(
        kernel,
        grid=(heads,),
        in_specs=[
            pl.BlockSpec((rows, 3 * head_dim), lambda h: (0, h)),
            pl.BlockSpec((rows, head_dim), lambda h: (0, part * heads + h)),
            pl.BlockSpec((1, 1, rows), lambda h: (h, 0, 0)),
            pl.BlockSpec((rows, 1), lambda h: (0, 0)),
        ],
        out_specs=[
            pl.BlockSpec((rows, 3 * head_dim), lambda h: (0, h)),
            pl.BlockSpec((1, 3 * head_dim), lambda h: (0, h)),
        ],
        out_shape=[
            jax.ShapeDtypeStruct(qkv.shape, BF),
            jax.ShapeDtypeStruct((1, qkv.shape[1]), F32),
        ],
        compiler_params=pltpu.CompilerParams(vmem_limit_bytes=VMEM_LIMIT),
        cost_estimate=FREE,
    )(qkv, dcontext, log_total, mask)


def place_rows(pieces, places, shape):
    count, (rows, width) = len(pieces), pieces[0].shape

    def kernel(places_ref, *refs):
        for i in range(count):

            @pl.when(pl.program_id(0) == i)
            def _(i=i):
                refs[-1][...] = refs[i][...].astype(F32)

    return pl.pallas_call(
        kernel,
        grid_spec=pltpu.PrefetchScalarGridSpec(
            num_scalar_prefetch=1,
            grid=(count,),
            in_specs=[pl.BlockSpec((rows, width), lambda i, s: (0, 0))] * count,
            out_specs=pl.BlockSpec((rows, width), lambda i, s: (s[i], 0)),
        ),
        out_shape=jax.ShapeDtypeStruct(shape, F32),
        compiler_params=pltpu.CompilerParams(vmem_limit_bytes=VMEM_LIMIT),
        cost_estimate=FREE,
    )(jnp.stack(places).astype(jnp.int32), *pieces)


def place_columns(pieces, places, shape, block, column):
    count, (rows, width) = len(pieces), pieces[0].shape
    step = min(64, rows)

    def kernel(places_ref, *refs):
        for p in range(count):
            for i in range(width // block):
                at = pl.multiple_of(column(i, places_ref[p]) * block, block)
                value = refs[p][:, i * block : (i + 1) * block].astype(F32)
                refs[-1][:, pl.ds(at, block)] = value

    return pl.pallas_call(
        kernel,
        grid_spec=pltpu.PrefetchScalarGridSpec(
            num_scalar_prefetch=1,
            grid=(rows // step,),
            in_specs=[pl.BlockSpec((step, width), lambda i, s: (i, 0))] * count,
            out_specs=pl.BlockSpec((step, shape[1]), lambda i, s: (i, 0)),
        ),
        out_shape=jax.ShapeDtypeStruct(shape, F32),
        compiler_params=pltpu.CompilerParams(vmem_limit_bytes=VMEM_LIMIT),
        cost_estimate=FREE,
    )(jnp.stack(places).astype(jnp.int32), *pieces)


def take_columns(arrays, index, count, block):
    if block % LANES != 0:
        pieces = []
        for i in range(count):
            for w in arrays:
                pieces.append(lax.dynamic_slice_in_dim(w, index[i] * block, block, 1))
        return jnp.concatenate(pieces, axis=1)
    rows, n = arrays[0].shape[0], len(arrays)

    def kernel(index_ref, *refs):
        for i in range(n):
            refs[-1][:, i * block : (i + 1) * block] = refs[i][...]

    return pl.pallas_call(
        kernel,
        grid_spec=pltpu.PrefetchScalarGridSpec(
            num_scalar_prefetch=1,
            grid=(count,),
            in_specs=[pl.BlockSpec((rows, block), lambda i, s: (0, s[i]))] * n,
            out_specs=pl.BlockSpec((rows, n * block), lambda i, s: (0, i)),
        ),
        out_shape=jax.ShapeDtypeStruct((rows, count * n * block), BF),
        compiler_params=pltpu.CompilerParams(vmem_limit_bytes=VMEM_LIMIT),
        cost_estimate=FREE,
    )(jnp.stack(index).astype(jnp.int32), *arrays)


def place_heads_grad(gathered, reps, run, head_dim):
    shard = gathered.shape[1]
    step = min(64, shard)

    def kernel(in_ref, *outs):
        for r in range(reps):
            for j in range(run):
                at = (((r // TEAM) * run + j) * TEAM + r % TEAM) * head_dim
                for i in range(3):
                    start = (3 * j + i) * head_dim
                    value = in_ref[r, :, start : start + head_dim].astype(F32)
                    outs[i][:, at : at + head_dim] = value

    return pl.pallas_call(
        kernel,
        grid=(shard // step,),
        in_specs=[pl.BlockSpec((reps, step, run * 3 * head_dim), lambda i: (0, i, 0))],
        out_specs=[pl.BlockSpec((step, HEADS * head_dim), lambda i: (i, 0))] * 3,
        out_shape=[jax.ShapeDtypeStruct((shard, HEADS * head_dim), F32)] * 3,
        compiler_params=pltpu.CompilerParams(vmem_limit_bytes=VMEM_LIMIT),
        cost_estimate=FREE,
    )(gathered)


def local(
    tokens,
    lengths,
    query_weight,
    key_weight,
    value_weight,
    out_weight,
    query_bias,
    value_bias,
    out_bias,
    first_gain,
    first_shift,
    up_weight,
    up_bias,
    down_weight,
    down_bias,
    second_gain,
    second_shift,
    cotangent,
):
    slots_here, block, width = tokens.shape
    reps, parts = lax.axis_size("rep"), lax.axis_size("fsdp")
    copies = reps // TEAM
    hidden = up_weight.shape[1]
    shard = query_weight.shape[0]
    head_dim = width // HEADS
    team_heads = HEADS // TEAM
    run = team_heads // copies
    rep, z = lax.axis_index("rep"), lax.axis_index("fsdp")
    q, d = rep % TEAM, rep // TEAM
    parity = z % 2
    held = TEAM * slots_here // parts
    rows = slots_here * block
    half = rows // 2
    unit = hidden // parts // reps
    wide = width // copies
    halves = 2 if unit % (2 * LANES) == 0 else 1
    half_unit = unit // halves
    per_shard = HEADS // parts

    def swap(x, mask):
        return lax.ppermute(x, "rep", [(i, i ^ mask) for i in range(reps)])

    def shift(x, by):
        return lax.ppermute(x, "fsdp", [(i, (i - by) % parts) for i in range(parts)])

    def from_next(k):
        return (z + k) % parts

    def routes(turn):
        pairs = []
        for copy in range(copies):
            for member in range(TEAM):
                for place in range(parts):
                    slot = member * slots_here + (place + turn) % 2
                    to_member = ((slot // parts) * parts + place) // 2
                    source = (copy * TEAM + member) * parts + place
                    target = (copy * TEAM + to_member) * parts + slot % parts
                    pairs.append((source, target))
        return pairs

    even, odd = routes(0), routes(1)
    axes = ("rep", "fsdp")
    v = {}

    def order(*names):
        names = list(dict.fromkeys(names))
        v.update(zip(names, tie(*[v[n] for n in names]), strict=True))

    def to_team(x):
        first = lax.ppermute(pick(x, parity), axes, even)
        second = lax.ppermute(pick(x, 1 - parity), axes, odd)
        return first, second

    def from_team(first, second):
        return settle(*leave_team(first, second))

    def leave_team(first, second):
        first = lax.ppermute(first, axes, [(b, a) for a, b in even])
        second = lax.ppermute(second, axes, [(b, a) for a, b in odd])
        return first, second

    def settle(first, second):
        straight = jnp.stack([first, second])
        turned = jnp.stack([second, first])
        return jnp.where(parity == 0, straight, turned)

    vectors = jnp.concatenate(
        [
            query_bias,
            value_bias,
            out_bias,
            first_gain,
            first_shift,
            down_bias,
            second_gain,
            second_shift,
            up_bias,
        ]
    )[None]
    pieces = [vectors] + [shift(vectors, k) for k in range(1, parts)]
    there = [lengths] + [swap(lengths, m) for m in range(1, TEAM)]
    first, second = to_team(tokens)
    first, second, *pieces = tie(first, second, *pieces, *there)
    pieces, there = pieces[:parts], pieces[parts:]
    vectors = jnp.zeros((parts, vectors.shape[1]), BF)
    for k, piece in enumerate(pieces):
        vectors = lax.dynamic_update_slice(vectors, piece, (from_next(k), 0))
    vectors = vectors.astype(F32)
    names = [vectors[:, i * shard : (i + 1) * shard].reshape(width) for i in range(8)]
    bias_query, bias_value, bias_out, gain_one, shift_one, bias_down, gain_two, shift_two = names
    bias_up = vectors[:, 8 * shard :].reshape(parts, reps, unit)
    slot_lengths = jnp.zeros((TEAM, slots_here), jnp.int32)
    for m in range(TEAM):
        slot_lengths = lax.dynamic_update_slice(slot_lengths, there[m][None], (q ^ m, 0))
    slot_lengths = slot_lengths.reshape(-1)

    def live(member):
        place = [
            ((member * 2 + o) % parts) * block + jnp.arange(block) for o in (parity, 1 - parity)
        ]
        length = pick(slot_lengths, ((member * 2) // parts) * parts + z)
        return jnp.concatenate(place) < length

    masks = [live(q ^ m).astype(F32) for m in range(TEAM)]
    valid = masks[0][:, None]
    mask_mine, mask_other = jnp.concatenate(masks[:2]), jnp.concatenate(masks[2:])

    def head_columns(w, e):
        lead = w.shape[:-1]
        at = len(lead)
        split = w.reshape(lead + (copies, run, TEAM, head_dim))
        return pick(pick(split, e, at), q, at + 1)

    def over_z(x):
        return lax.all_gather(x, "fsdp", axis=0, tiled=True)

    def spread(x):
        return [x] + [swap(x, TEAM * m) for m in range(1, copies)]

    heads_here = [(d * run + j) * TEAM + q for j in range(run)]
    qkv_own = [
        take_columns([query_weight, key_weight, value_weight], [h], 1, head_dim)
        for h in heads_here
    ]
    split_out = out_weight.reshape(-1, head_dim, copies, wide)
    split_out = pick(split_out, d, 2)
    if per_shard >= TEAM:
        split_out = split_out.reshape(per_shard // TEAM, TEAM, head_dim, wide)
        out_own = pick(split_out, q, 1)
    else:
        out_own = pick(split_out, q % per_shard, 0)[None]
    up_own = [
        take_columns(
            [up_weight],
            [(t * reps + rep) * halves + h for t in range(parts)],
            parts,
            half_unit,
        )
        for h in range(halves)
    ]
    down_split = pick(down_weight.reshape(reps, halves, half_unit, width), rep)
    down_own = [down_split[h] for h in range(halves)]
    first, second, out_own, *own = tie(first, second, out_own, *qkv_own, *up_own, *down_own)
    qkv_own, up_own, down_own = own[:run], own[run : run + halves], own[run + halves :]
    for j in range(run):
        v[QKV_Z, j] = over_z(qkv_own[j])
    v[OUT_Z] = over_z(out_own)
    for h in range(halves):
        v[UP_Z, h] = over_z(up_own[h])
    for h in range(halves):
        v[DOWN_Z, h] = over_z(down_own[h])
    own_tokens = jnp.concatenate([first, second], axis=0)
    v[FAR, 0], v[FAR, 1] = swap(first, 2), swap(second, 2)
    near = [swap(x, 1) for x in (first, second)]
    order((FAR, 0), (FAR, 1), (QKV_Z, 0))
    for m in range(1, copies):
        v[QKV, 0, m] = swap(v[QKV_Z, 0], TEAM * m)
    far = [v[FAR, 0], v[FAR, 1]]
    far_near = [swap(x, 1) for x in far]

    def own_units(table, m):
        return pick(table, rep ^ (TEAM * m), 1).transpose(1, 0, 2).reshape(1, -1)

    bias_up = bias_up.reshape(parts, reps, halves, half_unit)
    up_biases = [own_units(bias_up, m) for m in range(copies)]
    qkv_bias = []
    for m in range(copies):
        qb, vb = head_columns(bias_query, d ^ m), head_columns(bias_value, d ^ m)
        qkv_bias.append(jnp.stack([qb, jnp.zeros_like(qb), vb], axis=1).reshape(1, -1))
    span = run * head_dim

    tokens_mine = jnp.concatenate([first, second] + near, axis=0)
    tokens_other = jnp.concatenate(far + far_near, axis=0)
    v[OTHER] = tokens_other
    order(OTHER, *[(QKV_Z, j) for j in range(run)])
    tokens_other = v[OTHER]
    for j in range(1, run):
        for m in range(1, copies):
            v[QKV, j, m] = swap(v[QKV_Z, j], TEAM * m)
    qkv_weight = {0: jnp.concatenate([v[QKV_Z, j] for j in range(run)], axis=1)}

    if held == 2:
        slots = (OTHER, MINE)
        v[MINE] = tokens_mine
        slot_masks = {OTHER: mask_other, MINE: mask_mine}
    else:
        slots = (BOTH,)
        v[BOTH] = jnp.concatenate([tokens_mine, tokens_other], axis=0)
        slot_masks = {BOTH: jnp.concatenate([mask_mine, mask_other])}
    log_totals = {}

    def project_step(name, m):
        v[QKV, name, m] = dot(
            "nn", [(v[name], qkv_weight[m])], lambda t, b: (t + b,), [BF], columns=[qkv_bias[m]]
        )

    def attend_only(name, m):
        qkv = v[QKV, name, m]
        context, log_totals[name, m] = attend(qkv, slot_masks[name][None], run)
        v[CONTEXT, name, m] = context

    def attend_step(name, m):
        project_step(name, m)
        attend_only(name, m)

    def out_step(name, first):
        at = (0, 1) if held == 2 else (int(name == OTHER), 2)
        pairs = [
            (v[CONTEXT, name if held == 2 else BOTH, m], out_full[m * span : (m + 1) * span])
            for m in range(copies)
        ]
        return dot("nn", pairs, plain, [first, BF], rows=at, split=ROWS)

    def add(x, received):
        total = x.astype(F32)
        for y in received:
            total = total + y.astype(F32)
        return total.astype(BF)

    def next_hop():
        return add(v[KEPT], [v[AWAY]])

    attend_step(slots[0], 0)
    if held == 2:
        order(MINE, (CONTEXT, OTHER, 0))
        attend_step(MINE, 0)
    order(
        (CONTEXT, slots[-1], 0),
        OUT_Z,
        *[(QKV, j, m) for j in range(run) for m in range(1, copies)],
    )
    out_z = v[OUT_Z]
    if per_shard < TEAM:
        fill = TEAM // per_shard
        out_z = out_z.reshape(HEADS // TEAM, fill, head_dim, wide)
        out_z = pick(out_z, q // per_shard, 1)
    out_z = out_z.reshape(team_heads * head_dim, wide)
    out_swapped = [out_z] + [swap(out_z, TEAM * m) for m in range(1, copies)]
    for m in range(1, copies):
        qkv_weight[m] = jnp.concatenate([v[QKV, j, m] for j in range(run)], axis=1)
        attend_step(slots[0], m)
        if m == 1:
            v[OUT_SWAPPED] = jnp.stack(out_swapped)
            order(OUT_SWAPPED, (CONTEXT, slots[0], m))
    out_columns = v[OUT_SWAPPED]
    out_full = jnp.concatenate([pick(out_columns, d ^ e) for e in range(copies)], axis=1)
    out_rows = [
        lax.dynamic_slice_in_dim(out_full, (d ^ m) * span, span, 0) for m in range(copies)
    ]
    out_full = jnp.concatenate(out_rows, axis=0)
    if held == 2:
        v[KEPT], v[AWAY] = out_step(OTHER, BF)
        order(KEPT, AWAY, MINE)
        v[AWAY] = swap(v[AWAY], 1)
        project_step(MINE, 1)
        order(AWAY, (QKV, MINE, 1))
        v[SEND] = next_hop()
        order(SEND, (QKV, MINE, 1), (UP_Z, 0))
        v[BACK] = swap(v[SEND], 2)
        for m in range(1, copies):
            if m > 1:
                project_step(MINE, m)
            attend_only(MINE, m)
        v[OWN], v[THEIRS] = out_step(MINE, F32)
    else:
        order((CONTEXT, BOTH, 0), (UP_Z, 0))
        v[KEPT], v[AWAY] = out_step(OTHER, BF)
        v[AWAY] = swap(v[AWAY], 1)
        v[BACK] = swap(next_hop(), 2)
        v[OWN], v[THEIRS] = out_step(MINE, F32)
    for m in range(1, copies):
        v[UP, 0, m] = swap(v[UP_Z, 0], TEAM * m)
    order(
        OWN,
        THEIRS,
        BACK,
        *[(UP_Z, h) for h in range(1, halves)],
        *[(UP, 0, m) for m in range(1, copies)],
    )
    for h in range(1, halves):
        for m in range(1, copies):
            v[UP, h, m] = swap(v[UP_Z, h], TEAM * m)
    v[ATTENDED] = v[OWN] + swap(v[THEIRS], 1).astype(F32)
    summed1 = own_tokens.astype(F32) + v[ATTENDED] + v[BACK].astype(F32) + bias_out
    normal1, scale1 = normalise(summed1)
    normed1 = normal1 * gain_one + shift_one

    def team_chunk(name):
        return jnp.concatenate([v[name], swap(v[name], 1)], axis=0)

    v[NEAR] = normed1.astype(BF)
    v[FAR] = swap(v[NEAR], 2)
    v[HIDDEN, 0] = team_chunk(NEAR)
    up_parts = {0: jnp.concatenate([v[UP_Z, h] for h in range(halves)], axis=1)}

    def up_step(i, m):
        v[VALUE, i, m], v[SLOPE, i, m] = dot(
            "nn",
            [(v[HIDDEN, i], up_parts[m])],
            lambda t, b: gelu_parts(t + b),
            [BF, BF],
            columns=[up_biases[m]],
        )

    up_step(0, 0)
    order(
        (VALUE, 0, 0),
        (DOWN_Z, 0),
        *[(UP, h, m) for h in range(1, halves) for m in range(1, copies)],
    )
    for m in range(1, copies):
        v[DOWN, 0, m] = swap(v[DOWN_Z, 0], TEAM * m)
    order((VALUE, 0, 0), FAR)
    v[HIDDEN, 1] = team_chunk(FAR)
    up_step(1, 0)
    for m in range(1, copies):
        up_parts[m] = jnp.concatenate([v[UP, h, m] for h in range(halves)], axis=1)
        up_step(1, m)
    order(
        *[(VALUE, 1, m) for m in range(copies)],
        (HIDDEN, 0),
        *[(DOWN_Z, h) for h in range(1, halves)],
    )
    for h in range(1, halves):
        for n in range(1, copies):
            v[DOWN, h, n] = swap(v[DOWN_Z, h], TEAM * n)
    for m in range(1, copies):
        up_step(0, m)
    order(
        *[(VALUE, i, m) for i in range(2) for m in range(copies)],
        *[(DOWN, 0, n) for n in range(1, copies)],
    )
    down_parts = {0: jnp.concatenate([v[DOWN_Z, h] for h in range(halves)], axis=0)}
    for m in range(1, copies):
        down_parts[m] = jnp.concatenate([v[DOWN, h, m] for h in range(halves)], axis=0)

    def down_step(i, kinds, **which):
        pairs = [(v[VALUE, i, m], down_parts[m]) for m in range(copies)]
        return dot("nn", pairs, plain, kinds, **which)

    v[KEPT], v[AWAY] = down_step(1, [BF, BF], split=ROWS)
    order(KEPT, AWAY, (VALUE, 0, 0))
    v[AWAY] = swap(v[AWAY], 1)
    order(KEPT, AWAY, (VALUE, 0, 0))
    v[SEND] = next_hop()
    order(SEND, (VALUE, 0, 0))
    v[BACK] = swap(v[SEND], 2)
    v[THEIRS] = down_step(0, [BF], rows=(1, 2))
    order(THEIRS, (VALUE, 0, 0))
    v[THEIRS] = jnp.concatenate(
        [swap(v[THEIRS][:half], 1), swap(v[THEIRS][half:], 1)], axis=0
    )
    v[OWN] = down_step(0, [F32], rows=(0, 2))
    order(OWN, THEIRS, BACK)

    def team_sum():
        return v[OWN] + v[THEIRS].astype(F32) + v[BACK].astype(F32)

    summed2 = normed1 + team_sum() + bias_down
    normal2, scale2 = normalise(summed2)
    result = (valid * (normal2 * gain_two + shift_two)).astype(BF)

    v[COTANGENT] = cotangent
    order(COTANGENT, (VALUE, 0, 0))
    v[COT, 0], v[COT, 1] = to_team(v[COTANGENT])
    v[NORMAL2] = normal2
    order(NORMAL2, (COT, 0), (COT, 1))
    normal2 = v[NORMAL2]
    grad_out = jnp.concatenate([v[COT, 0], v[COT, 1]], axis=0).astype(F32) * valid
    dsum2 = norm_backward(grad_out, gain_two, normal2, scale2)
    gain_two_grad = jnp.sum(grad_out * normal2, axis=0)
    shift_two_grad = jnp.sum(grad_out, axis=0)
    v[NEAR] = dsum2.astype(BF)
    down_bias_grad = jnp.sum(v[NEAR].astype(F32), axis=0)
    v[RESULT] = result
    order(RESULT, NEAR)
    v[LAYER, 0], v[LAYER, 1] = leave_team(v[RESULT][:block], v[RESULT][block:])

    def over_copies(shares):
        total = shares[0].astype(F32)
        for m in range(1, copies):
            total = total + swap(shares[m], TEAM * m).astype(F32)
        return total.astype(BF)

    def to_owner(x):
        return lax.psum_scatter(x, "fsdp", scatter_dimension=0, tiled=True)

    def from_all(x):
        return lax.all_gather(x, "rep", axis=0, tiled=True)

    def in_order(pieces):
        stacked = jnp.stack([pieces[m] for m in range(reps)])
        return jnp.stack([pick(stacked, rep ^ r) for r in range(reps)])

    sub = parts * half_unit

    def backward_step(i, first):
        for m in range(copies):
            v[DBEFORE, i, m] = dot(
                "nt",
                [(v[DDOWN, i], down_parts[m])],
                lambda t, s: (t * s.astype(F32),),
                [BF],
                tiles=[v[SLOPE, i, m]],
            )
        pairs = [(v[DBEFORE, i, m], up_parts[m]) for m in range(copies)]
        return dot("nt", pairs, plain, [first, BF], split=ROWS)

    def down_grad_step(m, *those):
        pairs = [(v[VALUE, i, m], v[DDOWN, i]) for i in range(2)]
        if len(those) == 2:
            both = dot("tn", pairs, plain, [BF, BF], split=ROWS)
        else:
            both = [dot("tn", pairs, plain, [BF], left=(h, halves)) for h in those]
        for h, share in zip(those, both, strict=True):
            v[DOWN, SHARE, h, m] = share

    def up_grad_step(m, *those):
        pairs = [(v[HIDDEN, i], v[DBEFORE, i, m]) for i in range(2)]
        if len(those) == 2:
            both = dot("tn", pairs, plain, [BF, BF], split=COLUMNS)
        else:
            both = [dot("tn", pairs, plain, [BF], right=(h, halves)) for h in those]
        for h, share in zip(those, both, strict=True):
            v[UP, SHARE, h, m] = share

    def swap_share(kind, h):
        for m in range(1, copies):
            v[kind, RECEIVED, h, m] = swap(v[kind, SHARE, h, m], TEAM * m)

    def shares(kind, *those):
        return [(kind, SHARE, h, m) for h in those for m in range(1, copies)]

    def received(kind, *those):
        return [(kind, RECEIVED, h, m) for h in those for m in range(1, copies)]

    def reduce_step(kind, h):
        total = add(v[kind, SHARE, h, 0], [v[n] for n in received(kind, h)])
        v[kind, PART, h] = to_owner(total)

    more = range(1, copies)
    late = range(1, halves)
    v[FAR] = swap(v[NEAR], 2)
    v[DDOWN, 0] = team_chunk(NEAR)
    v[OWN], v[THEIRS] = backward_step(0, F32)
    order(THEIRS, FAR, (VALUE, 0, 0))
    v[THEIRS] = swap(v[THEIRS], 1)
    v[DDOWN, 1] = team_chunk(FAR)
    for m in more:
        down_grad_step(m, *range(halves))
    order(*shares(DOWN, *range(halves)), (DDOWN, 1))
    for h in range(halves):
        swap_share(DOWN, h)
    v[KEPT], v[AWAY] = backward_step(1, BF)
    order(KEPT, AWAY, (DDOWN, 0))
    v[AWAY] = swap(v[AWAY], 1)
    order(KEPT, AWAY, (DDOWN, 0))
    v[SEND] = next_hop()
    order(SEND, (DDOWN, 0))
    v[BACK] = swap(v[SEND], 2)
    for h in range(halves):
        down_grad_step(0, h)
    order(*[(DOWN, SHARE, h, 0) for h in range(halves)], *received(DOWN, 0))
    reduce_step(DOWN, 0)
    order(
        OWN,
        BACK,
        THEIRS,
        (LAYER, 0),
        (LAYER, 1),
        *[(DOWN, SHARE, h, 0) for h in late],
    )
    dnormed1 = dsum2 + team_sum()
    dsum1 = norm_backward(dnormed1, gain_one, normal1, scale1)
    gain_one_grad = jnp.sum(dnormed1 * normal1, axis=0)
    shift_one_grad = jnp.sum(dnormed1, axis=0)
    v[DATTN] = dsum1.astype(BF)
    out_bias_grad = jnp.sum(v[DATTN].astype(F32), axis=0)

    order((HIDDEN, 0), DATTN)
    v[DATTN_NEAR] = swap(v[DATTN], 1)
    v[DATTN_FAR] = swap(v[DATTN], 2)
    for m in more:
        up_grad_step(m, *range(halves))
    order(
        *shares(UP, *range(halves)),
        DATTN_NEAR,
        (HIDDEN, 0),
        *received(DOWN, *late),
        *[(DOWN, SHARE, h, 0) for h in late],
    )
    for h in range(halves):
        swap_share(UP, h)
    for h in late:
        reduce_step(DOWN, h)

    v[DATTN_MINE] = jnp.concatenate([v[DATTN], v[DATTN_NEAR]], axis=0)
    qkv_sums = {}

    def back_step(name, dcontext, m):
        v[DQKV, name, m], qkv_sums[name, m] = attend_backward(
            v[QKV, name, m], dcontext, log_totals[name, m], slot_masks[name][:, None], run, m
        )

    def context_grad(x):
        return dot("nt", [(x, out_full)], plain, [BF])

    def far_rows():
        return jnp.concatenate([v[DATTN_FAR], swap(v[DATTN_FAR], 1)], axis=0)

    def out_grad_step():
        if held == 2:
            share = jnp.concatenate(
                [
                    dot(
                        "tn",
                        [
                            (v[CONTEXT, MINE, m], v[DATTN_MINE]),
                            (v[CONTEXT, OTHER, m], dattn_other),
                        ],
                        plain,
                        [BF],
                    )
                    for m in range(copies)
                ],
                axis=0,
            )
        else:
            pairs = [[(v[CONTEXT, BOTH, m], dattn_both)] for m in range(copies)]
            share = jnp.concatenate([dot("tn", p, plain, [BF]) for p in pairs], axis=0)
        for m in range(copies):
            rows_of = [
                lax.dynamic_slice(share, ((d ^ e) * span, (d ^ m) * wide), (span, wide))
                for e in range(copies)
            ]
            v[OUT, SHARE, 0, m] = jnp.concatenate(rows_of, axis=0)

    def out_reduce_step():
        total = add(v[OUT, SHARE, 0, 0], [v[n] for n in received(OUT, 0)])
        if per_shard < TEAM:
            fill = TEAM // per_shard
            total = total.reshape(HEADS // TEAM, 1, head_dim, -1)
            chosen = (jnp.arange(fill) == q // per_shard)[None, :, None, None]
            total = jnp.where(chosen, total, jnp.zeros((), BF))
            total = total.reshape(parts * head_dim, -1)
        v[OUT, PART, 0] = to_owner(total)

    def to_more(kind, mask):
        for m in [m for m in range(reps) if (kind, WHOLE, m) in v]:
            v[kind, WHOLE, m ^ mask] = swap(v[kind, WHOLE, m], mask)

    def all_of(kind):
        return [(kind, WHOLE, m) for m in range(reps) if (kind, WHOLE, m) in v]

    near_far = [2] + [TEAM << i for i in range(copies.bit_length() - 1)]

    def vector_table():
        def place_heads(i):
            full = jnp.zeros((copies, run, TEAM, head_dim), F32)
            for m in range(copies):
                share = sum(qkv_sums[name, m] for name in names)
                share = share.reshape(run, 3, head_dim)[:, i].reshape(1, run, 1, head_dim)
                full = lax.dynamic_update_slice(full, share, (d ^ m, 0, q, 0))
            return full.reshape(width)

        up_sums = jnp.zeros((parts, reps, halves, half_unit), F32)
        for m in range(copies):
            share = sum(jnp.sum(v[DBEFORE, i, m].astype(F32), axis=0) for i in range(2))
            share = share.reshape(halves, parts, half_unit).transpose(1, 0, 2)[:, None]
            up_sums = lax.dynamic_update_slice(up_sums, share, (0, rep ^ (TEAM * m), 0, 0))
        vector_sums = [
            place_heads(0),
            place_heads(2),
            out_bias_grad,
            gain_one_grad,
            shift_one_grad,
            down_bias_grad,
            gain_two_grad,
            shift_two_grad,
        ]
        return jnp.concatenate(
            [s.reshape(parts, shard) for s in vector_sums] + [up_sums.reshape(parts, -1)], axis=1
        )

    def vector_start():
        vector_sums = vector_table()
        v[VECTOR, 0] = pick(vector_sums, z)
        for k in range(1, parts):
            v[VECTOR, k] = shift(pick(vector_sums, (z - k) % parts), k)

    def vector_names():
        return [(VECTOR, k) for k in range(parts)]

    def vector_step(mask):
        if mask == 1:
            v[VECTOR, 0] = sum(v[n] for n in vector_names())
        v[VECTOR, 0] = v[VECTOR, 0] + swap(v[VECTOR, 0], mask)

    backwards = list(reversed(range(copies)))
    if held == 2:
        names = (MINE, OTHER)
        dcontext = context_grad(v[DATTN_MINE])
        for m in backwards:
            back_step(MINE, dcontext, m)
        order(
            DATTN_FAR,
            *[(DQKV, MINE, m) for m in range(copies)],
            *received(UP, 0),
        )
        v[DATTN_OTHER] = far_rows()
        dattn_other = v[DATTN_OTHER]
        out_grad_step()
        order(*[(OUT, SHARE, 0, m) for m in range(copies)], DATTN_OTHER, (HIDDEN, 0))
        swap_share(OUT, 0)
        up_grad_step(0, 0)
        order(DATTN_OTHER, (UP, SHARE, 0, 0))
        reduce_step(UP, 0)
        dattn_other = v[DATTN_OTHER]
        dcontext = context_grad(dattn_other)
        for m in backwards:
            back_step(OTHER, dcontext, m)
    else:
        names = (BOTH,)
        dattn_other = far_rows()
        dattn_both = jnp.concatenate([v[DATTN_MINE], dattn_other], axis=0)
        dcontext = context_grad(dattn_both)
        for m in backwards:
            back_step(BOTH, dcontext, m)
        up_grad_step(0, 0)
        reduce_step(UP, 0)
        out_grad_step()
        swap_share(OUT, 0)
        for m in range(copies):
            v[DQKV, MINE, m] = v[DQKV, BOTH, m][: 2 * rows]
            v[DQKV, OTHER, m] = v[DQKV, BOTH, m][2 * rows :]
    order(
        *[(DQKV, OTHER, m) for m in range(copies)],
        *[(DOWN, PART, h) for h in range(halves)],
        *received(UP, *late),
    )

    def qkv_grad_step(m):
        pairs = [(tokens_mine, v[DQKV, MINE, m]), (tokens_other, v[DQKV, OTHER, m])]
        v[QKV, SHARE, 0, m] = dot("tn", pairs, plain, [BF])

    def dtokens_partial(name, first):
        pairs = [(v[DQKV, name, m], qkv_weight[m]) for m in range(copies)]
        return dot("nt", pairs, plain, [first, BF], split=ROWS)

    for m in more:
        qkv_grad_step(m)
    order(
        *shares(QKV, 0),
        *[(DQKV, name, m) for name in (MINE, OTHER) for m in range(copies)],
        (HIDDEN, 0),
        *received(OUT, 0),
        (OUT, SHARE, 0, 0),
    )
    swap_share(QKV, 0)
    v[KEPT], v[AWAY] = dtokens_partial(OTHER, BF)
    order(
        KEPT,
        AWAY,
        *[(DQKV, MINE, m) for m in range(copies)],
        (HIDDEN, 0),
    )
    v[AWAY] = swap(v[AWAY], 1)
    order(KEPT, AWAY, *[(DQKV, MINE, m) for m in range(copies)], (HIDDEN, 0))
    v[SEND] = next_hop()
    v[BACK] = swap(v[SEND], 2)
    vector_start()
    for h in late:
        up_grad_step(0, h)
        reduce_step(UP, h)
    out_reduce_step()
    qkv_grad_step(0)
    v[OWN], v[THEIRS] = dtokens_partial(MINE, F32)
    order(
        THEIRS,
        BACK,
        (QKV, SHARE, 0, 0),
        *received(QKV, 0),
        *all_of(DOWN),
        *[(UP, PART, h) for h in range(halves)],
        *vector_names(),
    )
    reduce_step(QKV, 0)
    vector_step(1)
    v[DOWN, WHOLE, 0] = jnp.concatenate([v[DOWN, PART, h] for h in range(halves)], axis=0)
    to_more(DOWN, near_far[0])
    v[THEIRS] = swap(v[THEIRS], 1)
    v[UP, WHOLE, 0] = jnp.concatenate([v[UP, PART, h] for h in range(halves)], axis=1)
    far_near = near_far[1:] + near_far[:1]
    to_more(UP, far_near[0])
    order(OWN, THEIRS, BACK, *all_of(UP), *all_of(DOWN), (OUT, PART, 0))
    v[OUT, WHOLE, 0] = v[OUT, PART, 0]
    to_more(OUT, far_near[0])
    for i, mask in enumerate(far_near[1:]):
        to_more(UP, mask)
        to_more(DOWN, near_far[1 + i])
    v[OWN] = (dsum1 + team_sum()).astype(BF)
    order((QKV, PART, 0), OWN, (VECTOR, 0), *all_of(UP), *all_of(DOWN), *all_of(OUT))
    qkv_part = lax.all_gather(v[QKV, PART, 0], "rep", axis=0, tiled=False)
    v[GRAD, 0], v[GRAD, 1] = leave_team(v[OWN][:block], v[OWN][block:])
    to_more(UP, 1)
    to_more(DOWN, 1)
    for mask in far_near[1:]:
        to_more(OUT, mask)
    vector_step(2)
    layer_out = settle(v[LAYER, 0], v[LAYER, 1])
    order(*all_of(UP), *all_of(DOWN))
    places = [rep ^ m for m in range(reps)]
    aligned = half_unit % LANES == 0 and head_dim % LANES == 0
    if aligned:
        v[DOWN_GRAD] = place_rows(
            [v[DOWN, WHOLE, m] for m in range(reps)], places, (hidden // parts, width)
        )
        v[UP_GRAD] = place_columns(
            [v[UP, WHOLE, m] for m in range(reps)],
            places,
            (shard, hidden),
            half_unit,
            lambda i, r: ((i % parts) * reps + r) * halves + i // parts,
        )
        order(DOWN_GRAD, UP_GRAD, *all_of(OUT), (VECTOR, 0))
    to_more(OUT, 1)
    for mask in near_far[1:]:
        vector_step(mask)
    tokens_grad = settle(v[GRAD, 0], v[GRAD, 1]).astype(F32)
    out_grad = in_order({m: v[OUT, WHOLE, m] for m in range(reps)})

    if per_shard >= TEAM:
        out_grad = out_grad.reshape(copies, TEAM, per_shard // TEAM, head_dim, wide)
        out_grad = out_grad.transpose(2, 1, 3, 0, 4)
    else:
        fill = TEAM // per_shard
        out_grad = out_grad.reshape(copies, fill, per_shard, head_dim, wide)
        out_grad = pick(out_grad, z % fill, 1).transpose(1, 2, 0, 3)
    out_grad = out_grad.reshape(-1, width).astype(F32)

    if aligned:
        down_grad, up_grad = v[DOWN_GRAD], v[UP_GRAD]
        qkv_grads = place_heads_grad(qkv_part, reps, run, head_dim)
    else:
        def in_order_of(kind):
            return in_order({m: v[kind, WHOLE, m] for m in range(reps)})

        down_grad = in_order_of(DOWN).reshape(-1, width).astype(F32)
        up_grad = in_order_of(UP).reshape(reps, shard, halves, parts, half_unit)
        up_grad = up_grad.transpose(1, 3, 0, 2, 4).reshape(shard, hidden).astype(F32)
        qkv_final = qkv_part.reshape(copies, TEAM, shard, run, 3, head_dim)
        qkv_grads = [
            qkv_final[:, :, :, :, i].transpose(2, 0, 3, 1, 4).reshape(shard, width).astype(F32)
            for i in range(3)
        ]

    total = v[VECTOR, 0]
    small = [total[i * shard : (i + 1) * shard] for i in range(8)]
    up_bias_grad = total[8 * shard :]
    return (
        layer_out,
        tokens_grad,
        qkv_grads[0],
        qkv_grads[1],
        qkv_grads[2],
        out_grad,
        small[0],
        small[1],
        small[2],
        small[3],
        small[4],
        up_grad,
        up_bias_grad,
        down_grad,
        small[5],
        small[6],
        small[7],
    )


def solution(mesh):
    three, two, one = P("rep", "fsdp", None), P("fsdp", None), P("fsdp")
    placed = (three, P("rep"), two, two, two, two, one, one, one, one, one)
    placed += (two, one, two, one, one, one, three)
    given = (three, three, two, two, two, two, one, one, one, one, one)
    given += (two, one, two, one, one, one)
    return jax.shard_map(local, mesh=mesh, in_specs=placed, out_specs=given, check_vma=False)
```

```python
import jax
import jax.numpy as jnp
from jax import lax
from jax.experimental import pallas as pl
from jax.experimental.pallas import tpu as pltpu
from jax.sharding import PartitionSpec as P

HEADS = 16
TEAM = 4
LANES = 128
EPSILON = 1e-06
BF = jnp.bfloat16
F32 = jnp.float32
VMEM_LIMIT = 48 * 1024 * 1024
FREE = pl.CostEstimate(flops=0, bytes_accessed=0, transcendentals=0)

(
    ROWS,
    COLUMNS,
    QKV_Z,
    OUT_Z,
    UP_Z,
    DOWN_Z,
    FAR,
    QKV,
    OTHER,
    MINE,
    BOTH,
    CONTEXT,
    KEPT,
    AWAY,
    OUT_SWAPPED,
    SEND,
    BACK,
    OWN,
    THEIRS,
    UP,
    ATTENDED,
    NEAR,
    HIDDEN,
    VALUE,
    SLOPE,
    DOWN,
    COTANGENT,
    COT,
    NORMAL2,
    RESULT,
    LAYER,
    DBEFORE,
    DDOWN,
    SHARE,
    RECEIVED,
    PART,
    DATTN,
    DATTN_NEAR,
    DATTN_FAR,
    DATTN_MINE,
    DQKV,
    OUT,
    WHOLE,
    VECTOR,
    DATTN_OTHER,
    GRAD,
    DOWN_GRAD,
    UP_GRAD,
) = range(48)


def mm(left, right):
    return jnp.dot(left, right, preferred_element_type=F32)


def mm_t(left, right):
    return lax.dot_general(left, right, (((1,), (1,)), ((), ())), preferred_element_type=F32)


def t_mm(left, right):
    return lax.dot_general(left, right, (((0,), (0,)), ((), ())), preferred_element_type=F32)


def pick(array, index, axis=0):
    return lax.dynamic_index_in_dim(array, index, axis, keepdims=False)


def tie(*arrays):
    return lax.optimization_barrier(arrays)


def normalise(summed):
    center = summed - jnp.mean(summed, axis=-1, keepdims=True)
    spread = jnp.mean(center * center, axis=-1, keepdims=True)
    scale = lax.rsqrt(spread + EPSILON)
    return center * scale, scale


def norm_backward(grad, gain, normal, scale):
    dn = grad * gain
    first = jnp.mean(dn, axis=-1, keepdims=True)
    second = jnp.mean(dn * normal, axis=-1, keepdims=True)
    return scale * (dn - first - normal * second)


def gelu_parts(u):
    inner = 0.7978845608 * (u + 0.044715 * u * u * u)
    t = jnp.tanh(inner)
    half = 0.5 * (1.0 + t)
    slope = half + 0.5 * u * (1.0 - t * t) * (0.7978845608 + 0.7978845608 * 0.134145 * u * u)
    return u * half, slope


def dot(
    kind, pairs, finish, outs, columns=(), tiles=(), left=(0, 1), right=(0, 1), rows=(0, 1), split=None
):
    count = len(pairs)
    xs, ws = [x for x, _ in pairs], [w for _, w in pairs]
    flip = kind == "tn"
    m = xs[0].shape[1] // left[1] if flip else xs[0].shape[0] // rows[1]
    n = ws[0].shape[0] if kind == "nt" else ws[0].shape[1] // right[1]
    depths = [x.shape[0] if flip else x.shape[1] for x in xs]
    by_rows = flip and m > n
    size = m if by_rows else n
    step = next((s for s in (512, 384, 256) if size % s == 0), size)
    m_block, n_block = (step, n) if by_rows else (m, step)
    strip = next((s for s in (512, 256, 128, 64) if (m_block // 2) % s == 0), m_block // 2)
    inputs = 2 * count + len(columns) + len(tiles)

    def kernel(*refs):
        x_refs, w_refs = refs[:count], refs[count : 2 * count]
        column_refs = refs[2 * count : 2 * count + len(columns)]
        tile_refs = refs[2 * count + len(columns) : inputs]
        out_refs = refs[inputs : inputs + len(outs)]
        if flip:
            flipped = refs[inputs + len(outs) :]

            def turn():
                for a, b in zip(flipped, x_refs, strict=True):
                    a[...] = b[...].T

            if by_rows:
                turn()
            else:
                pl.when(pl.program_id(0) == 0)(turn)
            x_refs = flipped
        for at in range(0, m_block, strip):
            some = slice(at, at + strip)
            total = 0.0
            for x, w in zip(x_refs, w_refs, strict=True):
                product = mm_t(x[some, :], w[...]) if kind == "nt" else mm(x[some, :], w[...])
                total = total + product
            extra = [c[...] for c in column_refs] + [t[some, :] for t in tile_refs]
            values = finish(total, *extra)
            if split == ROWS:
                to = at * 2 // m_block
                at = at - to * (m_block // 2)
                out_refs[to][at : at + strip, :] = values[0].astype(out_refs[to].dtype)
                continue
            if split == COLUMNS:
                values = values[0][:, : n_block // 2], values[0][:, n_block // 2 :]
            for ref, value in zip(out_refs, values, strict=True):
                ref[some, :] = value.astype(ref.dtype)

    m_out, n_out = m // 2 if split == ROWS else m, n // 2 if split == COLUMNS else n
    if by_rows:
        per = left[0] * (m // step)
        x_specs = [pl.BlockSpec((k, step), lambda j: (0, per + j)) for k in depths]
        w_specs = [pl.BlockSpec((k, n), lambda j: (0, right[0])) for k in depths]
        out_spec = pl.BlockSpec((step, n_out), lambda j: (j, 0))
    else:
        per = right[0] * (n // step)
        if flip:
            x_specs = [pl.BlockSpec((k, m), lambda j: (0, left[0])) for k in depths]
        else:
            x_specs = [pl.BlockSpec((m, k), lambda j: (rows[0], 0)) for k in depths]
        if kind == "nt":
            w_specs = [pl.BlockSpec((step, k), lambda j: (j, 0)) for k in depths]
        else:
            w_specs = [pl.BlockSpec((k, step), lambda j: (0, per + j)) for k in depths]
        out_spec = pl.BlockSpec((m_out, step), lambda j: (0, j))
    results = pl.pallas_call(
        kernel,
        grid=(size // step,),
        in_specs=x_specs
        + w_specs
        + [pl.BlockSpec((1, step), lambda j: (0, j))] * len(columns)
        + [out_spec] * len(tiles),
        out_specs=[out_spec] * len(outs),
        out_shape=[jax.ShapeDtypeStruct((m_out, n_out), t) for t in outs],
        scratch_shapes=[pltpu.VMEM((m_block, k), BF) for k in depths] if flip else [],
        compiler_params=pltpu.CompilerParams(vmem_limit_bytes=VMEM_LIMIT),
        cost_estimate=FREE,
    )(*xs, *ws, *columns, *tiles)
    return results if len(outs) > 1 else results[0]


def plain(total):
    return (total,)


def attend(qkv, mask, heads):
    rows = qkv.shape[0]
    head_dim = qkv.shape[1] // (3 * heads)
    scaling = head_dim ** (-0.5)
    step = min(256, rows)

    def kernel(qkv_ref, mask_ref, context_ref, total_ref):
        keys = qkv_ref[:, head_dim : 2 * head_dim]
        values = qkv_ref[:, 2 * head_dim :]
        keep = mask_ref[...] > 0
        for at in range(0, rows, step):
            query = qkv_ref[at : at + step, :head_dim]
            scores = jnp.where(keep, mm_t(query, keys) * scaling, -1e30)
            most = jnp.max(scores, axis=1, keepdims=True)
            shares = jnp.exp(scores - most)
            total = jnp.sum(shares, axis=1, keepdims=True)
            probs = (shares * (1.0 / total)).astype(BF)
            context_ref[at : at + step, :] = mm(probs, values).astype(BF)
            log_total = jnp.broadcast_to(most + jnp.log(total), (step, 128))
            total_ref[0, :, at : at + step] = jnp.transpose(log_total)[0:1, :]

    return pl.pallas_call(
        kernel,
        grid=(heads,),
        in_specs=[
            pl.BlockSpec((rows, 3 * head_dim), lambda h: (0, h)),
            pl.BlockSpec((1, rows), lambda h: (0, 0)),
        ],
        out_specs=[
            pl.BlockSpec((rows, head_dim), lambda h: (0, h)),
            pl.BlockSpec((1, 1, rows), lambda h: (h, 0, 0)),
        ],
        out_shape=[
            jax.ShapeDtypeStruct((rows, heads * head_dim), BF),
            jax.ShapeDtypeStruct((heads, 1, rows), F32),
        ],
        compiler_params=pltpu.CompilerParams(vmem_limit_bytes=VMEM_LIMIT),
        cost_estimate=FREE,
    )(qkv, mask)


def attend_backward(qkv, dcontext, log_total, mask, heads, part):
    rows = qkv.shape[0]
    head_dim = qkv.shape[1] // (3 * heads)
    scaling = head_dim ** (-0.5)
    step = min(256, rows)

    def kernel(qkv_ref, dcontext_ref, total_ref, mask_ref, dqkv_ref, sums_ref):
        keys = qkv_ref[:, head_dim : 2 * head_dim]
        values = qkv_ref[:, 2 * head_dim :]
        keep = mask_ref[...] > 0
        dkeys, dvalues, query_sum = 0.0, 0.0, 0.0
        for at in range(0, rows, step):
            query = qkv_ref[at : at + step, :head_dim]
            dctx = dcontext_ref[at : at + step, :]
            scores = mm_t(keys, query) * scaling
            probs = jnp.exp(scores - total_ref[0, :, at : at + step])
            probs = jnp.where(keep, probs, 0.0)
            dprobs = mm_t(values, dctx)
            delta = jnp.sum(dprobs * probs, axis=0, keepdims=True)
            dscores = (probs * (dprobs - delta)).astype(BF)
            dvalues = dvalues + mm(probs.astype(BF), dctx)
            dkeys = dkeys + mm(dscores, query)
            dquery = (t_mm(dscores, keys) * scaling).astype(BF)
            dqkv_ref[at : at + step, :head_dim] = dquery
            query_sum = query_sum + jnp.sum(dquery.astype(F32), axis=0, keepdims=True)
        dvalues = dvalues.astype(BF)
        dqkv_ref[:, head_dim : 2 * head_dim] = (dkeys * scaling).astype(BF)
        dqkv_ref[:, 2 * head_dim :] = dvalues
        value_sum = jnp.sum(dvalues.astype(F32), axis=0, keepdims=True)
        sums_ref[...] = jnp.concatenate([query_sum, query_sum, value_sum], axis=1)

    return pl.pallas_call(
        kernel,
        grid=(heads,),
        in_specs=[
            pl.BlockSpec((rows, 3 * head_dim), lambda h: (0, h)),
            pl.BlockSpec((rows, head_dim), lambda h: (0, part * heads + h)),
            pl.BlockSpec((1, 1, rows), lambda h: (h, 0, 0)),
            pl.BlockSpec((rows, 1), lambda h: (0, 0)),
        ],
        out_specs=[
            pl.BlockSpec((rows, 3 * head_dim), lambda h: (0, h)),
            pl.BlockSpec((1, 3 * head_dim), lambda h: (0, h)),
        ],
        out_shape=[
            jax.ShapeDtypeStruct(qkv.shape, BF),
            jax.ShapeDtypeStruct((1, qkv.shape[1]), F32),
        ],
        compiler_params=pltpu.CompilerParams(vmem_limit_bytes=VMEM_LIMIT),
        cost_estimate=FREE,
    )(qkv, dcontext, log_total, mask)


def place_rows(pieces, places, shape, spot=lambda place: (place, 0)):
    count, (rows, width) = len(pieces), pieces[0].shape

    def kernel(places_ref, *refs):
        for i in range(count):

            @pl.when(pl.program_id(0) == i)
            def _(i=i):
                refs[-1][...] = refs[i][...].astype(F32)

    return pl.pallas_call(
        kernel,
        grid_spec=pltpu.PrefetchScalarGridSpec(
            num_scalar_prefetch=1,
            grid=(count,),
            in_specs=[pl.BlockSpec((rows, width), lambda i, s: (0, 0))] * count,
            out_specs=pl.BlockSpec((rows, width), lambda i, s: spot(s[i])),
        ),
        out_shape=jax.ShapeDtypeStruct(shape, F32),
        compiler_params=pltpu.CompilerParams(vmem_limit_bytes=VMEM_LIMIT),
        cost_estimate=FREE,
    )(jnp.stack(places).astype(jnp.int32), *pieces)


def place_columns(pieces, places, shape, block, column):
    count, (rows, width) = len(pieces), pieces[0].shape
    step = min(64, rows)

    def kernel(places_ref, *refs):
        for p in range(count):
            for i in range(width // block):
                at = pl.multiple_of(column(i, places_ref[p]) * block, block)
                value = refs[p][:, i * block : (i + 1) * block].astype(F32)
                refs[-1][:, pl.ds(at, block)] = value

    return pl.pallas_call(
        kernel,
        grid_spec=pltpu.PrefetchScalarGridSpec(
            num_scalar_prefetch=1,
            grid=(rows // step,),
            in_specs=[pl.BlockSpec((step, width), lambda i, s: (i, 0))] * count,
            out_specs=pl.BlockSpec((step, shape[1]), lambda i, s: (i, 0)),
        ),
        out_shape=jax.ShapeDtypeStruct(shape, F32),
        compiler_params=pltpu.CompilerParams(vmem_limit_bytes=VMEM_LIMIT),
        cost_estimate=FREE,
    )(jnp.stack(places).astype(jnp.int32), *pieces)


def take_columns(arrays, index, count, block):
    if block % LANES != 0:
        pieces = []
        for i in range(count):
            for w in arrays:
                pieces.append(lax.dynamic_slice_in_dim(w, index[i] * block, block, 1))
        return jnp.concatenate(pieces, axis=1)
    rows, n = arrays[0].shape[0], len(arrays)

    def kernel(index_ref, *refs):
        for i in range(n):
            refs[-1][:, i * block : (i + 1) * block] = refs[i][...]

    return pl.pallas_call(
        kernel,
        grid_spec=pltpu.PrefetchScalarGridSpec(
            num_scalar_prefetch=1,
            grid=(count,),
            in_specs=[pl.BlockSpec((rows, block), lambda i, s: (0, s[i]))] * n,
            out_specs=pl.BlockSpec((rows, n * block), lambda i, s: (0, i)),
        ),
        out_shape=jax.ShapeDtypeStruct((rows, count * n * block), BF),
        compiler_params=pltpu.CompilerParams(vmem_limit_bytes=VMEM_LIMIT),
        cost_estimate=FREE,
    )(jnp.stack(index).astype(jnp.int32), *arrays)


def place_heads_grad(gathered, reps, run, head_dim):
    shard = gathered.shape[1]
    step = min(64, shard)

    def kernel(in_ref, *outs):
        for r in range(reps):
            for j in range(run):
                at = (((r // TEAM) * run + j) * TEAM + r % TEAM) * head_dim
                for i in range(3):
                    start = (3 * j + i) * head_dim
                    value = in_ref[r, :, start : start + head_dim].astype(F32)
                    outs[i][:, at : at + head_dim] = value

    return pl.pallas_call(
        kernel,
        grid=(shard // step,),
        in_specs=[pl.BlockSpec((reps, step, run * 3 * head_dim), lambda i: (0, i, 0))],
        out_specs=[pl.BlockSpec((step, HEADS * head_dim), lambda i: (i, 0))] * 3,
        out_shape=[jax.ShapeDtypeStruct((shard, HEADS * head_dim), F32)] * 3,
        compiler_params=pltpu.CompilerParams(vmem_limit_bytes=VMEM_LIMIT),
        cost_estimate=FREE,
    )(gathered)


def local(
    tokens,
    lengths,
    query_weight,
    key_weight,
    value_weight,
    out_weight,
    query_bias,
    value_bias,
    out_bias,
    first_gain,
    first_shift,
    up_weight,
    up_bias,
    down_weight,
    down_bias,
    second_gain,
    second_shift,
    cotangent,
):
    slots_here, block, width = tokens.shape
    reps, parts = lax.axis_size("rep"), lax.axis_size("fsdp")
    copies = reps // TEAM
    hidden = up_weight.shape[1]
    shard = query_weight.shape[0]
    head_dim = width // HEADS
    team_heads = HEADS // TEAM
    run = team_heads // copies
    rep, z = lax.axis_index("rep"), lax.axis_index("fsdp")
    q, d = rep % TEAM, rep // TEAM
    parity = z % 2
    held = TEAM * slots_here // parts
    rows = slots_here * block
    half = rows // 2
    unit = hidden // parts // reps
    wide = width // copies
    halves = 2 if unit % (2 * LANES) == 0 else 1
    half_unit = unit // halves
    per_shard = HEADS // parts

    def swap(x, mask):
        return lax.ppermute(x, "rep", [(i, i ^ mask) for i in range(reps)])

    def shift(x, by):
        return lax.ppermute(x, "fsdp", [(i, (i - by) % parts) for i in range(parts)])

    def from_next(k):
        return (z + k) % parts

    def routes(turn):
        pairs = []
        for copy in range(copies):
            for member in range(TEAM):
                for place in range(parts):
                    slot = member * slots_here + (place + turn) % 2
                    to_member = ((slot // parts) * parts + place) // 2
                    source = (copy * TEAM + member) * parts + place
                    target = (copy * TEAM + to_member) * parts + slot % parts
                    pairs.append((source, target))
        return pairs

    even, odd = routes(0), routes(1)
    axes = ("rep", "fsdp")
    v = {}

    def order(*names):
        names = list(dict.fromkeys(names))
        v.update(zip(names, tie(*[v[n] for n in names]), strict=True))

    def to_team(x):
        first = lax.ppermute(pick(x, parity), axes, even)
        second = lax.ppermute(pick(x, 1 - parity), axes, odd)
        return first, second

    def from_team(first, second):
        return settle(*leave_team(first, second))

    def leave_team(first, second):
        first = lax.ppermute(first, axes, [(b, a) for a, b in even])
        second = lax.ppermute(second, axes, [(b, a) for a, b in odd])
        return first, second

    def settle(first, second):
        straight = jnp.stack([first, second])
        turned = jnp.stack([second, first])
        return jnp.where(parity == 0, straight, turned)

    vectors = jnp.concatenate(
        [
            query_bias,
            value_bias,
            out_bias,
            first_gain,
            first_shift,
            down_bias,
            second_gain,
            second_shift,
            up_bias,
        ]
    )[None]
    pieces = [vectors] + [shift(vectors, k) for k in range(1, parts)]
    there = [lengths] + [swap(lengths, m) for m in range(1, TEAM)]
    first, second = to_team(tokens)
    first, second, *pieces = tie(first, second, *pieces, *there)
    pieces, there = pieces[:parts], pieces[parts:]
    vectors = jnp.zeros((parts, vectors.shape[1]), BF)
    for k, piece in enumerate(pieces):
        vectors = lax.dynamic_update_slice(vectors, piece, (from_next(k), 0))
    vectors = vectors.astype(F32)
    names = [vectors[:, i * shard : (i + 1) * shard].reshape(width) for i in range(8)]
    bias_query, bias_value, bias_out, gain_one, shift_one, bias_down, gain_two, shift_two = names
    bias_up = vectors[:, 8 * shard :].reshape(parts, reps, unit)
    slot_lengths = jnp.zeros((TEAM, slots_here), jnp.int32)
    for m in range(TEAM):
        slot_lengths = lax.dynamic_update_slice(slot_lengths, there[m][None], (q ^ m, 0))
    slot_lengths = slot_lengths.reshape(-1)

    def live(member):
        place = [
            ((member * 2 + o) % parts) * block + jnp.arange(block) for o in (parity, 1 - parity)
        ]
        length = pick(slot_lengths, ((member * 2) // parts) * parts + z)
        return jnp.concatenate(place) < length

    masks = [live(q ^ m).astype(F32) for m in range(TEAM)]
    valid = masks[0][:, None]
    mask_mine, mask_other = jnp.concatenate(masks[:2]), jnp.concatenate(masks[2:])

    def head_columns(w, e):
        lead = w.shape[:-1]
        at = len(lead)
        split = w.reshape(lead + (copies, run, TEAM, head_dim))
        return pick(pick(split, e, at), q, at + 1)

    def over_z(x):
        return lax.all_gather(x, "fsdp", axis=0, tiled=True)

    def spread(x):
        return [x] + [swap(x, TEAM * m) for m in range(1, copies)]

    heads_here = [(d * run + j) * TEAM + q for j in range(run)]
    qkv_own = [
        take_columns([query_weight, key_weight, value_weight], [h], 1, head_dim)
        for h in heads_here
    ]
    split_out = out_weight.reshape(-1, head_dim, copies, wide)
    split_out = pick(split_out, d, 2)
    if per_shard >= TEAM:
        split_out = split_out.reshape(per_shard // TEAM, TEAM, head_dim, wide)
        out_own = pick(split_out, q, 1)
    else:
        out_own = pick(split_out, q % per_shard, 0)[None]
    up_own = [
        take_columns(
            [up_weight],
            [(t * reps + rep) * halves + h for t in range(parts)],
            parts,
            half_unit,
        )
        for h in range(halves)
    ]
    down_split = pick(down_weight.reshape(reps, halves, half_unit, width), rep)
    down_own = [down_split[h] for h in range(halves)]
    first, second, out_own, *own = tie(first, second, out_own, *qkv_own, *up_own, *down_own)
    qkv_own, up_own, down_own = own[:run], own[run : run + halves], own[run + halves :]
    for j in range(run):
        v[QKV_Z, j] = over_z(qkv_own[j])
    v[OUT_Z] = over_z(out_own)
    for h in range(halves):
        v[UP_Z, h] = over_z(up_own[h])
    for h in range(halves):
        v[DOWN_Z, h] = over_z(down_own[h])
    own_tokens = jnp.concatenate([first, second], axis=0)
    v[FAR, 0], v[FAR, 1] = swap(first, 2), swap(second, 2)
    near = [swap(x, 1) for x in (first, second)]
    order((FAR, 0), (FAR, 1), (QKV_Z, 0))
    for m in range(1, copies):
        v[QKV, 0, m] = swap(v[QKV_Z, 0], TEAM * m)
    far = [v[FAR, 0], v[FAR, 1]]
    far_near = [swap(x, 1) for x in far]

    def own_units(table, m):
        return pick(table, rep ^ (TEAM * m), 1).transpose(1, 0, 2).reshape(1, -1)

    bias_up = bias_up.reshape(parts, reps, halves, half_unit)
    up_biases = [own_units(bias_up, m) for m in range(copies)]
    qkv_bias = []
    for m in range(copies):
        qb, vb = head_columns(bias_query, d ^ m), head_columns(bias_value, d ^ m)
        qkv_bias.append(jnp.stack([qb, jnp.zeros_like(qb), vb], axis=1).reshape(1, -1))
    span = run * head_dim

    tokens_mine = jnp.concatenate([first, second] + near, axis=0)
    tokens_other = jnp.concatenate(far + far_near, axis=0)
    v[OTHER] = tokens_other
    order(OTHER, *[(QKV_Z, j) for j in range(run)])
    tokens_other = v[OTHER]
    for j in range(1, run):
        for m in range(1, copies):
            v[QKV, j, m] = swap(v[QKV_Z, j], TEAM * m)
    qkv_weight = {0: jnp.concatenate([v[QKV_Z, j] for j in range(run)], axis=1)}

    if held == 2:
        slots = (OTHER, MINE)
        v[MINE] = tokens_mine
        slot_masks = {OTHER: mask_other, MINE: mask_mine}
    else:
        slots = (BOTH,)
        v[BOTH] = jnp.concatenate([tokens_mine, tokens_other], axis=0)
        slot_masks = {BOTH: jnp.concatenate([mask_mine, mask_other])}
    log_totals = {}

    def project_step(name, m):
        v[QKV, name, m] = dot(
            "nn", [(v[name], qkv_weight[m])], lambda t, b: (t + b,), [BF], columns=[qkv_bias[m]]
        )

    def attend_only(name, m):
        qkv = v[QKV, name, m]
        context, log_totals[name, m] = attend(qkv, slot_masks[name][None], run)
        v[CONTEXT, name, m] = context

    def attend_step(name, m):
        project_step(name, m)
        attend_only(name, m)

    def out_step(name, first):
        at = (0, 1) if held == 2 else (int(name == OTHER), 2)
        pairs = [
            (v[CONTEXT, name if held == 2 else BOTH, m], out_full[m * span : (m + 1) * span])
            for m in range(copies)
        ]
        return dot("nn", pairs, plain, [first, BF], rows=at, split=ROWS)

    def add(x, received):
        total = x.astype(F32)
        for y in received:
            total = total + y.astype(F32)
        return total.astype(BF)

    def next_hop():
        return add(v[KEPT], [v[AWAY]])

    attend_step(slots[0], 0)
    if held == 2:
        order(MINE, (CONTEXT, OTHER, 0))
        attend_step(MINE, 0)
    order(
        (CONTEXT, slots[-1], 0),
        OUT_Z,
        *[(QKV, j, m) for j in range(run) for m in range(1, copies)],
    )
    out_z = v[OUT_Z]
    if per_shard < TEAM:
        fill = TEAM // per_shard
        out_z = out_z.reshape(HEADS // TEAM, fill, head_dim, wide)
        out_z = pick(out_z, q // per_shard, 1)
    out_z = out_z.reshape(team_heads * head_dim, wide)
    out_swapped = [out_z] + [swap(out_z, TEAM * m) for m in range(1, copies)]
    for m in range(1, copies):
        qkv_weight[m] = jnp.concatenate([v[QKV, j, m] for j in range(run)], axis=1)
        attend_step(slots[0], m)
        if m == 1:
            v[OUT_SWAPPED] = jnp.stack(out_swapped)
            order(OUT_SWAPPED, (CONTEXT, slots[0], m))
    out_columns = v[OUT_SWAPPED]
    out_full = jnp.concatenate([pick(out_columns, d ^ e) for e in range(copies)], axis=1)
    out_rows = [
        lax.dynamic_slice_in_dim(out_full, (d ^ m) * span, span, 0) for m in range(copies)
    ]
    out_full = jnp.concatenate(out_rows, axis=0)
    if held == 2:
        v[KEPT], v[AWAY] = out_step(OTHER, BF)
        order(KEPT, AWAY, MINE)
        v[AWAY] = swap(v[AWAY], 1)
        project_step(MINE, 1)
        order(AWAY, (QKV, MINE, 1))
        v[SEND] = next_hop()
        order(SEND, (QKV, MINE, 1), (UP_Z, 0))
        v[BACK] = swap(v[SEND], 2)
        for m in range(1, copies):
            if m > 1:
                project_step(MINE, m)
            attend_only(MINE, m)
        v[OWN], v[THEIRS] = out_step(MINE, F32)
    else:
        order((CONTEXT, BOTH, 0), (UP_Z, 0))
        v[KEPT], v[AWAY] = out_step(OTHER, BF)
        v[AWAY] = swap(v[AWAY], 1)
        v[BACK] = swap(next_hop(), 2)
        v[OWN], v[THEIRS] = out_step(MINE, F32)
    for m in range(1, copies):
        v[UP, 0, m] = swap(v[UP_Z, 0], TEAM * m)
    order(
        OWN,
        THEIRS,
        BACK,
        *[(UP_Z, h) for h in range(1, halves)],
        *[(UP, 0, m) for m in range(1, copies)],
    )
    for h in range(1, halves):
        for m in range(1, copies):
            v[UP, h, m] = swap(v[UP_Z, h], TEAM * m)
    v[ATTENDED] = v[OWN] + swap(v[THEIRS], 1).astype(F32)
    summed1 = own_tokens.astype(F32) + v[ATTENDED] + v[BACK].astype(F32) + bias_out
    normal1, scale1 = normalise(summed1)
    normed1 = normal1 * gain_one + shift_one

    def team_chunk(name):
        return jnp.concatenate([v[name], swap(v[name], 1)], axis=0)

    v[NEAR] = normed1.astype(BF)
    v[FAR] = swap(v[NEAR], 2)
    v[HIDDEN, 0] = team_chunk(NEAR)
    up_parts = {0: jnp.concatenate([v[UP_Z, h] for h in range(halves)], axis=1)}

    def up_step(i, m):
        v[VALUE, i, m], v[SLOPE, i, m] = dot(
            "nn",
            [(v[HIDDEN, i], up_parts[m])],
            lambda t, b: gelu_parts(t + b),
            [BF, BF],
            columns=[up_biases[m]],
        )

    up_step(0, 0)
    order(
        (VALUE, 0, 0),
        (DOWN_Z, 0),
        *[(UP, h, m) for h in range(1, halves) for m in range(1, copies)],
    )
    for m in range(1, copies):
        v[DOWN, 0, m] = swap(v[DOWN_Z, 0], TEAM * m)
    order((VALUE, 0, 0), FAR)
    v[HIDDEN, 1] = team_chunk(FAR)
    up_step(1, 0)
    for m in range(1, copies):
        up_parts[m] = jnp.concatenate([v[UP, h, m] for h in range(halves)], axis=1)
        up_step(1, m)
    order(
        *[(VALUE, 1, m) for m in range(copies)],
        (HIDDEN, 0),
        *[(DOWN_Z, h) for h in range(1, halves)],
    )
    for h in range(1, halves):
        for n in range(1, copies):
            v[DOWN, h, n] = swap(v[DOWN_Z, h], TEAM * n)
    for m in range(1, copies):
        up_step(0, m)
    order(
        *[(VALUE, i, m) for i in range(2) for m in range(copies)],
        *[(DOWN, 0, n) for n in range(1, copies)],
    )
    down_parts = {0: jnp.concatenate([v[DOWN_Z, h] for h in range(halves)], axis=0)}
    for m in range(1, copies):
        down_parts[m] = jnp.concatenate([v[DOWN, h, m] for h in range(halves)], axis=0)

    def down_step(i, kinds, **which):
        pairs = [(v[VALUE, i, m], down_parts[m]) for m in range(copies)]
        return dot("nn", pairs, plain, kinds, **which)

    v[KEPT], v[AWAY] = down_step(1, [BF, BF], split=ROWS)
    order(KEPT, AWAY, (VALUE, 0, 0))
    v[AWAY] = swap(v[AWAY], 1)
    order(KEPT, AWAY, (VALUE, 0, 0))
    v[SEND] = next_hop()
    order(SEND, (VALUE, 0, 0))
    v[BACK] = swap(v[SEND], 2)
    v[THEIRS] = down_step(0, [BF], rows=(1, 2))
    order(THEIRS, (VALUE, 0, 0))
    v[THEIRS] = jnp.concatenate(
        [swap(v[THEIRS][:half], 1), swap(v[THEIRS][half:], 1)], axis=0
    )
    v[OWN] = down_step(0, [F32], rows=(0, 2))
    order(OWN, THEIRS, BACK)

    def team_sum():
        return v[OWN] + v[THEIRS].astype(F32) + v[BACK].astype(F32)

    summed2 = normed1 + team_sum() + bias_down
    normal2, scale2 = normalise(summed2)
    result = (valid * (normal2 * gain_two + shift_two)).astype(BF)

    v[COTANGENT] = cotangent
    order(COTANGENT, (VALUE, 0, 0))
    v[COT, 0], v[COT, 1] = to_team(v[COTANGENT])
    v[NORMAL2] = normal2
    order(NORMAL2, (COT, 0), (COT, 1))
    normal2 = v[NORMAL2]
    grad_out = jnp.concatenate([v[COT, 0], v[COT, 1]], axis=0).astype(F32) * valid
    dsum2 = norm_backward(grad_out, gain_two, normal2, scale2)
    gain_two_grad = jnp.sum(grad_out * normal2, axis=0)
    shift_two_grad = jnp.sum(grad_out, axis=0)
    v[NEAR] = dsum2.astype(BF)
    down_bias_grad = jnp.sum(v[NEAR].astype(F32), axis=0)
    v[RESULT] = result
    order(RESULT, NEAR)
    v[LAYER, 0], v[LAYER, 1] = leave_team(v[RESULT][:block], v[RESULT][block:])

    def over_copies(shares):
        total = shares[0].astype(F32)
        for m in range(1, copies):
            total = total + swap(shares[m], TEAM * m).astype(F32)
        return total.astype(BF)

    def to_owner(x):
        return lax.psum_scatter(x, "fsdp", scatter_dimension=0, tiled=True)

    def from_all(x):
        return lax.all_gather(x, "rep", axis=0, tiled=True)

    def in_order(pieces):
        stacked = jnp.stack([pieces[m] for m in range(reps)])
        return jnp.stack([pick(stacked, rep ^ r) for r in range(reps)])

    sub = parts * half_unit

    def backward_step(i, first):
        for m in range(copies):
            v[DBEFORE, i, m] = dot(
                "nt",
                [(v[DDOWN, i], down_parts[m])],
                lambda t, s: (t * s.astype(F32),),
                [BF],
                tiles=[v[SLOPE, i, m]],
            )
        pairs = [(v[DBEFORE, i, m], up_parts[m]) for m in range(copies)]
        return dot("nt", pairs, plain, [first, BF], split=ROWS)

    def down_grad_step(m, *those):
        pairs = [(v[VALUE, i, m], v[DDOWN, i]) for i in range(2)]
        if len(those) == 2:
            both = dot("tn", pairs, plain, [BF, BF], split=ROWS)
        else:
            both = [dot("tn", pairs, plain, [BF], left=(h, halves)) for h in those]
        for h, share in zip(those, both, strict=True):
            v[DOWN, SHARE, h, m] = share

    def up_grad_step(m, *those):
        pairs = [(v[HIDDEN, i], v[DBEFORE, i, m]) for i in range(2)]
        if len(those) == 2:
            both = dot("tn", pairs, plain, [BF, BF], split=COLUMNS)
        else:
            both = [dot("tn", pairs, plain, [BF], right=(h, halves)) for h in those]
        for h, share in zip(those, both, strict=True):
            v[UP, SHARE, h, m] = share

    def swap_share(kind, h):
        for m in range(1, copies):
            v[kind, RECEIVED, h, m] = swap(v[kind, SHARE, h, m], TEAM * m)

    def shares(kind, *those):
        return [(kind, SHARE, h, m) for h in those for m in range(1, copies)]

    def received(kind, *those):
        return [(kind, RECEIVED, h, m) for h in those for m in range(1, copies)]

    def reduce_step(kind, h):
        total = add(v[kind, SHARE, h, 0], [v[n] for n in received(kind, h)])
        v[kind, PART, h] = to_owner(total)

    more = range(1, copies)
    late = range(1, halves)
    v[FAR] = swap(v[NEAR], 2)
    v[DDOWN, 0] = team_chunk(NEAR)
    v[OWN], v[THEIRS] = backward_step(0, F32)
    order(THEIRS, FAR, (VALUE, 0, 0))
    v[THEIRS] = swap(v[THEIRS], 1)
    v[DDOWN, 1] = team_chunk(FAR)
    for m in more:
        down_grad_step(m, *range(halves))
    order(*shares(DOWN, *range(halves)), (DDOWN, 1))
    for h in range(halves):
        swap_share(DOWN, h)
    v[KEPT], v[AWAY] = backward_step(1, BF)
    order(KEPT, AWAY, (DDOWN, 0))
    v[AWAY] = swap(v[AWAY], 1)
    order(KEPT, AWAY, (DDOWN, 0))
    v[SEND] = next_hop()
    order(SEND, (DDOWN, 0))
    v[BACK] = swap(v[SEND], 2)
    for h in range(halves):
        down_grad_step(0, h)
    order(*[(DOWN, SHARE, h, 0) for h in range(halves)], *received(DOWN, 0))
    reduce_step(DOWN, 0)
    order(
        OWN,
        BACK,
        THEIRS,
        (LAYER, 0),
        (LAYER, 1),
        *[(DOWN, SHARE, h, 0) for h in late],
    )
    dnormed1 = dsum2 + team_sum()
    dsum1 = norm_backward(dnormed1, gain_one, normal1, scale1)
    gain_one_grad = jnp.sum(dnormed1 * normal1, axis=0)
    shift_one_grad = jnp.sum(dnormed1, axis=0)
    v[DATTN] = dsum1.astype(BF)
    out_bias_grad = jnp.sum(v[DATTN].astype(F32), axis=0)

    order((HIDDEN, 0), DATTN)
    v[DATTN_NEAR] = swap(v[DATTN], 1)
    v[DATTN_FAR] = swap(v[DATTN], 2)
    for m in more:
        up_grad_step(m, *range(halves))
    order(
        *shares(UP, *range(halves)),
        DATTN_NEAR,
        (HIDDEN, 0),
        *received(DOWN, *late),
        *[(DOWN, SHARE, h, 0) for h in late],
    )
    for h in range(halves):
        swap_share(UP, h)
    for h in late:
        reduce_step(DOWN, h)

    v[DATTN_MINE] = jnp.concatenate([v[DATTN], v[DATTN_NEAR]], axis=0)
    qkv_sums = {}

    def back_step(name, dcontext, m):
        v[DQKV, name, m], qkv_sums[name, m] = attend_backward(
            v[QKV, name, m], dcontext, log_totals[name, m], slot_masks[name][:, None], run, m
        )

    def context_grad(x):
        return dot("nt", [(x, out_full)], plain, [BF])

    def far_rows():
        return jnp.concatenate([v[DATTN_FAR], swap(v[DATTN_FAR], 1)], axis=0)

    def out_grad_step():
        if held == 2:
            share = jnp.concatenate(
                [
                    dot(
                        "tn",
                        [
                            (v[CONTEXT, MINE, m], v[DATTN_MINE]),
                            (v[CONTEXT, OTHER, m], dattn_other),
                        ],
                        plain,
                        [BF],
                    )
                    for m in range(copies)
                ],
                axis=0,
            )
        else:
            pairs = [[(v[CONTEXT, BOTH, m], dattn_both)] for m in range(copies)]
            share = jnp.concatenate([dot("tn", p, plain, [BF]) for p in pairs], axis=0)
        for m in range(copies):
            rows_of = [
                lax.dynamic_slice(share, ((d ^ e) * span, (d ^ m) * wide), (span, wide))
                for e in range(copies)
            ]
            v[OUT, SHARE, 0, m] = jnp.concatenate(rows_of, axis=0)

    def out_reduce_step():
        total = add(v[OUT, SHARE, 0, 0], [v[n] for n in received(OUT, 0)])
        if per_shard < TEAM:
            fill = TEAM // per_shard
            total = total.reshape(HEADS // TEAM, 1, head_dim, -1)
            chosen = (jnp.arange(fill) == q // per_shard)[None, :, None, None]
            total = jnp.where(chosen, total, jnp.zeros((), BF))
            total = total.reshape(parts * head_dim, -1)
        v[OUT, PART, 0] = to_owner(total)

    def to_more(kind, mask):
        for m in [m for m in range(reps) if (kind, WHOLE, m) in v]:
            v[kind, WHOLE, m ^ mask] = swap(v[kind, WHOLE, m], mask)

    def all_of(kind):
        return [(kind, WHOLE, m) for m in range(reps) if (kind, WHOLE, m) in v]

    near_far = [2] + [TEAM << i for i in range(copies.bit_length() - 1)]

    def vector_table():
        def place_heads(i):
            full = jnp.zeros((copies, run, TEAM, head_dim), F32)
            for m in range(copies):
                share = sum(qkv_sums[name, m] for name in names)
                share = share.reshape(run, 3, head_dim)[:, i].reshape(1, run, 1, head_dim)
                full = lax.dynamic_update_slice(full, share, (d ^ m, 0, q, 0))
            return full.reshape(width)

        up_sums = jnp.zeros((parts, reps, halves, half_unit), F32)
        for m in range(copies):
            share = sum(jnp.sum(v[DBEFORE, i, m].astype(F32), axis=0) for i in range(2))
            share = share.reshape(halves, parts, half_unit).transpose(1, 0, 2)[:, None]
            up_sums = lax.dynamic_update_slice(up_sums, share, (0, rep ^ (TEAM * m), 0, 0))
        vector_sums = [
            place_heads(0),
            place_heads(2),
            out_bias_grad,
            gain_one_grad,
            shift_one_grad,
            down_bias_grad,
            gain_two_grad,
            shift_two_grad,
        ]
        return jnp.concatenate(
            [s.reshape(parts, shard) for s in vector_sums] + [up_sums.reshape(parts, -1)], axis=1
        )

    def vector_start():
        vector_sums = vector_table()
        v[VECTOR, 0] = pick(vector_sums, z)
        for k in range(1, parts):
            v[VECTOR, k] = shift(pick(vector_sums, (z - k) % parts), k)

    def vector_names():
        return [(VECTOR, k) for k in range(parts)]

    def vector_step(mask):
        if mask == 1:
            v[VECTOR, 0] = sum(v[n] for n in vector_names())
        v[VECTOR, 0] = v[VECTOR, 0] + swap(v[VECTOR, 0], mask)

    backwards = list(reversed(range(copies)))
    if held == 2:
        names = (MINE, OTHER)
        dcontext = context_grad(v[DATTN_MINE])
        for m in backwards:
            back_step(MINE, dcontext, m)
        order(
            DATTN_FAR,
            *[(DQKV, MINE, m) for m in range(copies)],
            *received(UP, 0),
        )
        v[DATTN_OTHER] = far_rows()
        dattn_other = v[DATTN_OTHER]
        out_grad_step()
        order(*[(OUT, SHARE, 0, m) for m in range(copies)], DATTN_OTHER, (HIDDEN, 0))
        swap_share(OUT, 0)
        up_grad_step(0, 0)
        order(DATTN_OTHER, (UP, SHARE, 0, 0))
        reduce_step(UP, 0)
        dattn_other = v[DATTN_OTHER]
        dcontext = context_grad(dattn_other)
        for m in backwards:
            back_step(OTHER, dcontext, m)
    else:
        names = (BOTH,)
        dattn_other = far_rows()
        dattn_both = jnp.concatenate([v[DATTN_MINE], dattn_other], axis=0)
        dcontext = context_grad(dattn_both)
        for m in backwards:
            back_step(BOTH, dcontext, m)
        up_grad_step(0, 0)
        reduce_step(UP, 0)
        out_grad_step()
        swap_share(OUT, 0)
        for m in range(copies):
            v[DQKV, MINE, m] = v[DQKV, BOTH, m][: 2 * rows]
            v[DQKV, OTHER, m] = v[DQKV, BOTH, m][2 * rows :]
    order(
        *[(DQKV, OTHER, m) for m in range(copies)],
        *[(DOWN, PART, h) for h in range(halves)],
        *received(UP, *late),
    )

    def qkv_grad_step(m):
        pairs = [(tokens_mine, v[DQKV, MINE, m]), (tokens_other, v[DQKV, OTHER, m])]
        v[QKV, SHARE, 0, m] = dot("tn", pairs, plain, [BF])

    def dtokens_partial(name, first):
        pairs = [(v[DQKV, name, m], qkv_weight[m]) for m in range(copies)]
        return dot("nt", pairs, plain, [first, BF], split=ROWS)

    for m in more:
        qkv_grad_step(m)
    order(
        *shares(QKV, 0),
        *[(DQKV, name, m) for name in (MINE, OTHER) for m in range(copies)],
        (HIDDEN, 0),
        *received(OUT, 0),
        (OUT, SHARE, 0, 0),
    )
    swap_share(QKV, 0)
    v[KEPT], v[AWAY] = dtokens_partial(OTHER, BF)
    order(
        KEPT,
        AWAY,
        *[(DQKV, MINE, m) for m in range(copies)],
        (HIDDEN, 0),
    )
    v[AWAY] = swap(v[AWAY], 1)
    order(KEPT, AWAY, *[(DQKV, MINE, m) for m in range(copies)], (HIDDEN, 0))
    v[SEND] = next_hop()
    v[BACK] = swap(v[SEND], 2)
    vector_start()
    for h in late:
        up_grad_step(0, h)
        reduce_step(UP, h)
    out_reduce_step()
    qkv_grad_step(0)
    v[OWN], v[THEIRS] = dtokens_partial(MINE, F32)
    order(
        THEIRS,
        BACK,
        (QKV, SHARE, 0, 0),
        *received(QKV, 0),
        *all_of(DOWN),
        *[(UP, PART, h) for h in range(halves)],
        *vector_names(),
    )
    reduce_step(QKV, 0)
    vector_step(1)
    v[DOWN, WHOLE, 0] = jnp.concatenate([v[DOWN, PART, h] for h in range(halves)], axis=0)
    to_more(DOWN, near_far[0])
    v[THEIRS] = swap(v[THEIRS], 1)
    v[UP, WHOLE, 0] = jnp.concatenate([v[UP, PART, h] for h in range(halves)], axis=1)
    far_near = near_far[1:] + near_far[:1]
    to_more(UP, far_near[0])
    order(OWN, THEIRS, BACK, *all_of(UP), *all_of(DOWN), (OUT, PART, 0))
    v[OUT, WHOLE, 0] = v[OUT, PART, 0]
    to_more(OUT, far_near[0])
    for i, mask in enumerate(far_near[1:]):
        to_more(UP, mask)
        to_more(DOWN, near_far[1 + i])
    v[OWN] = (dsum1 + team_sum()).astype(BF)
    order((QKV, PART, 0), OWN, (VECTOR, 0), *all_of(UP), *all_of(DOWN), *all_of(OUT))
    qkv_part = lax.all_gather(v[QKV, PART, 0], "rep", axis=0, tiled=False)
    v[GRAD, 0], v[GRAD, 1] = leave_team(v[OWN][:block], v[OWN][block:])
    to_more(UP, 1)
    to_more(DOWN, 1)
    for mask in far_near[1:]:
        to_more(OUT, mask)
    vector_step(2)
    layer_out = settle(v[LAYER, 0], v[LAYER, 1])
    order(*all_of(UP), *all_of(DOWN))
    places = [rep ^ m for m in range(reps)]
    aligned = half_unit % LANES == 0 and head_dim % LANES == 0
    if aligned:
        v[DOWN_GRAD] = place_rows(
            [v[DOWN, WHOLE, m] for m in range(reps)], places, (hidden // parts, width)
        )
        v[UP_GRAD] = place_columns(
            [v[UP, WHOLE, m] for m in range(reps)],
            places,
            (shard, hidden),
            half_unit,
            lambda i, r: ((i % parts) * reps + r) * halves + i // parts,
        )
        order(DOWN_GRAD, UP_GRAD, *all_of(OUT), (VECTOR, 0))
    to_more(OUT, 1)
    for mask in near_far[1:]:
        vector_step(mask)
    tokens_grad = settle(v[GRAD, 0], v[GRAD, 1]).astype(F32)

    if aligned and per_shard == TEAM:
        out_grad = place_rows(
            [v[OUT, WHOLE, m].reshape(head_dim, wide) for m in range(reps)],
            places,
            (shard, width),
            lambda place: (lax.rem(place, TEAM), lax.div(place, TEAM)),
        )
    else:
        out_grad = in_order({m: v[OUT, WHOLE, m] for m in range(reps)})
        if per_shard >= TEAM:
            out_grad = out_grad.reshape(copies, TEAM, per_shard // TEAM, head_dim, wide)
            out_grad = out_grad.transpose(2, 1, 3, 0, 4)
        else:
            fill = TEAM // per_shard
            out_grad = out_grad.reshape(copies, fill, per_shard, head_dim, wide)
            out_grad = pick(out_grad, z % fill, 1).transpose(1, 2, 0, 3)
        out_grad = out_grad.reshape(-1, width).astype(F32)

    if aligned:
        down_grad, up_grad = v[DOWN_GRAD], v[UP_GRAD]
        qkv_grads = place_heads_grad(qkv_part, reps, run, head_dim)
    else:
        def in_order_of(kind):
            return in_order({m: v[kind, WHOLE, m] for m in range(reps)})

        down_grad = in_order_of(DOWN).reshape(-1, width).astype(F32)
        up_grad = in_order_of(UP).reshape(reps, shard, halves, parts, half_unit)
        up_grad = up_grad.transpose(1, 3, 0, 2, 4).reshape(shard, hidden).astype(F32)
        qkv_final = qkv_part.reshape(copies, TEAM, shard, run, 3, head_dim)
        qkv_grads = [
            qkv_final[:, :, :, :, i].transpose(2, 0, 3, 1, 4).reshape(shard, width).astype(F32)
            for i in range(3)
        ]

    total = v[VECTOR, 0]
    small = [total[i * shard : (i + 1) * shard] for i in range(8)]
    up_bias_grad = total[8 * shard :]
    return (
        layer_out,
        tokens_grad,
        qkv_grads[0],
        qkv_grads[1],
        qkv_grads[2],
        out_grad,
        small[0],
        small[1],
        small[2],
        small[3],
        small[4],
        up_grad,
        up_bias_grad,
        down_grad,
        small[5],
        small[6],
        small[7],
    )


def solution(mesh):
    three, two, one = P("rep", "fsdp", None), P("fsdp", None), P("fsdp")
    placed = (three, P("rep"), two, two, two, two, one, one, one, one, one)
    placed += (two, one, two, one, one, one, three)
    given = (three, three, two, two, two, two, one, one, one, one, one)
    given += (two, one, two, one, one, one)
    return jax.shard_map(local, mesh=mesh, in_specs=placed, out_specs=given, check_vma=False)
```
